32 devices in a mesh: gx: 4 (over x, core), gy: 2 (over y), gz: 4 (over z).
Axes of the slice: x: 2, y: 2, z: 4, core: 2. Of those that a mesh axis runs over, the one named last changes fastest.
Arguments:
- thermal_anomaly: float32 [64, 16, 512], P('gz', 'gy', 'gx'), may hold values from -6 to 6
- material_label: int32 [64, 16, 512], P('gz', 'gy', 'gx'), may hold values from 0 to 12
- label_thermal_table: float32 [13], replicated, may hold values from 0.25 to 4
- bottom_edge_option: int32 [16, 512], P('gy', 'gx'), may hold values from 0 to 1
Outputs:
- heated: float32 [64, 16, 512], P('gz', 'gy', 'gx')
The draws below stay inside these ranges and needn't reach their ends.
Inputs may be any that keep to these rules, and one draw needn't show every extreme that they name: material_label picks an entry of label_thermal_table. bottom_edge_option is 1 where the ground under the column is held at zero anomaly and 0 where it is insulated.
All inputs are finite; a program needn't handle non-finite values.
Results may differ from the reference program's by a relative error of at most 0.0006.
Values sent between devices are 32-bit elements; how exact they have to be, the bound alone decides.
No kernel may reach another device: no remote copies, remote signals or barrier semaphores. Data moves between devices by JAX's collectives and lax.ppermute only.
A program may use at most 64 MiB of HBM per device.

```python
import math
import jax
import jax.numpy as jnp
from jax import lax

NCLASS = 13
WIDTH_COUNT = 512
DEPTH_COUNT = 16
HEIGHT_COUNT = 64


def touch_ends(values, key, smallest, high):
    index_at = [jax.random.randint(jax.random.fold_in(key, axis), (), 0, length) for axis, length in enumerate(values.shape)]
    widest = values.shape.index(max(values.shape))
    next_to = index_at[:widest] + [(index_at[widest] + 1) % values.shape[widest]] + index_at[widest + 1:]
    return values.at[tuple(index_at)].set(smallest).at[tuple(next_to)].set(high)


def block_scale(key, extent, shards, low, high):
    loudness = 1.0
    for dim, shards_of in shards:
        steps = jax.random.uniform(jax.random.fold_in(jax.random.fold_in(key, 6), dim), (shards_of,), jnp.float32, low / len(shards), high / len(shards))
        loudness = loudness * jnp.repeat(jnp.exp(steps), extent[dim] // shards_of).reshape((-1,) + (1,) * (len(extent) - 1 - dim))
    return loudness


def gaussian(rng, extent, width, limit, split=(), held_as=jnp.bfloat16):
    factor_of = block_scale(rng, extent, split, -0.22, 0.18) if split else 1.0
    entries = jax.random.normal(rng, extent, jnp.float32) * width * factor_of
    return jnp.minimum(jnp.maximum(entries, -limit), limit).astype(held_as)


def setup_inputs(seed: int = 0) -> dict:
    keys = jax.random.split(jax.random.key(seed), 5)
    return {
        "thermal_anomaly": gaussian(keys[0], (HEIGHT_COUNT, DEPTH_COUNT, WIDTH_COUNT), 1.0, 6.0, ((0, 4), (1, 2), (2, 4)), jnp.float32),
        "material_label": touch_ends(jax.random.randint(keys[1], (HEIGHT_COUNT, DEPTH_COUNT, WIDTH_COUNT), 0, NCLASS), jax.random.fold_in(keys[1], 1), 0, NCLASS - 1).astype(jnp.int32),
        "label_thermal_table": jnp.clip(jnp.exp(jax.random.uniform(keys[2], (NCLASS,), jnp.float32, math.log(0.25), math.log(4.0))), 0.25, 4.0),
        "bottom_edge_option": touch_ends(jax.random.randint(keys[3], (DEPTH_COUNT, WIDTH_COUNT), 0, 2), jax.random.fold_in(keys[3], 1), 0, 1).astype(jnp.int32),
    }


THETA_FACTOR = 0.5
FLAT_SCALE = 1000.0
UPWARD_SCALE = 200.0

def shifted(values, offset, along, pad_value):
    length = values.shape[along]
    pad_shape = list(values.shape)
    pad_shape[along] = abs(offset)
    filler = jnp.full(pad_shape, pad_value, values.dtype)
    if offset > 0:
        return jnp.concatenate([filler, lax.slice_in_dim(values, 0, length - offset, axis=along)], along)
    return jnp.concatenate([lax.slice_in_dim(values, -offset, length, axis=along), filler], along)

def face_conductance(local_thermal_rate, along, factor):
    before = shifted(local_thermal_rate, 1, along, 0.0)
    return factor * (2.0 * local_thermal_rate * before) / (local_thermal_rate + before)

def heat_spread_operator(values, faces, along):
    beyond = shifted(faces, -1, along, 0.0)
    return beyond * (shifted(values, -1, along, 0.0) - values) - faces * (values - shifted(values, 1, along, 0.0))

def solve_lines(faces, source, along):
    beyond = shifted(faces, -1, along, 0.0)
    main_band = 1.0 + THETA_FACTOR * (faces + beyond)
    position = lax.broadcasted_iota(jnp.int32, faces.shape, along)
    low_band = jnp.where(position > 0, -THETA_FACTOR * faces, jnp.zeros_like(faces))
    high_band = -THETA_FACTOR * beyond
    moved_bands = [jnp.moveaxis(each_band, along, -1) for each_band in (low_band, main_band, high_band, source)]
    answer = lax.linalg.tridiagonal_solve(moved_bands[0], moved_bands[1], moved_bands[2], moved_bands[3][..., None])[..., 0]
    return jnp.moveaxis(answer, -1, along)

def reference(thermal_anomaly, material_label, label_thermal_table, bottom_edge_option):
    local_thermal_rate = jnp.take(label_thermal_table, material_label, axis=0)
    first_interface_transfer = face_conductance(local_thermal_rate, 2, FLAT_SCALE)
    second_interface_transfer = face_conductance(local_thermal_rate, 1, FLAT_SCALE)
    upward_interface_transfer = face_conductance(local_thermal_rate, 0, UPWARD_SCALE)
    ground = UPWARD_SCALE * 2.0 * local_thermal_rate[0] * bottom_edge_option.astype(local_thermal_rate.dtype)
    upward_interface_transfer = upward_interface_transfer.at[0].set(ground)
    solve_first_direction = heat_spread_operator(thermal_anomaly, first_interface_transfer, 2)
    solve_second_direction = heat_spread_operator(thermal_anomaly, second_interface_transfer, 1)
    solve_upward_direction = heat_spread_operator(thermal_anomaly, upward_interface_transfer, 0)
    forward_euler_change = thermal_anomaly + (1.0 - THETA_FACTOR) * solve_first_direction + solve_second_direction + solve_upward_direction
    after_x = solve_lines(first_interface_transfer, forward_euler_change, 2)
    after_y = solve_lines(second_interface_transfer, after_x - THETA_FACTOR * solve_second_direction, 1)
    return solve_lines(upward_interface_transfer, after_y - THETA_FACTOR * solve_upward_direction, 0)
```

```python
import functools

import jax
import jax.numpy as jnp
from jax import lax
from jax.experimental import pallas as pl
from jax.experimental.pallas import tpu as pltpu
from jax.sharding import PartitionSpec as P

FLAT_SCALE = 1000.0
UPWARD_SCALE = 200.0
F32 = jnp.float32


def link_of(scale, one, other):
    return scale * one * other / (one + other)


def roll(values, offset, axis):
    if axis == 0 and values.ndim == 3:
        offset = offset % values.shape[0]
        return jnp.concatenate([values[-offset:], values[:-offset]], 0)
    return pltpu.roll(values, offset % values.shape[axis], axis)


def steps_of(length):
    steps, distance = [], 1
    while distance < length - 1:
        steps.append(distance)
        distance *= 2
    return steps


def reduce_interior(link, axis, left_ref, right_ref):
    length = link.shape[axis]
    row = lax.broadcasted_iota(jnp.int32, link.shape, axis)
    low, high, own = link, roll(link, -1, axis), jnp.ones_like(link)
    high = jnp.where(row == length - 1, 0.0, high)
    for step, distance in enumerate(steps_of(length)):
        inverse = 1.0 / (own + low + high)
        open_low, open_high = row > distance, row < length - 1 - distance
        left = jnp.where(open_low, low * roll(inverse, distance, axis), 0.0)
        right = jnp.where(open_high, high * roll(inverse, -distance, axis), 0.0)
        left_ref[step], right_ref[step] = left, right
        own = own + left * roll(own, distance, axis) + right * roll(own, -distance, axis)
        low = jnp.where(open_low, left * roll(low, distance, axis), low)
        high = jnp.where(open_high, right * roll(high, -distance, axis), high)
    inverse = 1.0 / (own + low + high)
    inner = (row > 0) & (row < length - 1)
    share_low = jnp.where(inner, low * inverse, jnp.where(row == 0, 1.0, 0.0))
    share_high = jnp.where(inner, high * inverse, jnp.where(row == 0, 0.0, 1.0))
    return share_low, share_high, jnp.where(inner, inverse, 0.0), own * inverse


def reduce_source(source, axis, left_ref, right_ref, inverse):
    length = source.shape[axis]
    for step, distance in enumerate(steps_of(length)):
        source = (
            source
            + left_ref[step] * roll(source, distance, axis)
            + right_ref[step] * roll(source, -distance, axis)
        )
    return source * inverse


def chain(blocks, count, index, state):
    own = [blocks[k][3] + (blocks[k + 1][1] if k + 1 < count else 0.0) for k in range(count)]
    source = [blocks[k][4] + (blocks[k + 1][2] if k + 1 < count else 0.0) for k in range(count)]
    shape = own[0].shape
    state[0, 0], state[1, 0] = jnp.ones(shape, F32), jnp.zeros(shape, F32)
    up_own, up_source = own[0], source[0]
    for k in range(1, count):
        state[0, k], state[1, k] = up_own, up_source
        factor = blocks[k][0] / (up_own + blocks[k][0])
        up_own, up_source = own[k] + factor * up_own, source[k] + factor * up_source
    down_own, down_source = own[count - 1], source[count - 1]
    state[2, count - 1], state[3, count - 1] = down_own, down_source
    for k in range(count - 2, -1, -1):
        factor = blocks[k + 1][0] / (down_own + blocks[k + 1][0])
        down_own, down_source = own[k] + factor * down_own, source[k] + factor * down_source
        state[2, k], state[3, k] = down_own, down_source
    for k in range(count):
        state[4, k] = blocks[k][0]
    up_own, up_source, down_own, down_source, link = (state[i, index] for i in range(5))
    inverse = 1.0 / (up_own * down_own + link * (up_own + down_own))
    below = ((down_own + link) * up_source + link * down_source) * inverse
    here = ((up_own + link) * down_source + link * up_source) * inverse
    return below, here


def pick_halo(name, received, odd):
    first = received[0][...]
    second = received[1][...] if len(received) > 1 else jnp.zeros_like(first)
    index, count = lax.axis_index(name), lax.axis_size(name)
    below = jnp.where(odd, first, second)
    above = jnp.where(odd, second, first)
    return jnp.where(index > 0, below, 0.0), jnp.where(index < count - 1, above, 0.0)


def start_kernel(heat_ref, label_ref, table_ref, conduct_ref, za_ref, zb_ref, ya_ref, yb_ref):
    label = label_ref[...]
    conduct = jnp.full(label.shape, table_ref[0], F32)
    for entry in range(1, table_ref.shape[0]):
        conduct = jnp.where(label == entry, table_ref[entry], conduct)
    conduct_ref[...] = conduct
    odd_z = lax.axis_index("gz") % 2 == 1
    odd_y = lax.axis_index("gy") % 2 == 1
    for i, ref in enumerate((heat_ref, conduct_ref)):
        low, high = ref[0], ref[ref.shape[0] - 1]
        za_ref[i] = jnp.where(odd_z, low, high)
        zb_ref[i] = jnp.where(odd_z, high, low)
        low, high = ref[:, 0, :], ref[:, ref.shape[1] - 1, :]
        ya_ref[i] = jnp.where(odd_y, low, high)
        yb_ref[i] = jnp.where(odd_y, high, low)


def x_bands_kernel(
    heat_ref, conduct_ref, left_ref, right_ref, low_ref, high_ref, inverse_ref, ends_ref, local_ref
):
    nz, ny, nx = conduct_ref.shape
    conduct = conduct_ref[...]
    heat = heat_ref[...]
    local = 2.0 * heat
    across = 2.0 * link_of(UPWARD_SCALE, conduct[1:], conduct[:-1]) * (heat[1:] - heat[:-1])
    nothing = jnp.zeros_like(heat[:1])
    local = local + jnp.concatenate([across, nothing], 0) - jnp.concatenate([nothing, across], 0)
    row = lax.broadcasted_iota(jnp.int32, conduct.shape, 1)
    across = 2.0 * link_of(FLAT_SCALE, conduct, roll(conduct, 1, 1)) * (heat - roll(heat, 1, 1))
    across = jnp.where(row > 0, across, 0.0)
    local_ref[...] = local - across + roll(across, -1, 1)
    lines = conduct.reshape(nz * ny, nx).T
    row = lax.broadcasted_iota(jnp.int32, lines.shape, 0)
    link = jnp.where(row > 0, link_of(FLAT_SCALE, lines, roll(lines, 1, 0)), 0.0)
    low, high, inverse, own = reduce_interior(link, 0, left_ref, right_ref)
    low_ref[...], high_ref[...], inverse_ref[...] = low, high, inverse
    first, last = link[1:2], link[nx - 1 :]
    ends_ref[...] = jnp.concatenate(
        [
            first,
            last,
            1.0 + first * own[1:2],
            1.0 + last * own[nx - 2 : nx - 1],
            first * high[1:2],
            lines[:1],
            lines[nx - 1 :],
            jnp.zeros_like(first),
        ],
        0,
    )


def x_source_kernel(
    halo_counts, heat_ref, conduct_ref, edge_ref, local_ref, left_ref, right_ref, inverse_ref,
    ends_ref, *refs
):
    z_halo, y_halo = refs[: halo_counts[0]], refs[halo_counts[0] : sum(halo_counts)]
    part_ref, message_ref, source_ref = refs[sum(halo_counts) :]
    nz, ny, nx = conduct_ref.shape
    index_z, index_y = lax.axis_index("gz"), lax.axis_index("gy")
    below, above = pick_halo("gz", z_halo, index_z % 2 == 1)
    source_ref[...] = local_ref[...]
    ground = UPWARD_SCALE * conduct_ref[0] * edge_ref[...].astype(F32)
    ground = jnp.where(index_z == 0, ground, 0.0)
    flow = link_of(UPWARD_SCALE, conduct_ref[0], below[1]) * (below[0] - heat_ref[0])
    source_ref[0] += 2.0 * (flow - ground * heat_ref[0])
    flow = link_of(UPWARD_SCALE, conduct_ref[nz - 1], above[1]) * (above[0] - heat_ref[nz - 1])
    source_ref[nz - 1] += 2.0 * flow
    below, above = pick_halo("gy", y_halo, index_y % 2 == 1)
    flow = link_of(FLAT_SCALE, conduct_ref[:, 0, :], below[1]) * (below[0] - heat_ref[:, 0, :])
    source_ref[:, 0, :] += 2.0 * flow
    flow = link_of(FLAT_SCALE, conduct_ref[:, ny - 1, :], above[1])
    source_ref[:, ny - 1, :] += 2.0 * flow * (above[0] - heat_ref[:, ny - 1, :])
    source = source_ref[...].reshape(nz * ny, nx).T
    part = reduce_source(source, 0, left_ref, right_ref, inverse_ref[...])
    part_ref[...] = part
    message_ref[...] = jnp.concatenate(
        [
            source[:1] + ends_ref[0:1] * part[1:2],
            source[nx - 1 :] + ends_ref[1:2] * part[nx - 2 : nx - 1],
            ends_ref[2:8],
        ],
        0,
    )


def end_bands(link, first, last, axis, high, own):
    length = high.shape[axis]
    at = lambda values, i: lax.index_in_dim(values, i, axis, keepdims=False)
    return (
        1.0 + first * at(own, 1),
        1.0 + last * at(own, length - 2),
        first * at(high, 1),
    )


def yz_bands_kernel(
    halo_counts, conduct_ref, edge_ref, *refs
):
    z_halo, y_halo = refs[: halo_counts[0]], refs[halo_counts[0] : sum(halo_counts)]
    (
        yl_ref, yr_ref, ylow_ref, yhigh_ref, yinv_ref, yends_ref,
        zl_ref, zr_ref, zlow_ref, zhigh_ref, zinv_ref, zends_ref,
    ) = refs[sum(halo_counts) :]
    nz, ny, nx = conduct_ref.shape
    index_z, index_y = lax.axis_index("gz"), lax.axis_index("gy")
    conduct = conduct_ref[...]
    row = lax.broadcasted_iota(jnp.int32, conduct.shape, 1)
    link = jnp.where(row > 0, link_of(FLAT_SCALE, conduct, roll(conduct, 1, 1)), 0.0)
    low, high, inverse, own = reduce_interior(link, 1, yl_ref, yr_ref)
    ylow_ref[...], yhigh_ref[...], yinv_ref[...] = low, high, inverse
    below, above = pick_halo("gy", y_halo, index_y % 2 == 1)
    first = link_of(FLAT_SCALE, conduct_ref[:, 0, :], conduct_ref[:, 1, :])
    last = link_of(FLAT_SCALE, conduct_ref[:, ny - 1, :], conduct_ref[:, ny - 2, :])
    own_first, own_last, between = end_bands(link, first, last, 1, high, own)
    outer_low = link_of(FLAT_SCALE, conduct_ref[:, 0, :], below[1])
    outer_high = link_of(FLAT_SCALE, conduct_ref[:, ny - 1, :], above[1])
    for i, value in enumerate((first, last, own_first, own_last, between, outer_low, outer_high)):
        yends_ref[i] = value
    link = link_of(UPWARD_SCALE, conduct[1:], conduct[:-1])
    link = jnp.concatenate([jnp.zeros_like(conduct[:1]), link], 0)
    low, high, inverse, own = reduce_interior(link, 0, zl_ref, zr_ref)
    zlow_ref[...], zhigh_ref[...], zinv_ref[...] = low, high, inverse
    below, above = pick_halo("gz", z_halo, index_z % 2 == 1)
    own_first, own_last, between = end_bands(link, link[1], link[nz - 1], 0, high, own)
    ground = UPWARD_SCALE * conduct[0] * edge_ref[...].astype(F32)
    own_first = own_first + jnp.where(index_z == 0, ground, 0.0)
    outer = link_of(UPWARD_SCALE, conduct[0], below[1])
    for i, value in enumerate((link[1], link[nz - 1], own_first, own_last, between, outer)):
        zends_ref[i] = value


def chain_message(ends_ref, source_first, source_last, message_ref):
    own_first, own_last, between, outer = (ends_ref[i] for i in range(2, 6))
    inverse = 1.0 / (own_first + between + outer)
    message_ref[0] = outer * between * inverse
    message_ref[1] = outer * own_first * inverse
    message_ref[2] = outer * inverse * source_first
    message_ref[3] = own_last + between * own_first * inverse
    message_ref[4] = source_last + between * inverse * source_first


def chain_ends(name, messages, ends_ref, source_first, blocks_ref, state_ref):
    count, index = lax.axis_size(name), lax.axis_index(name)
    for mask, message in enumerate(messages):
        blocks_ref[index ^ mask] = message[...]
    blocks = [tuple(blocks_ref[k, i] for i in range(5)) for k in range(count)]
    below, last = chain(blocks, count, index, state_ref)
    own_first, between, outer = ends_ref[2], ends_ref[4], ends_ref[5]
    first = (source_first + outer * below + between * last) / (own_first + between + outer)
    return first, last


def y_source_kernel(
    count_x, count_y, heat_ref, part_ref, low_ref, high_ref, yl_ref, yr_ref, yinv_ref, yends_ref,
    *refs
):
    messages, (ypart_ref, ysource_ref, message_ref, blocks_ref, rows_ref, state_ref, d_ref) = (
        refs[:count_x], refs[count_x:]
    )
    nz, ny, nx = heat_ref.shape
    index = lax.axis_index("gx")
    for mask, message in enumerate(messages):
        blocks_ref[index ^ mask] = message[...]
    first, last, own_first, own_last, between, c_first, c_last = (
        blocks_ref[:, i, :] for i in range(7)
    )
    before = jnp.concatenate([jnp.zeros_like(c_last[:1]), c_last[:-1]], 0)
    outer = link_of(FLAT_SCALE, c_first, before)
    inverse = 1.0 / (own_first + between + outer)
    rows = (
        outer * between * inverse,
        outer * own_first * inverse,
        outer * inverse * first,
        own_last + between * own_first * inverse,
        last + between * inverse * first,
        first * inverse,
        outer * inverse,
        between * inverse,
    )
    for i, value in enumerate(rows):
        rows_ref[i] = value
    whole = lambda i, k: jnp.broadcast_to(rows_ref[i, pl.ds(k, 1), :], (8, rows_ref.shape[2]))
    blocks = [tuple(whole(i, k) for i in range(5)) for k in range(count_x)]
    below, last = chain(blocks, count_x, index, state_ref)
    first = whole(5, index) + whole(6, index) * below + whole(7, index) * last
    lines = part_ref[...] + low_ref[...] * first[:1] + high_ref[...] * last[:1]
    source = lines.T.reshape(nz, ny, nx) - 2.0 * heat_ref[...]
    d_ref[...] = source
    part = reduce_source(source, 1, yl_ref, yr_ref, yinv_ref[...])
    ypart_ref[...] = part
    source_first = d_ref[:, 0, :] + yends_ref[0] * ypart_ref[:, 1, :]
    source_last = d_ref[:, ny - 1, :] + yends_ref[1] * ypart_ref[:, ny - 2, :]
    ysource_ref[0], ysource_ref[1] = source_first, source_last
    if count_y > 2:
        chain_message(yends_ref, source_first, source_last, message_ref)
        return
    odd = lax.axis_index("gy") % 2 == 1
    near_own = jnp.where(odd, yends_ref[2], yends_ref[3])
    far_own = jnp.where(odd, yends_ref[3], yends_ref[2])
    share = yends_ref[4] / (far_own + yends_ref[4])
    message_ref[0] = near_own + share * far_own
    message_ref[1] = jnp.where(odd, source_first, source_last) + share * jnp.where(
        odd, source_last, source_first
    )


def z_source_kernel(
    count_y, ypart_ref, ylow_ref, yhigh_ref, yends_ref, ysource_ref, zl_ref, zr_ref, zinv_ref,
    zends_ref, *refs
):
    messages, (zpart_ref, zsource_ref, message_ref, ends_ref, blocks_ref, state_ref) = (
        refs[:count_y], refs[count_y:]
    )
    nz, ny, nx = ypart_ref.shape
    if count_y > 2:
        first, last = chain_ends("gy", messages, yends_ref, ysource_ref[0], blocks_ref, state_ref)
    else:
        odd = lax.axis_index("gy") % 2 == 1
        mine, other = messages
        outer = jnp.where(odd, yends_ref[5], yends_ref[6])
        between = yends_ref[4]
        factor = outer / (other[0] + outer)
        near = (mine[1] + factor * other[1]) / (mine[0] + factor * other[0])
        far_own = jnp.where(odd, yends_ref[3], yends_ref[2])
        far_source = jnp.where(odd, ysource_ref[1], ysource_ref[0])
        far = (far_source + between * near) / (far_own + between)
        first, last = jnp.where(odd, near, far), jnp.where(odd, far, near)
    ends_ref[0], ends_ref[1] = first, last
    source = jnp.stack(
        [
            ypart_ref[k]
            + ylow_ref[k] * ends_ref[0, pl.ds(k, 1), :]
            + yhigh_ref[k] * ends_ref[1, pl.ds(k, 1), :]
            for k in range(nz)
        ],
        0,
    )
    part = reduce_source(source, 0, zl_ref, zr_ref, zinv_ref[...])
    zpart_ref[...] = part
    source_first = source[0] + zends_ref[0] * part[1]
    source_last = source[nz - 1] + zends_ref[1] * part[nz - 2]
    zsource_ref[...] = source_first
    chain_message(zends_ref, source_first, source_last, message_ref)


def finish_kernel(
    count_z, heat_ref, zpart_ref, zlow_ref, zhigh_ref, zends_ref, zsource_ref, *refs
):
    messages, (out_ref, blocks_ref, state_ref) = refs[:count_z], refs[count_z:]
    first, last = chain_ends("gz", messages, zends_ref, zsource_ref[...], blocks_ref, state_ref)
    out_ref[...] = heat_ref[...] + zpart_ref[...] + zlow_ref[...] * first + zhigh_ref[...] * last


VMEM = pl.BlockSpec(memory_space=pltpu.VMEM)
SMEM = pl.BlockSpec(memory_space=pltpu.SMEM)


def call(kernel, outs, operands, scratch=(), specs=None, ops=200_000):
    return pl.pallas_call(
        kernel,
        out_shape=[jax.ShapeDtypeStruct(shape, F32) for shape in outs],
        in_specs=specs or [VMEM] * len(operands),
        out_specs=[VMEM] * len(outs),
        scratch_shapes=[pltpu.VMEM(shape, F32) for shape in scratch],
        compiler_params=pltpu.CompilerParams(vmem_limit_bytes=32 * 1024 * 1024),
        cost_estimate=pl.CostEstimate(flops=ops, bytes_accessed=ops, transcendentals=0),
    )(*operands)


def neighbour_swaps(name, other, low_first, second):
    count, width = lax.axis_size(name), lax.axis_size(other)
    received = [lax.ppermute(low_first, name, [(i, i ^ 1) for i in range(count)])]
    if count > 2:
        pairs = []
        for j in range(width):
            for i in range(count):
                at = (j ^ 1, i) if i in (0, count - 1) else (j, ((i + 1) ^ 1) - 1)
                pairs.append(((j, i), at))
        if (other, name) == ("gy", "gz"):
            axes, place = (other, name), lambda at: at[0] * count + at[1]
        else:
            axes, place = (name, other), lambda at: at[1] * width + at[0]
        pairs = [(place(source), place(target)) for source, target in pairs]
        received.append(lax.ppermute(second, axes, pairs))
    return received


def swap_all(name, message):
    count = lax.axis_size(name)
    return [message] + [
        lax.ppermute(message, name, [(i, i ^ mask) for i in range(count)])
        for mask in range(1, count)
    ]


def local(heat, label, table, edge):
    nz, ny, nx = heat.shape
    block, lines, layer, rows = (nz, ny, nx), (nx, nz * ny), (ny, nx), (nz, nx)
    count_x, count_y, count_z = (lax.axis_size(name) for name in ("gx", "gy", "gz"))
    x_steps, y_steps, z_steps = (len(steps_of(length)) for length in (nx, ny, nz))

    conduct, za, zb, ya, yb = call(
        start_kernel,
        [block, (2, *layer), (2, *layer), (2, *rows), (2, *rows)],
        [heat, label, table],
        specs=[VMEM, VMEM, SMEM],
    )
    z_halo = neighbour_swaps("gz", "gy", za, zb)
    y_halo = neighbour_swaps("gy", "gz", ya, yb)
    halo_counts = (len(z_halo), len(y_halo))

    x_left, x_right, x_low, x_high, x_inverse, x_ends, source = call(
        x_bands_kernel,
        [(x_steps, *lines)] * 2 + [lines] * 3 + [(8, lines[1]), block],
        [heat, conduct],
    )
    x_part, x_message = call(
        functools.partial(x_source_kernel, halo_counts),
        [lines, (8, lines[1])],
        [heat, conduct, edge, source, x_left, x_right, x_inverse, x_ends, *z_halo, *y_halo],
        [block],
    )
    x_messages = swap_all("gx", x_message)
    (
        y_left, y_right, y_low, y_high, y_inverse, y_ends,
        z_left, z_right, z_low, z_high, z_inverse, z_ends,
    ) = call(
        functools.partial(yz_bands_kernel, halo_counts),
        [(y_steps, *block)] * 2 + [block] * 3 + [(7, *rows)]
        + [(z_steps, *block)] * 2 + [block] * 3 + [(6, *layer)],
        [conduct, edge, *z_halo, *y_halo],
    )
    y_rows = 5 if count_y > 2 else 2
    y_part, y_source, y_message = call(
        functools.partial(y_source_kernel, count_x, count_y),
        [block, (2, *rows), (y_rows, *rows)],
        [heat, x_part, x_low, x_high, y_left, y_right, y_inverse, y_ends, *x_messages],
        [(count_x, 8, lines[1]), (8, count_x, lines[1]), (5, count_x, 8, lines[1]), block],
    )
    y_messages = swap_all("gy", y_message)
    z_part, z_source, z_message = call(
        functools.partial(z_source_kernel, count_y),
        [block, layer, (5, *layer)],
        [y_part, y_low, y_high, y_ends, y_source, z_left, z_right, z_inverse, z_ends, *y_messages],
        [(2, *rows), (count_y, y_rows, *rows), (5, count_y, *rows)],
    )
    z_messages = swap_all("gz", z_message)
    (heated,) = call(
        functools.partial(finish_kernel, count_z),
        [block],
        [heat, z_part, z_low, z_high, z_ends, z_source, *z_messages],
        [(count_z, 5, *layer), (5, count_z, *layer)],
    )
    return heated


def solution(mesh):
    return jax.shard_map(
        local,
        mesh=mesh,
        in_specs=(P("gz", "gy", "gx"), P("gz", "gy", "gx"), P(), P("gy", "gx")),
        out_specs=P("gz", "gy", "gx"),
        check_vma=False,
    )
```

```python
import functools

import jax
import jax.numpy as jnp
from jax import lax
from jax.experimental import pallas as pl
from jax.experimental.pallas import tpu as pltpu
from jax.sharding import PartitionSpec as P

FLAT_SCALE = 1000.0
UPWARD_SCALE = 200.0
F32 = jnp.float32


def link_of(scale, one, other):
    return scale * one * other / (one + other)


def roll(values, offset, axis):
    if axis == 0 and values.ndim == 3:
        offset = offset % values.shape[0]
        return jnp.concatenate([values[-offset:], values[:-offset]], 0)
    return pltpu.roll(values, offset % values.shape[axis], axis)


def steps_of(length):
    steps, distance = [], 1
    while distance < length - 1:
        steps.append(distance)
        distance *= 2
    return steps


def reduce_interior(link, axis, left_ref, right_ref):
    length = link.shape[axis]
    row = lax.broadcasted_iota(jnp.int32, link.shape, axis)
    low, high, own = link, roll(link, -1, axis), jnp.ones_like(link)
    high = jnp.where(row == length - 1, 0.0, high)
    for step, distance in enumerate(steps_of(length)):
        inverse = 1.0 / (own + low + high)
        open_low, open_high = row > distance, row < length - 1 - distance
        left = jnp.where(open_low, low * roll(inverse, distance, axis), 0.0)
        right = jnp.where(open_high, high * roll(inverse, -distance, axis), 0.0)
        left_ref[step], right_ref[step] = left, right
        own = own + left * roll(own, distance, axis) + right * roll(own, -distance, axis)
        low = jnp.where(open_low, left * roll(low, distance, axis), low)
        high = jnp.where(open_high, right * roll(high, -distance, axis), high)
    inverse = 1.0 / (own + low + high)
    inner = (row > 0) & (row < length - 1)
    share_low = jnp.where(inner, low * inverse, jnp.where(row == 0, 1.0, 0.0))
    share_high = jnp.where(inner, high * inverse, jnp.where(row == 0, 0.0, 1.0))
    return share_low, share_high, jnp.where(inner, inverse, 0.0), own * inverse


def reduce_source(source, axis, left_ref, right_ref, inverse):
    length = source.shape[axis]
    for step, distance in enumerate(steps_of(length)):
        source = (
            source
            + left_ref[step] * roll(source, distance, axis)
            + right_ref[step] * roll(source, -distance, axis)
        )
    return source * inverse


def chain(blocks, count, index, state):
    own = [blocks[k][3] + (blocks[k + 1][1] if k + 1 < count else 0.0) for k in range(count)]
    source = [blocks[k][4] + (blocks[k + 1][2] if k + 1 < count else 0.0) for k in range(count)]
    shape = own[0].shape
    state[0, 0], state[1, 0] = jnp.ones(shape, F32), jnp.zeros(shape, F32)
    up_own, up_source = own[0], source[0]
    for k in range(1, count):
        state[0, k], state[1, k] = up_own, up_source
        factor = blocks[k][0] / (up_own + blocks[k][0])
        up_own, up_source = own[k] + factor * up_own, source[k] + factor * up_source
    down_own, down_source = own[count - 1], source[count - 1]
    state[2, count - 1], state[3, count - 1] = down_own, down_source
    for k in range(count - 2, -1, -1):
        factor = blocks[k + 1][0] / (down_own + blocks[k + 1][0])
        down_own, down_source = own[k] + factor * down_own, source[k] + factor * down_source
        state[2, k], state[3, k] = down_own, down_source
    for k in range(count):
        state[4, k] = blocks[k][0]
    up_own, up_source, down_own, down_source, link = (state[i, index] for i in range(5))
    inverse = 1.0 / (up_own * down_own + link * (up_own + down_own))
    below = ((down_own + link) * up_source + link * down_source) * inverse
    here = ((up_own + link) * down_source + link * up_source) * inverse
    return below, here


def pick_halo(name, received, odd):
    first = received[0][...]
    second = received[1][...] if len(received) > 1 else jnp.zeros_like(first)
    index, count = lax.axis_index(name), lax.axis_size(name)
    below = jnp.where(odd, first, second)
    above = jnp.where(odd, second, first)
    return jnp.where(index > 0, below, 0.0), jnp.where(index < count - 1, above, 0.0)


def look_up(label, table_ref):
    conduct = jnp.broadcast_to(table_ref[0], label.shape)
    for entry in range(1, table_ref.shape[0]):
        conduct = jnp.where(label == entry, table_ref[entry], conduct)
    return conduct


def stage_kernel(
    heat_in, label_in, table_in, edge_in, heat_ref, conduct_ref, table_ref, edge_ref, label_ref,
    entries_ref, sems
):
    copies = [
        pltpu.make_async_copy(source, target, sems.at[i])
        for i, (source, target) in enumerate(
            (
                (table_in, entries_ref), (label_in, label_ref), (heat_in, heat_ref),
                (edge_in, edge_ref),
            )
        )
    ]
    for copy in copies:
        copy.start()
    copies[0].wait()
    for entry in range(table_ref.shape[0]):
        table_ref[entry] = jnp.full(table_ref.shape[1:], entries_ref[entry], F32)
    copies[1].wait()
    conduct_ref[...] = look_up(label_ref[...], table_ref)
    copies[2].wait()
    copies[3].wait()


def start_kernel(
    heat_a_ref, label_a_ref, edge_a_ref, heat_b_ref, conduct_b_ref, edge_b_ref, table_ref,
    heat_ref, conduct_ref, edge_ref, za_ref, zb_ref, ya_ref, yb_ref
):
    nx = heat_a_ref.shape[-1]
    heat_ref[:, :, :nx], heat_ref[:, :, nx:] = heat_a_ref[...], heat_b_ref[...]
    conduct_ref[:, :, :nx] = look_up(label_a_ref[...], table_ref)
    conduct_ref[:, :, nx:] = conduct_b_ref[...]
    edge_ref[:, :nx] = edge_a_ref[...].astype(F32)
    edge_ref[:, nx:] = edge_b_ref[...].astype(F32)
    odd_z = lax.axis_index("gz") % 2 == 1
    odd_y = lax.axis_index("gy") % 2 == 1
    for i, ref in enumerate((heat_ref, conduct_ref)):
        low, high = ref[0], ref[ref.shape[0] - 1]
        za_ref[i] = jnp.where(odd_z, low, high)
        zb_ref[i] = jnp.where(odd_z, high, low)
        low, high = ref[:, 0, :], ref[:, ref.shape[1] - 1, :]
        ya_ref[i] = jnp.where(odd_y, low, high)
        yb_ref[i] = jnp.where(odd_y, high, low)


def x_bands_kernel(
    heat_ref, conduct_ref, left_ref, right_ref, low_ref, high_ref, inverse_ref, ends_ref, local_ref
):
    nz, ny, nx = conduct_ref.shape
    conduct = conduct_ref[...]
    heat = heat_ref[...]
    local = 2.0 * heat
    across = 2.0 * link_of(UPWARD_SCALE, conduct[1:], conduct[:-1]) * (heat[1:] - heat[:-1])
    nothing = jnp.zeros_like(heat[:1])
    local = local + jnp.concatenate([across, nothing], 0) - jnp.concatenate([nothing, across], 0)
    row = lax.broadcasted_iota(jnp.int32, conduct.shape, 1)
    across = 2.0 * link_of(FLAT_SCALE, conduct, roll(conduct, 1, 1)) * (heat - roll(heat, 1, 1))
    across = jnp.where(row > 0, across, 0.0)
    local_ref[...] = local - across + roll(across, -1, 1)
    lines = conduct.reshape(nz * ny, nx).T
    row = lax.broadcasted_iota(jnp.int32, lines.shape, 0)
    link = jnp.where(row > 0, link_of(FLAT_SCALE, lines, roll(lines, 1, 0)), 0.0)
    low, high, inverse, own = reduce_interior(link, 0, left_ref, right_ref)
    low_ref[...], high_ref[...], inverse_ref[...] = low, high, inverse
    first, last = link[1:2], link[nx - 1 :]
    ends_ref[...] = jnp.concatenate(
        [
            first,
            last,
            1.0 + first * own[1:2],
            1.0 + last * own[nx - 2 : nx - 1],
            first * high[1:2],
            lines[:1],
            lines[nx - 1 :],
            jnp.zeros_like(first),
        ],
        0,
    )


def x_source_kernel(
    halo_counts, heat_ref, conduct_ref, edge_ref, local_ref, left_ref, right_ref, inverse_ref,
    ends_ref, *refs
):
    z_halo, y_halo = refs[: halo_counts[0]], refs[halo_counts[0] : sum(halo_counts)]
    part_ref, message_ref, source_ref = refs[sum(halo_counts) :]
    nz, ny, nx = conduct_ref.shape
    index_z, index_y = lax.axis_index("gz"), lax.axis_index("gy")
    below, above = pick_halo("gz", z_halo, index_z % 2 == 1)
    source_ref[...] = local_ref[...]
    ground = UPWARD_SCALE * conduct_ref[0] * edge_ref[...]
    ground = jnp.where(index_z == 0, ground, 0.0)
    flow = link_of(UPWARD_SCALE, conduct_ref[0], below[1]) * (below[0] - heat_ref[0])
    source_ref[0] += 2.0 * (flow - ground * heat_ref[0])
    flow = link_of(UPWARD_SCALE, conduct_ref[nz - 1], above[1]) * (above[0] - heat_ref[nz - 1])
    source_ref[nz - 1] += 2.0 * flow
    below, above = pick_halo("gy", y_halo, index_y % 2 == 1)
    flow = link_of(FLAT_SCALE, conduct_ref[:, 0, :], below[1]) * (below[0] - heat_ref[:, 0, :])
    source_ref[:, 0, :] += 2.0 * flow
    flow = link_of(FLAT_SCALE, conduct_ref[:, ny - 1, :], above[1])
    source_ref[:, ny - 1, :] += 2.0 * flow * (above[0] - heat_ref[:, ny - 1, :])
    source = source_ref[...].reshape(nz * ny, nx).T
    part = reduce_source(source, 0, left_ref, right_ref, inverse_ref[...])
    part_ref[...] = part
    message_ref[...] = jnp.concatenate(
        [
            source[:1] + ends_ref[0:1] * part[1:2],
            source[nx - 1 :] + ends_ref[1:2] * part[nx - 2 : nx - 1],
            ends_ref[2:8],
        ],
        0,
    )


def end_bands(link, first, last, axis, high, own):
    length = high.shape[axis]
    at = lambda values, i: lax.index_in_dim(values, i, axis, keepdims=False)
    return (
        1.0 + first * at(own, 1),
        1.0 + last * at(own, length - 2),
        first * at(high, 1),
    )


def yz_bands_kernel(
    halo_counts, conduct_ref, edge_ref, *refs
):
    z_halo, y_halo = refs[: halo_counts[0]], refs[halo_counts[0] : sum(halo_counts)]
    (
        yl_ref, yr_ref, ylow_ref, yhigh_ref, yinv_ref, yends_ref,
        zl_ref, zr_ref, zlow_ref, zhigh_ref, zinv_ref, zends_ref,
    ) = refs[sum(halo_counts) :]
    nz, ny, nx = conduct_ref.shape
    index_z, index_y = lax.axis_index("gz"), lax.axis_index("gy")
    conduct = conduct_ref[...]
    row = lax.broadcasted_iota(jnp.int32, conduct.shape, 1)
    link = jnp.where(row > 0, link_of(FLAT_SCALE, conduct, roll(conduct, 1, 1)), 0.0)
    low, high, inverse, own = reduce_interior(link, 1, yl_ref, yr_ref)
    ylow_ref[...], yhigh_ref[...], yinv_ref[...] = low, high, inverse
    below, above = pick_halo("gy", y_halo, index_y % 2 == 1)
    first = link_of(FLAT_SCALE, conduct_ref[:, 0, :], conduct_ref[:, 1, :])
    last = link_of(FLAT_SCALE, conduct_ref[:, ny - 1, :], conduct_ref[:, ny - 2, :])
    own_first, own_last, between = end_bands(link, first, last, 1, high, own)
    outer_low = link_of(FLAT_SCALE, conduct_ref[:, 0, :], below[1])
    outer_high = link_of(FLAT_SCALE, conduct_ref[:, ny - 1, :], above[1])
    for i, value in enumerate((first, last, own_first, own_last, between, outer_low, outer_high)):
        yends_ref[i] = value
    link = link_of(UPWARD_SCALE, conduct[1:], conduct[:-1])
    link = jnp.concatenate([jnp.zeros_like(conduct[:1]), link], 0)
    low, high, inverse, own = reduce_interior(link, 0, zl_ref, zr_ref)
    zlow_ref[...], zhigh_ref[...], zinv_ref[...] = low, high, inverse
    below, above = pick_halo("gz", z_halo, index_z % 2 == 1)
    own_first, own_last, between = end_bands(link, link[1], link[nz - 1], 0, high, own)
    ground = UPWARD_SCALE * conduct[0] * edge_ref[...]
    own_first = own_first + jnp.where(index_z == 0, ground, 0.0)
    outer = link_of(UPWARD_SCALE, conduct[0], below[1])
    for i, value in enumerate((link[1], link[nz - 1], own_first, own_last, between, outer)):
        zends_ref[i] = value


def chain_message(ends_ref, source_first, source_last, message_ref):
    own_first, own_last, between, outer = (ends_ref[i] for i in range(2, 6))
    inverse = 1.0 / (own_first + between + outer)
    message_ref[0] = outer * between * inverse
    message_ref[1] = outer * own_first * inverse
    message_ref[2] = outer * inverse * source_first
    message_ref[3] = own_last + between * own_first * inverse
    message_ref[4] = source_last + between * inverse * source_first


def chain_ends(name, messages, ends_ref, source_first, blocks_ref, state_ref):
    count, index = lax.axis_size(name), lax.axis_index(name)
    for mask, message in enumerate(messages):
        blocks_ref[index ^ mask] = message[...]
    blocks = [tuple(blocks_ref[k, i] for i in range(5)) for k in range(count)]
    below, last = chain(blocks, count, index, state_ref)
    own_first, between, outer = ends_ref[2], ends_ref[4], ends_ref[5]
    first = (source_first + outer * below + between * last) / (own_first + between + outer)
    return first, last


def y_source_kernel(
    count_x, count_y, heat_ref, part_ref, low_ref, high_ref, yl_ref, yr_ref, yinv_ref, yends_ref,
    *refs
):
    messages, (ypart_ref, ysource_ref, message_ref, blocks_ref, rows_ref, state_ref, d_ref) = (
        refs[:count_x], refs[count_x:]
    )
    nz, ny, nx = heat_ref.shape
    index = lax.axis_index("gx") // 2
    for mask, message in enumerate(messages):
        blocks_ref[index ^ mask] = message[...]
    first, last, own_first, own_last, between, c_first, c_last = (
        blocks_ref[:, i, :] for i in range(7)
    )
    before = jnp.concatenate([jnp.zeros_like(c_last[:1]), c_last[:-1]], 0)
    outer = link_of(FLAT_SCALE, c_first, before)
    inverse = 1.0 / (own_first + between + outer)
    rows = (
        outer * between * inverse,
        outer * own_first * inverse,
        outer * inverse * first,
        own_last + between * own_first * inverse,
        last + between * inverse * first,
        first * inverse,
        outer * inverse,
        between * inverse,
    )
    for i, value in enumerate(rows):
        rows_ref[i] = value
    whole = lambda i, k: jnp.broadcast_to(rows_ref[i, pl.ds(k, 1), :], (8, rows_ref.shape[2]))
    blocks = [tuple(whole(i, k) for i in range(5)) for k in range(count_x)]
    below, last = chain(blocks, count_x, index, state_ref)
    first = whole(5, index) + whole(6, index) * below + whole(7, index) * last
    lines = part_ref[...] + low_ref[...] * first[:1] + high_ref[...] * last[:1]
    source = lines.T.reshape(nz, ny, nx) - 2.0 * heat_ref[...]
    d_ref[...] = source
    part = reduce_source(source, 1, yl_ref, yr_ref, yinv_ref[...])
    ypart_ref[...] = part
    source_first = d_ref[:, 0, :] + yends_ref[0] * ypart_ref[:, 1, :]
    source_last = d_ref[:, ny - 1, :] + yends_ref[1] * ypart_ref[:, ny - 2, :]
    ysource_ref[0], ysource_ref[1] = source_first, source_last
    if count_y > 2:
        chain_message(yends_ref, source_first, source_last, message_ref)
        return
    odd = lax.axis_index("gy") % 2 == 1
    near_own = jnp.where(odd, yends_ref[2], yends_ref[3])
    far_own = jnp.where(odd, yends_ref[3], yends_ref[2])
    share = yends_ref[4] / (far_own + yends_ref[4])
    message_ref[0] = near_own + share * far_own
    message_ref[1] = jnp.where(odd, source_first, source_last) + share * jnp.where(
        odd, source_last, source_first
    )


def z_source_kernel(
    count_y, ypart_ref, ylow_ref, yhigh_ref, yends_ref, ysource_ref, zl_ref, zr_ref, zinv_ref,
    zends_ref, *refs
):
    messages, (zpart_ref, zsource_ref, message_ref, ends_ref, blocks_ref, state_ref) = (
        refs[:count_y], refs[count_y:]
    )
    nz, ny, nx = ypart_ref.shape
    if count_y > 2:
        first, last = chain_ends("gy", messages, yends_ref, ysource_ref[0], blocks_ref, state_ref)
    else:
        odd = lax.axis_index("gy") % 2 == 1
        mine, other = messages
        outer = jnp.where(odd, yends_ref[5], yends_ref[6])
        between = yends_ref[4]
        factor = outer / (other[0] + outer)
        near = (mine[1] + factor * other[1]) / (mine[0] + factor * other[0])
        far_own = jnp.where(odd, yends_ref[3], yends_ref[2])
        far_source = jnp.where(odd, ysource_ref[1], ysource_ref[0])
        far = (far_source + between * near) / (far_own + between)
        first, last = jnp.where(odd, near, far), jnp.where(odd, far, near)
    ends_ref[0], ends_ref[1] = first, last
    source = jnp.stack(
        [
            ypart_ref[k]
            + ylow_ref[k] * ends_ref[0, pl.ds(k, 1), :]
            + yhigh_ref[k] * ends_ref[1, pl.ds(k, 1), :]
            for k in range(nz)
        ],
        0,
    )
    part = reduce_source(source, 0, zl_ref, zr_ref, zinv_ref[...])
    zpart_ref[...] = part
    source_first = source[0] + zends_ref[0] * part[1]
    source_last = source[nz - 1] + zends_ref[1] * part[nz - 2]
    zsource_ref[...] = source_first
    chain_message(zends_ref, source_first, source_last, message_ref)


def finish_kernel(
    count_z, heat_ref, zpart_ref, zlow_ref, zhigh_ref, zends_ref, zsource_ref, *refs
):
    messages, (theirs_ref, mine_ref, blocks_ref, state_ref) = refs[:count_z], refs[count_z:]
    first, last = chain_ends("gz", messages, zends_ref, zsource_ref[...], blocks_ref, state_ref)
    nx = theirs_ref.shape[-1]
    heated = heat_ref[...] + zpart_ref[...] + zlow_ref[...] * first + zhigh_ref[...] * last
    theirs_ref[...], mine_ref[...] = heated[:, :, :nx], heated[:, :, nx:]


VMEM = pl.BlockSpec(memory_space=pltpu.VMEM)
HBM = pl.BlockSpec(memory_space=pltpu.HBM)


def call(kernel, outs, operands, scratch=(), specs=None, ops=200_000, vmem=32):
    return pl.pallas_call(
        kernel,
        out_shape=[jax.ShapeDtypeStruct(out, F32) if isinstance(out, tuple) else out for out in outs],
        in_specs=specs or [VMEM] * len(operands),
        out_specs=[VMEM] * len(outs),
        scratch_shapes=[pltpu.VMEM(item, F32) if isinstance(item, tuple) else item for item in scratch],
        compiler_params=pltpu.CompilerParams(vmem_limit_bytes=vmem * 1024 * 1024),
        cost_estimate=pl.CostEstimate(flops=ops, bytes_accessed=ops, transcendentals=0),
    )(*operands)


def neighbour_swaps(name, other, low_first, second):
    count, width = lax.axis_size(name), lax.axis_size(other)
    received = [lax.ppermute(low_first, name, [(i, i ^ 1) for i in range(count)])]
    if count > 2:
        pairs = []
        for j in range(width):
            for i in range(count):
                at = (j ^ 1, i) if i in (0, count - 1) else (j, ((i + 1) ^ 1) - 1)
                pairs.append(((j, i), at))
        if (other, name) == ("gy", "gz"):
            axes, place = (other, name), lambda at: at[0] * count + at[1]
        else:
            axes, place = (name, other), lambda at: at[1] * width + at[0]
        pairs = [(place(source), place(target)) for source, target in pairs]
        received.append(lax.ppermute(second, axes, pairs))
    return received


def swap_all(name, message, stride=1):
    count = lax.axis_size(name)
    return [message] + [
        lax.ppermute(message, name, [(i, i ^ mask) for i in range(count)])
        for mask in range(stride, count, stride)
    ]


def other_core(values):
    count = lax.axis_size("gx")
    return lax.ppermute(values, "gx", [(i, i ^ 1) for i in range(count)])


def chip_step(heat_a, label_a, edge_a, heat_b, conduct_b, edge_b, table):
    nz, ny, half = heat_a.shape
    nx = 2 * half
    block, lines, layer, rows = (nz, ny, nx), (nx, nz * ny), (ny, nx), (nz, nx)
    count_x, count_y, count_z = (lax.axis_size(name) for name in ("gx", "gy", "gz"))
    count_x = count_x // 2
    x_steps, y_steps, z_steps = (len(steps_of(length)) for length in (nx, ny, nz))

    heat, conduct, edge, za, zb, ya, yb = call(
        start_kernel,
        [block, block, layer, (2, *layer), (2, *layer), (2, *rows), (2, *rows)],
        [heat_a, label_a, edge_a, heat_b, conduct_b, edge_b, table],
    )
    z_halo = neighbour_swaps("gz", "gy", za, zb)
    y_halo = neighbour_swaps("gy", "gz", ya, yb)
    halo_counts = (len(z_halo), len(y_halo))

    x_left, x_right, x_low, x_high, x_inverse, x_ends, source = call(
        x_bands_kernel,
        [(x_steps, *lines)] * 2 + [lines] * 3 + [(8, lines[1]), block],
        [heat, conduct],
    )
    x_part, x_message = call(
        functools.partial(x_source_kernel, halo_counts),
        [lines, (8, lines[1])],
        [heat, conduct, edge, source, x_left, x_right, x_inverse, x_ends, *z_halo, *y_halo],
        [block],
    )
    x_messages = swap_all("gx", x_message, 2)
    (
        y_left, y_right, y_low, y_high, y_inverse, y_ends,
        z_left, z_right, z_low, z_high, z_inverse, z_ends,
    ) = call(
        functools.partial(yz_bands_kernel, halo_counts),
        [(y_steps, *block)] * 2 + [block] * 3 + [(7, *rows)]
        + [(z_steps, *block)] * 2 + [block] * 3 + [(6, *layer)],
        [conduct, edge, *z_halo, *y_halo],
    )
    y_rows = 5 if count_y > 2 else 2
    y_part, y_source, y_message = call(
        functools.partial(y_source_kernel, count_x, count_y),
        [block, (2, *rows), (y_rows, *rows)],
        [heat, x_part, x_low, x_high, y_left, y_right, y_inverse, y_ends, *x_messages],
        [(count_x, 8, lines[1]), (8, count_x, lines[1]), (5, count_x, 8, lines[1]), block],
    )
    y_messages = swap_all("gy", y_message)
    z_part, z_source, z_message = call(
        functools.partial(z_source_kernel, count_y),
        [block, layer, (5, *layer)],
        [y_part, y_low, y_high, y_ends, y_source, z_left, z_right, z_inverse, z_ends, *y_messages],
        [(2, *rows), (count_y, y_rows, *rows), (5, count_y, *rows)],
    )
    z_messages = swap_all("gz", z_message)
    return call(
        functools.partial(finish_kernel, count_z),
        [heat_a.shape] * 2,
        [heat, z_part, z_low, z_high, z_ends, z_source, *z_messages],
        [(count_z, 5, *layer), (5, count_z, *layer)],
    )


def local(heat, label, table, edge):
    others = [other_core(values) for values in (label, heat, edge)]
    entries = table.shape[0]
    own_heat, own_conduct, rows, own_edge = call(
        stage_kernel,
        [heat.shape, heat.shape, (entries, 8, heat.shape[-1]),
         jax.ShapeDtypeStruct(edge.shape, edge.dtype)],
        [heat, label, table, edge],
        [pltpu.VMEM(label.shape, label.dtype), pltpu.SMEM(table.shape, F32),
         pltpu.SemaphoreType.DMA((4,))],
        [HBM] * 4,
        vmem=60,
    )
    label_a, heat_a, edge_a = others
    second = lax.axis_index("gx") % 2 == 1
    theirs, mine = lax.cond(
        second,
        chip_step,
        lambda heat_a, label_a, edge_a, heat_b, *rest: (heat_a, heat_b),
        heat_a, label_a, edge_a, own_heat, own_conduct, own_edge, rows,
    )
    return jnp.where(second, mine, other_core(theirs))


def solution(mesh):
    return jax.shard_map(
        local,
        mesh=mesh,
        in_specs=(P("gz", "gy", "gx"), P("gz", "gy", "gx"), P(), P("gy", "gx")),
        out_specs=P("gz", "gy", "gx"),
        check_vma=False,
    )
```

```python
import functools

import jax
import jax.numpy as jnp
from jax import lax
from jax.experimental import pallas as pl
from jax.experimental.pallas import tpu as pltpu
from jax.sharding import PartitionSpec as P

FLAT_SCALE = 1000.0
UPWARD_SCALE = 200.0
F32 = jnp.float32


def link_of(scale, one, other):
    return scale * one * other / (one + other)


def roll(values, offset, axis):
    if axis == 0 and values.ndim == 3:
        offset = offset % values.shape[0]
        return jnp.concatenate([values[-offset:], values[:-offset]], 0)
    return pltpu.roll(values, offset % values.shape[axis], axis)


def steps_of(length):
    steps, distance = [], 1
    while distance < length - 1:
        steps.append(distance)
        distance *= 2
    return steps


def reduce_interior(link, axis, left_ref, right_ref):
    length = link.shape[axis]
    row = lax.broadcasted_iota(jnp.int32, link.shape, axis)
    low, high, own = link, roll(link, -1, axis), jnp.ones_like(link)
    high = jnp.where(row == length - 1, 0.0, high)
    for step, distance in enumerate(steps_of(length)):
        inverse = 1.0 / (own + low + high)
        open_low, open_high = row > distance, row < length - 1 - distance
        left = jnp.where(open_low, low * roll(inverse, distance, axis), 0.0)
        right = jnp.where(open_high, high * roll(inverse, -distance, axis), 0.0)
        left_ref[step], right_ref[step] = left, right
        own = own + left * roll(own, distance, axis) + right * roll(own, -distance, axis)
        low = jnp.where(open_low, left * roll(low, distance, axis), low)
        high = jnp.where(open_high, right * roll(high, -distance, axis), high)
    inverse = 1.0 / (own + low + high)
    inner = (row > 0) & (row < length - 1)
    share_low = jnp.where(inner, low * inverse, jnp.where(row == 0, 1.0, 0.0))
    share_high = jnp.where(inner, high * inverse, jnp.where(row == 0, 0.0, 1.0))
    return share_low, share_high, jnp.where(inner, inverse, 0.0), own * inverse


def reduce_source(source, axis, left_ref, right_ref, inverse):
    length = source.shape[axis]
    for step, distance in enumerate(steps_of(length)):
        source = (
            source
            + left_ref[step] * roll(source, distance, axis)
            + right_ref[step] * roll(source, -distance, axis)
        )
    return source * inverse


def chain(blocks, count, index, state):
    own = [blocks[k][3] + (blocks[k + 1][1] if k + 1 < count else 0.0) for k in range(count)]
    source = [blocks[k][4] + (blocks[k + 1][2] if k + 1 < count else 0.0) for k in range(count)]
    shape = own[0].shape
    state[0, 0], state[1, 0] = jnp.ones(shape, F32), jnp.zeros(shape, F32)
    up_own, up_source = own[0], source[0]
    for k in range(1, count):
        state[0, k], state[1, k] = up_own, up_source
        factor = blocks[k][0] / (up_own + blocks[k][0])
        up_own, up_source = own[k] + factor * up_own, source[k] + factor * up_source
    down_own, down_source = own[count - 1], source[count - 1]
    state[2, count - 1], state[3, count - 1] = down_own, down_source
    for k in range(count - 2, -1, -1):
        factor = blocks[k + 1][0] / (down_own + blocks[k + 1][0])
        down_own, down_source = own[k] + factor * down_own, source[k] + factor * down_source
        state[2, k], state[3, k] = down_own, down_source
    for k in range(count):
        state[4, k] = blocks[k][0]
    up_own, up_source, down_own, down_source, link = (state[i, index] for i in range(5))
    inverse = 1.0 / (up_own * down_own + link * (up_own + down_own))
    below = ((down_own + link) * up_source + link * down_source) * inverse
    here = ((up_own + link) * down_source + link * up_source) * inverse
    return below, here


def pick_halo(name, received, odd):
    first = received[0][...]
    second = received[1][...] if len(received) > 1 else jnp.zeros_like(first)
    index, count = lax.axis_index(name), lax.axis_size(name)
    below = jnp.where(odd, first, second)
    above = jnp.where(odd, second, first)
    return jnp.where(index > 0, below, 0.0), jnp.where(index < count - 1, above, 0.0)


def swaps_along(name):
    return min(lax.axis_size(name) - 1, 2)


def look_up(label, table_ref):
    conduct = jnp.broadcast_to(table_ref[0], label.shape)
    for entry in range(1, table_ref.shape[0]):
        conduct = jnp.where(label == entry, table_ref[entry], conduct)
    return conduct


def stage_kernel(
    heat_in, label_in, table_in, edge_in, heat_ref, conduct_ref, table_ref, edge_ref, label_ref,
    entries_ref, sems
):
    copies = [
        pltpu.make_async_copy(source, target, sems.at[i])
        for i, (source, target) in enumerate(
            (
                (table_in, entries_ref), (label_in, label_ref), (heat_in, heat_ref),
                (edge_in, edge_ref),
            )
        )
    ]
    for copy in copies:
        copy.start()
    copies[0].wait()
    for entry in range(table_ref.shape[0]):
        table_ref[entry] = jnp.full(table_ref.shape[1:], entries_ref[entry], F32)
    copies[1].wait()
    conduct_ref[...] = look_up(label_ref[...], table_ref)
    copies[2].wait()
    copies[3].wait()


def join_halos(z_halo, y_halo):
    return [*z_halo[1:], *y_halo, z_halo[0]]


def split_halos(counts, refs):
    halos = refs[: sum(counts)]
    return [halos[-1], *halos[: counts[0] - 1]], halos[counts[0] - 1 : -1]


def start_kernel(
    heat_a_ref, label_a_ref, edge_a_ref, heat_b_ref, conduct_b_ref, edge_b_ref, table_ref,
    heat_ref, conduct_ref, edge_ref, *faces
):
    nx = heat_a_ref.shape[-1]
    heat_ref[:, :, :nx], heat_ref[:, :, nx:] = heat_a_ref[...], heat_b_ref[...]
    conduct_ref[:, :, :nx] = look_up(label_a_ref[...], table_ref)
    conduct_ref[:, :, nx:] = conduct_b_ref[...]
    edge_ref[:, :nx] = edge_a_ref[...].astype(F32)
    edge_ref[:, nx:] = edge_b_ref[...].astype(F32)
    z_faces, y_faces = faces[: swaps_along("gz")], faces[swaps_along("gz") :]
    odd_z = lax.axis_index("gz") % 2 == 1
    odd_y = lax.axis_index("gy") % 2 == 1
    for i, ref in enumerate((heat_ref, conduct_ref)):
        low, high = ref[0], ref[ref.shape[0] - 1]
        for face_ref, pick in zip(z_faces, (odd_z, ~odd_z)):
            face_ref[i] = jnp.where(pick, low, high)
        low, high = ref[:, 0, :], ref[:, ref.shape[1] - 1, :]
        for face_ref, pick in zip(y_faces, (odd_y, ~odd_y)):
            face_ref[i] = jnp.where(pick, low, high)


def x_bands_kernel(
    heat_ref, conduct_ref, left_ref, right_ref, low_ref, high_ref, inverse_ref, ends_ref, local_ref
):
    nz, ny, nx = conduct_ref.shape
    conduct = conduct_ref[...]
    heat = heat_ref[...]
    local = 2.0 * heat
    across = 2.0 * link_of(UPWARD_SCALE, conduct[1:], conduct[:-1]) * (heat[1:] - heat[:-1])
    nothing = jnp.zeros_like(heat[:1])
    local = local + jnp.concatenate([across, nothing], 0) - jnp.concatenate([nothing, across], 0)
    row = lax.broadcasted_iota(jnp.int32, conduct.shape, 1)
    across = 2.0 * link_of(FLAT_SCALE, conduct, roll(conduct, 1, 1)) * (heat - roll(heat, 1, 1))
    across = jnp.where(row > 0, across, 0.0)
    local_ref[...] = local - across + roll(across, -1, 1)
    lines = conduct.reshape(nz * ny, nx).T
    row = lax.broadcasted_iota(jnp.int32, lines.shape, 0)
    link = jnp.where(row > 0, link_of(FLAT_SCALE, lines, roll(lines, 1, 0)), 0.0)
    low, high, inverse, own = reduce_interior(link, 0, left_ref, right_ref)
    low_ref[...], high_ref[...], inverse_ref[...] = low, high, inverse
    first, last = link[1:2], link[nx - 1 :]
    ends_ref[...] = jnp.concatenate(
        [
            first,
            last,
            1.0 + first * own[1:2],
            1.0 + last * own[nx - 2 : nx - 1],
            first * high[1:2],
            lines[:1],
            lines[nx - 1 :],
            jnp.zeros_like(first),
        ],
        0,
    )


def x_source_kernel(
    halo_counts, heat_ref, conduct_ref, edge_ref, local_ref, left_ref, right_ref, inverse_ref,
    ends_ref, *refs
):
    z_halo, y_halo = split_halos(halo_counts, refs)
    part_ref, message_ref, source_ref = refs[sum(halo_counts) :]
    nz, ny, nx = conduct_ref.shape
    index_z, index_y = lax.axis_index("gz"), lax.axis_index("gy")
    below, above = pick_halo("gz", z_halo, index_z % 2 == 1)
    source_ref[...] = local_ref[...]
    ground = UPWARD_SCALE * conduct_ref[0] * edge_ref[...]
    ground = jnp.where(index_z == 0, ground, 0.0)
    flow = link_of(UPWARD_SCALE, conduct_ref[0], below[1]) * (below[0] - heat_ref[0])
    source_ref[0] += 2.0 * (flow - ground * heat_ref[0])
    flow = link_of(UPWARD_SCALE, conduct_ref[nz - 1], above[1]) * (above[0] - heat_ref[nz - 1])
    source_ref[nz - 1] += 2.0 * flow
    below, above = pick_halo("gy", y_halo, index_y % 2 == 1)
    flow = link_of(FLAT_SCALE, conduct_ref[:, 0, :], below[1]) * (below[0] - heat_ref[:, 0, :])
    source_ref[:, 0, :] += 2.0 * flow
    flow = link_of(FLAT_SCALE, conduct_ref[:, ny - 1, :], above[1])
    source_ref[:, ny - 1, :] += 2.0 * flow * (above[0] - heat_ref[:, ny - 1, :])
    source = source_ref[...].reshape(nz * ny, nx).T
    part = reduce_source(source, 0, left_ref, right_ref, inverse_ref[...])
    part_ref[...] = part
    message_ref[...] = jnp.concatenate(
        [
            source[:1] + ends_ref[0:1] * part[1:2],
            source[nx - 1 :] + ends_ref[1:2] * part[nx - 2 : nx - 1],
            ends_ref[2:8],
        ],
        0,
    )


def end_bands(link, first, last, axis, high, own):
    length = high.shape[axis]
    at = lambda values, i: lax.index_in_dim(values, i, axis, keepdims=False)
    return (
        1.0 + first * at(own, 1),
        1.0 + last * at(own, length - 2),
        first * at(high, 1),
    )


def yz_bands_kernel(
    halo_counts, conduct_ref, edge_ref, *refs
):
    z_halo, y_halo = split_halos(halo_counts, refs)
    (
        yl_ref, yr_ref, ylow_ref, yhigh_ref, yinv_ref, yends_ref,
        zl_ref, zr_ref, zlow_ref, zhigh_ref, zinv_ref, zends_ref,
    ) = refs[sum(halo_counts) :]
    nz, ny, nx = conduct_ref.shape
    index_z, index_y = lax.axis_index("gz"), lax.axis_index("gy")
    conduct = conduct_ref[...]
    row = lax.broadcasted_iota(jnp.int32, conduct.shape, 1)
    link = jnp.where(row > 0, link_of(FLAT_SCALE, conduct, roll(conduct, 1, 1)), 0.0)
    low, high, inverse, own = reduce_interior(link, 1, yl_ref, yr_ref)
    ylow_ref[...], yhigh_ref[...], yinv_ref[...] = low, high, inverse
    below, above = pick_halo("gy", y_halo, index_y % 2 == 1)
    first = link_of(FLAT_SCALE, conduct_ref[:, 0, :], conduct_ref[:, 1, :])
    last = link_of(FLAT_SCALE, conduct_ref[:, ny - 1, :], conduct_ref[:, ny - 2, :])
    own_first, own_last, between = end_bands(link, first, last, 1, high, own)
    outer_low = link_of(FLAT_SCALE, conduct_ref[:, 0, :], below[1])
    outer_high = link_of(FLAT_SCALE, conduct_ref[:, ny - 1, :], above[1])
    for i, value in enumerate((first, last, own_first, own_last, between, outer_low, outer_high)):
        yends_ref[i] = value
    link = link_of(UPWARD_SCALE, conduct[1:], conduct[:-1])
    link = jnp.concatenate([jnp.zeros_like(conduct[:1]), link], 0)
    low, high, inverse, own = reduce_interior(link, 0, zl_ref, zr_ref)
    zlow_ref[...], zhigh_ref[...], zinv_ref[...] = low, high, inverse
    below, above = pick_halo("gz", z_halo, index_z % 2 == 1)
    own_first, own_last, between = end_bands(link, link[1], link[nz - 1], 0, high, own)
    ground = UPWARD_SCALE * conduct[0] * edge_ref[...]
    own_first = own_first + jnp.where(index_z == 0, ground, 0.0)
    outer = link_of(UPWARD_SCALE, conduct[0], below[1])
    for i, value in enumerate((link[1], link[nz - 1], own_first, own_last, between, outer)):
        zends_ref[i] = value


def chain_message(ends_ref, source_first, source_last, message_ref):
    own_first, own_last, between, outer = (ends_ref[i] for i in range(2, 6))
    inverse = 1.0 / (own_first + between + outer)
    message_ref[0] = outer * between * inverse
    message_ref[1] = outer * own_first * inverse
    message_ref[2] = outer * inverse * source_first
    message_ref[3] = own_last + between * own_first * inverse
    message_ref[4] = source_last + between * inverse * source_first


def chain_ends(name, messages, ends_ref, source_first, blocks_ref, state_ref):
    count, index = lax.axis_size(name), lax.axis_index(name)
    for mask, message in enumerate(messages):
        blocks_ref[index ^ mask] = message[...]
    blocks = [tuple(blocks_ref[k, i] for i in range(5)) for k in range(count)]
    below, last = chain(blocks, count, index, state_ref)
    own_first, between, outer = ends_ref[2], ends_ref[4], ends_ref[5]
    first = (source_first + outer * below + between * last) / (own_first + between + outer)
    return first, last


def y_source_kernel(
    count_x, count_y, heat_ref, part_ref, low_ref, high_ref, yl_ref, yr_ref, yinv_ref, yends_ref,
    *refs
):
    messages, (ypart_ref, ysource_ref, message_ref, blocks_ref, rows_ref, state_ref, d_ref) = (
        refs[:count_x], refs[count_x:]
    )
    nz, ny, nx = heat_ref.shape
    index = lax.axis_index("gx") // 2
    for mask, message in enumerate(messages):
        blocks_ref[index ^ mask] = message[...]
    first, last, own_first, own_last, between, c_first, c_last = (
        blocks_ref[:, i, :] for i in range(7)
    )
    before = jnp.concatenate([jnp.zeros_like(c_last[:1]), c_last[:-1]], 0)
    outer = link_of(FLAT_SCALE, c_first, before)
    inverse = 1.0 / (own_first + between + outer)
    rows = (
        outer * between * inverse,
        outer * own_first * inverse,
        outer * inverse * first,
        own_last + between * own_first * inverse,
        last + between * inverse * first,
        first * inverse,
        outer * inverse,
        between * inverse,
    )
    for i, value in enumerate(rows):
        rows_ref[i] = value
    whole = lambda i, k: jnp.broadcast_to(rows_ref[i, pl.ds(k, 1), :], (8, rows_ref.shape[2]))
    blocks = [tuple(whole(i, k) for i in range(5)) for k in range(count_x)]
    below, last = chain(blocks, count_x, index, state_ref)
    first = whole(5, index) + whole(6, index) * below + whole(7, index) * last
    lines = part_ref[...] + low_ref[...] * first[:1] + high_ref[...] * last[:1]
    source = lines.T.reshape(nz, ny, nx) - 2.0 * heat_ref[...]
    d_ref[...] = source
    part = reduce_source(source, 1, yl_ref, yr_ref, yinv_ref[...])
    ypart_ref[...] = part
    source_first = d_ref[:, 0, :] + yends_ref[0] * ypart_ref[:, 1, :]
    source_last = d_ref[:, ny - 1, :] + yends_ref[1] * ypart_ref[:, ny - 2, :]
    ysource_ref[0], ysource_ref[1] = source_first, source_last
    if count_y > 2:
        chain_message(yends_ref, source_first, source_last, message_ref)
        return
    odd = lax.axis_index("gy") % 2 == 1
    near_own = jnp.where(odd, yends_ref[2], yends_ref[3])
    far_own = jnp.where(odd, yends_ref[3], yends_ref[2])
    share = yends_ref[4] / (far_own + yends_ref[4])
    message_ref[0] = near_own + share * far_own
    message_ref[1] = jnp.where(odd, source_first, source_last) + share * jnp.where(
        odd, source_last, source_first
    )


def z_source_kernel(
    count_y, ypart_ref, ylow_ref, yhigh_ref, yends_ref, ysource_ref, zl_ref, zr_ref, zinv_ref,
    zends_ref, *refs
):
    messages, (zpart_ref, zsource_ref, message_ref, ends_ref, blocks_ref, state_ref) = (
        refs[:count_y], refs[count_y:]
    )
    nz, ny, nx = ypart_ref.shape
    if count_y > 2:
        first, last = chain_ends("gy", messages, yends_ref, ysource_ref[0], blocks_ref, state_ref)
    else:
        odd = lax.axis_index("gy") % 2 == 1
        mine, other = messages
        outer = jnp.where(odd, yends_ref[5], yends_ref[6])
        between = yends_ref[4]
        factor = outer / (other[0] + outer)
        near = (mine[1] + factor * other[1]) / (mine[0] + factor * other[0])
        far_own = jnp.where(odd, yends_ref[3], yends_ref[2])
        far_source = jnp.where(odd, ysource_ref[1], ysource_ref[0])
        far = (far_source + between * near) / (far_own + between)
        first, last = jnp.where(odd, near, far), jnp.where(odd, far, near)
    ends_ref[0], ends_ref[1] = first, last
    source = jnp.stack(
        [
            ypart_ref[k]
            + ylow_ref[k] * ends_ref[0, pl.ds(k, 1), :]
            + yhigh_ref[k] * ends_ref[1, pl.ds(k, 1), :]
            for k in range(nz)
        ],
        0,
    )
    part = reduce_source(source, 0, zl_ref, zr_ref, zinv_ref[...])
    zpart_ref[...] = part
    source_first = source[0] + zends_ref[0] * part[1]
    source_last = source[nz - 1] + zends_ref[1] * part[nz - 2]
    zsource_ref[...] = source_first
    chain_message(zends_ref, source_first, source_last, message_ref)


def finish_kernel(
    count_z, heat_ref, zpart_ref, zlow_ref, zhigh_ref, zends_ref, zsource_ref, *refs
):
    messages = refs[:count_z][::-1]
    theirs_ref, mine_ref, blocks_ref, state_ref = refs[count_z:]
    first, last = chain_ends("gz", messages, zends_ref, zsource_ref[...], blocks_ref, state_ref)
    nx = theirs_ref.shape[-1]
    heated = heat_ref[...] + zpart_ref[...] + zlow_ref[...] * first + zhigh_ref[...] * last
    theirs_ref[...], mine_ref[...] = heated[:, :, :nx], heated[:, :, nx:]


VMEM = pl.BlockSpec(memory_space=pltpu.VMEM)
HBM = pl.BlockSpec(memory_space=pltpu.HBM)


def call(kernel, outs, operands, scratch=(), specs=None, ops=200_000, vmem=32):
    return pl.pallas_call(
        kernel,
        out_shape=[jax.ShapeDtypeStruct(out, F32) if isinstance(out, tuple) else out for out in outs],
        in_specs=specs or [VMEM] * len(operands),
        out_specs=[VMEM] * len(outs),
        scratch_shapes=[pltpu.VMEM(item, F32) if isinstance(item, tuple) else item for item in scratch],
        compiler_params=pltpu.CompilerParams(vmem_limit_bytes=vmem * 1024 * 1024),
        cost_estimate=pl.CostEstimate(flops=ops, bytes_accessed=ops, transcendentals=0),
    )(*operands)


def neighbour_swaps(name, other, faces):
    count, width = lax.axis_size(name), lax.axis_size(other)
    received = [lax.ppermute(faces[0], name, [(i, i ^ 1) for i in range(count)])]
    if count > 2:
        pairs = []
        for j in range(width):
            for i in range(count):
                at = (j ^ 1, i) if i in (0, count - 1) else (j, ((i + 1) ^ 1) - 1)
                pairs.append(((j, i), at))
        if (other, name) == ("gy", "gz"):
            axes, place = (other, name), lambda at: at[0] * count + at[1]
        else:
            axes, place = (name, other), lambda at: at[1] * width + at[0]
        pairs = [(place(source), place(target)) for source, target in pairs]
        received.append(lax.ppermute(faces[1], axes, pairs))
    return received


def swap_all(name, message, stride=1):
    count = lax.axis_size(name)
    return [message] + [
        lax.ppermute(message, name, [(i, i ^ mask) for i in range(count)])
        for mask in range(stride, count, stride)
    ]


def other_core(values):
    count = lax.axis_size("gx")
    return lax.ppermute(values, "gx", [(i, i ^ 1) for i in range(count)])


def chip_step(heat_a, label_a, edge_a, heat_b, conduct_b, edge_b, table):
    nz, ny, half = heat_a.shape
    nx = 2 * half
    block, lines, layer, rows = (nz, ny, nx), (nx, nz * ny), (ny, nx), (nz, nx)
    count_x, count_y, count_z = (lax.axis_size(name) for name in ("gx", "gy", "gz"))
    count_x = count_x // 2
    x_steps, y_steps, z_steps = (len(steps_of(length)) for length in (nx, ny, nz))

    halo_counts = swaps_along("gz"), swaps_along("gy")
    heat, conduct, edge, *faces = call(
        start_kernel,
        [block, block, layer] + [(2, *layer)] * halo_counts[0] + [(2, *rows)] * halo_counts[1],
        [heat_a, label_a, edge_a, heat_b, conduct_b, edge_b, table],
    )
    z_halo = neighbour_swaps("gz", "gy", faces[: halo_counts[0]])
    y_halo = neighbour_swaps("gy", "gz", faces[halo_counts[0] :])

    x_left, x_right, x_low, x_high, x_inverse, x_ends, source = call(
        x_bands_kernel,
        [(x_steps, *lines)] * 2 + [lines] * 3 + [(8, lines[1]), block],
        [heat, conduct],
    )
    x_part, x_message = call(
        functools.partial(x_source_kernel, halo_counts),
        [lines, (8, lines[1])],
        [heat, conduct, edge, source, x_left, x_right, x_inverse, x_ends, *join_halos(z_halo, y_halo)],
        [block],
    )
    x_messages = swap_all("gx", x_message, 2)
    (
        y_left, y_right, y_low, y_high, y_inverse, y_ends,
        z_left, z_right, z_low, z_high, z_inverse, z_ends,
    ) = call(
        functools.partial(yz_bands_kernel, halo_counts),
        [(y_steps, *block)] * 2 + [block] * 3 + [(7, *rows)]
        + [(z_steps, *block)] * 2 + [block] * 3 + [(6, *layer)],
        [conduct, edge, *join_halos(z_halo, y_halo)],
    )
    y_rows = 5 if count_y > 2 else 2
    y_part, y_source, y_message = call(
        functools.partial(y_source_kernel, count_x, count_y),
        [block, (2, *rows), (y_rows, *rows)],
        [heat, x_part, x_low, x_high, y_left, y_right, y_inverse, y_ends, *x_messages],
        [(count_x, 8, lines[1]), (8, count_x, lines[1]), (5, count_x, 8, lines[1]), block],
    )
    y_messages = swap_all("gy", y_message)
    z_part, z_source, z_message = call(
        functools.partial(z_source_kernel, count_y),
        [block, layer, (5, *layer)],
        [y_part, y_low, y_high, y_ends, y_source, z_left, z_right, z_inverse, z_ends, *y_messages],
        [(2, *rows), (count_y, y_rows, *rows), (5, count_y, *rows)],
    )
    z_messages = swap_all("gz", z_message)
    return call(
        functools.partial(finish_kernel, count_z),
        [heat_a.shape] * 2,
        [heat, z_part, z_low, z_high, z_ends, z_source, *z_messages[::-1]],
        [(count_z, 5, *layer), (5, count_z, *layer)],
    )


def local(heat, label, table, edge):
    others = [other_core(values) for values in (label, heat, edge)]
    entries = table.shape[0]
    own_heat, own_conduct, rows, own_edge = call(
        stage_kernel,
        [heat.shape, heat.shape, (entries, 8, heat.shape[-1]),
         jax.ShapeDtypeStruct(edge.shape, edge.dtype)],
        [heat, label, table, edge],
        [pltpu.VMEM(label.shape, label.dtype), pltpu.SMEM(table.shape, F32),
         pltpu.SemaphoreType.DMA((4,))],
        [HBM] * 4,
        vmem=60,
    )
    label_a, heat_a, edge_a = others
    second = lax.axis_index("gx") % 2 == 1
    theirs, mine = lax.cond(
        second,
        chip_step,
        lambda heat_a, label_a, edge_a, heat_b, *rest: (heat_a, heat_b),
        heat_a, label_a, edge_a, own_heat, own_conduct, own_edge, rows,
    )
    return jnp.where(second, mine, other_core(theirs))


def solution(mesh):
    return jax.shard_map(
        local,
        mesh=mesh,
        in_specs=(P("gz", "gy", "gx"), P("gz", "gy", "gx"), P(), P("gy", "gx")),
        out_specs=P("gz", "gy", "gx"),
        check_vma=False,
    )
```

```python
import functools

import jax
import jax.numpy as jnp
from jax import lax
from jax.experimental import pallas as pl
from jax.experimental.pallas import tpu as pltpu
from jax.sharding import PartitionSpec as P

FLAT_SCALE = 1000.0
UPWARD_SCALE = 200.0
F32 = jnp.float32


def link_of(scale, one, other):
    return scale * one * other / (one + other)


def roll(values, offset, axis):
    if axis == 0 and values.ndim == 3:
        offset = offset % values.shape[0]
        return jnp.concatenate([values[-offset:], values[:-offset]], 0)
    return pltpu.roll(values, offset % values.shape[axis], axis)


def steps_of(length):
    steps, distance = [], 1
    while distance < length - 1:
        steps.append(distance)
        distance *= 2
    return steps


def reduce_interior(link, axis, left_ref, right_ref):
    length = link.shape[axis]
    row = lax.broadcasted_iota(jnp.int32, link.shape, axis)
    low, high, own = link, roll(link, -1, axis), jnp.ones_like(link)
    high = jnp.where(row == length - 1, 0.0, high)
    for step, distance in enumerate(steps_of(length)):
        inverse = 1.0 / (own + low + high)
        open_low, open_high = row > distance, row < length - 1 - distance
        left = jnp.where(open_low, low * roll(inverse, distance, axis), 0.0)
        right = jnp.where(open_high, high * roll(inverse, -distance, axis), 0.0)
        left_ref[step], right_ref[step] = left, right
        own = own + left * roll(own, distance, axis) + right * roll(own, -distance, axis)
        low = jnp.where(open_low, left * roll(low, distance, axis), low)
        high = jnp.where(open_high, right * roll(high, -distance, axis), high)
    inverse = 1.0 / (own + low + high)
    inner = (row > 0) & (row < length - 1)
    share_low = jnp.where(inner, low * inverse, jnp.where(row == 0, 1.0, 0.0))
    share_high = jnp.where(inner, high * inverse, jnp.where(row == 0, 0.0, 1.0))
    return share_low, share_high, jnp.where(inner, inverse, 0.0), own * inverse


def reduce_source(source, axis, left_ref, right_ref, inverse):
    length = source.shape[axis]
    for step, distance in enumerate(steps_of(length)):
        source = (
            source
            + left_ref[step] * roll(source, distance, axis)
            + right_ref[step] * roll(source, -distance, axis)
        )
    return source * inverse


def chain(blocks, count, index, state):
    own = [blocks[k][3] + (blocks[k + 1][1] if k + 1 < count else 0.0) for k in range(count)]
    source = [blocks[k][4] + (blocks[k + 1][2] if k + 1 < count else 0.0) for k in range(count)]
    shape = own[0].shape
    state[0, 0], state[1, 0] = jnp.ones(shape, F32), jnp.zeros(shape, F32)
    up_own, up_source = own[0], source[0]
    for k in range(1, count):
        state[0, k], state[1, k] = up_own, up_source
        factor = blocks[k][0] / (up_own + blocks[k][0])
        up_own, up_source = own[k] + factor * up_own, source[k] + factor * up_source
    down_own, down_source = own[count - 1], source[count - 1]
    state[2, count - 1], state[3, count - 1] = down_own, down_source
    for k in range(count - 2, -1, -1):
        factor = blocks[k + 1][0] / (down_own + blocks[k + 1][0])
        down_own, down_source = own[k] + factor * down_own, source[k] + factor * down_source
        state[2, k], state[3, k] = down_own, down_source
    for k in range(count):
        state[4, k] = blocks[k][0]
    up_own, up_source, down_own, down_source, link = (state[i, index] for i in range(5))
    inverse = 1.0 / (up_own * down_own + link * (up_own + down_own))
    below = ((down_own + link) * up_source + link * down_source) * inverse
    here = ((up_own + link) * down_source + link * up_source) * inverse
    return below, here


def pick_halo(name, received, odd):
    first = received[0][...]
    second = received[1][...] if len(received) > 1 else jnp.zeros_like(first)
    index, count = lax.axis_index(name), lax.axis_size(name)
    below = jnp.where(odd, first, second)
    above = jnp.where(odd, second, first)
    return jnp.where(index > 0, below, 0.0), jnp.where(index < count - 1, above, 0.0)


def swaps_along(name):
    return min(lax.axis_size(name) - 1, 2)


def look_up(label, table_ref):
    conduct = jnp.broadcast_to(table_ref[0], label.shape)
    for entry in range(1, table_ref.shape[0]):
        conduct = jnp.where(label == entry, table_ref[entry], conduct)
    return conduct


def stage_kernel(
    heat_in, label_in, table_in, edge_in, heat_ref, conduct_ref, table_ref, edge_ref, label_ref,
    entries_ref, sems
):
    copies = [
        pltpu.make_async_copy(source, target, sems.at[i])
        for i, (source, target) in enumerate(
            (
                (table_in, entries_ref), (label_in, label_ref), (heat_in, heat_ref),
                (edge_in, edge_ref),
            )
        )
    ]
    for copy in copies:
        copy.start()
    copies[0].wait()
    for entry in range(table_ref.shape[0]):
        table_ref[entry] = jnp.full(table_ref.shape[1:], entries_ref[entry], F32)
    copies[1].wait()
    conduct_ref[...] = look_up(label_ref[...], table_ref)
    copies[2].wait()
    copies[3].wait()


def join_halos(z_halo, y_halo):
    return [*z_halo[1:], z_halo[0], *y_halo]


def split_halos(counts, refs):
    halos = refs[: sum(counts)]
    return [halos[counts[0] - 1], *halos[: counts[0] - 1]], halos[counts[0] :]


def start_kernel(
    heat_a_ref, label_a_ref, edge_a_ref, heat_b_ref, conduct_b_ref, edge_b_ref, table_ref,
    heat_ref, conduct_ref, edge_ref, *faces
):
    nx = heat_a_ref.shape[-1]
    heat_ref[:, :, :nx], heat_ref[:, :, nx:] = heat_a_ref[...], heat_b_ref[...]
    conduct_ref[:, :, :nx] = look_up(label_a_ref[...], table_ref)
    conduct_ref[:, :, nx:] = conduct_b_ref[...]
    edge_ref[:, :nx] = edge_a_ref[...].astype(F32)
    edge_ref[:, nx:] = edge_b_ref[...].astype(F32)
    z_faces, y_faces = faces[: swaps_along("gz")], faces[swaps_along("gz") :]
    odd_z = lax.axis_index("gz") % 2 == 1
    odd_y = lax.axis_index("gy") % 2 == 1
    for i, ref in enumerate((heat_ref, conduct_ref)):
        low, high = ref[0], ref[ref.shape[0] - 1]
        for face_ref, pick in zip(z_faces, (odd_z, ~odd_z)):
            face_ref[i] = jnp.where(pick, low, high)
        low, high = ref[:, 0, :], ref[:, ref.shape[1] - 1, :]
        for face_ref, pick in zip(y_faces, (odd_y, ~odd_y)):
            face_ref[i] = jnp.where(pick, low, high)


def x_bands_kernel(
    heat_ref, conduct_ref, left_ref, right_ref, low_ref, high_ref, inverse_ref, ends_ref, local_ref,
    low_block_ref, high_block_ref
):
    nz, ny, nx = conduct_ref.shape
    conduct = conduct_ref[...]
    heat = heat_ref[...]
    local = 2.0 * heat
    across = 2.0 * link_of(UPWARD_SCALE, conduct[1:], conduct[:-1]) * (heat[1:] - heat[:-1])
    nothing = jnp.zeros_like(heat[:1])
    local = local + jnp.concatenate([across, nothing], 0) - jnp.concatenate([nothing, across], 0)
    row = lax.broadcasted_iota(jnp.int32, conduct.shape, 1)
    across = 2.0 * link_of(FLAT_SCALE, conduct, roll(conduct, 1, 1)) * (heat - roll(heat, 1, 1))
    across = jnp.where(row > 0, across, 0.0)
    local = local - across + roll(across, -1, 1)
    local_ref[...] = local
    lines = conduct.reshape(nz * ny, nx).T
    row = lax.broadcasted_iota(jnp.int32, lines.shape, 0)
    link = jnp.where(row > 0, link_of(FLAT_SCALE, lines, roll(lines, 1, 0)), 0.0)
    low, high, inverse, own = reduce_interior(link, 0, left_ref, right_ref)
    low_ref[...], high_ref[...], inverse_ref[...] = low, high, inverse
    low_block_ref[...] = low.T.reshape(nz, ny, nx)
    high_block_ref[...] = high.T.reshape(nz, ny, nx)
    local = local.reshape(nz * ny, nx).T
    first, last = link[1:2], link[nx - 1 :]
    ends_ref[...] = jnp.concatenate(
        [
            jnp.sum(low * local, 0, keepdims=True),
            jnp.sum(high * local, 0, keepdims=True),
            1.0 + first * own[1:2],
            1.0 + last * own[nx - 2 : nx - 1],
            first * high[1:2],
            lines[:1],
            lines[nx - 1 :],
            jnp.zeros_like(first),
        ],
        0,
    )


def x_message_kernel(
    halo_counts, heat_ref, conduct_ref, edge_ref, low_ref, high_ref, ends_ref, *refs
):
    z_halo, y_halo = split_halos(halo_counts, refs)
    message_ref, z_flow_ref, y_flow_ref = refs[sum(halo_counts) :]
    nz, ny, nx = conduct_ref.shape
    lanes = nz * ny
    index_z, index_y = lax.axis_index("gz"), lax.axis_index("gy")
    below, above = pick_halo("gz", z_halo, index_z % 2 == 1)
    ground = jnp.where(index_z == 0, UPWARD_SCALE * conduct_ref[0] * edge_ref[...], 0.0)
    flow = link_of(UPWARD_SCALE, conduct_ref[0], below[1]) * (below[0] - heat_ref[0])
    z_flow_ref[0] = 2.0 * (flow - ground * heat_ref[0])
    flow = link_of(UPWARD_SCALE, conduct_ref[nz - 1], above[1]) * (above[0] - heat_ref[nz - 1])
    z_flow_ref[1] = 2.0 * flow
    below, above = pick_halo("gy", y_halo, index_y % 2 == 1)
    flow = link_of(FLAT_SCALE, conduct_ref[:, 0, :], below[1]) * (below[0] - heat_ref[:, 0, :])
    y_flow_ref[0] = 2.0 * flow
    flow = link_of(FLAT_SCALE, conduct_ref[:, ny - 1, :], above[1])
    y_flow_ref[1] = 2.0 * flow * (above[0] - heat_ref[:, ny - 1, :])

    def spread(values, first, step):
        shape = (values.shape[0], lanes)
        row = lax.broadcasted_iota(jnp.int32, shape, 0)
        lane = lax.broadcasted_iota(jnp.int32, shape, 1)
        return jnp.where(lane == first + step * row, jnp.sum(values, 1, keepdims=True), 0.0)

    sums = []
    for share in (low_ref, high_ref):
        layers = spread(share[0] * z_flow_ref[0], 0, 1)
        layers = layers + spread(share[nz - 1] * z_flow_ref[1], lanes - ny, 1)
        rows = spread(share[:, 0, :] * y_flow_ref[0], 0, ny)
        rows = rows + spread(share[:, ny - 1, :] * y_flow_ref[1], ny - 1, ny)
        sums.append(jnp.sum(layers, 0, keepdims=True) + jnp.sum(rows, 0, keepdims=True))
    ends = ends_ref[...]
    message_ref[...] = jnp.concatenate([ends[0:1] + sums[0], ends[1:2] + sums[1], ends[2:8]], 0)


def x_source_kernel(
    local_ref, z_flow_ref, y_flow_ref, left_ref, right_ref, inverse_ref, part_ref, source_ref
):
    nz, ny, nx = local_ref.shape
    source_ref[...] = local_ref[...]
    source_ref[0] += z_flow_ref[0]
    source_ref[nz - 1] += z_flow_ref[1]
    source_ref[:, 0, :] += y_flow_ref[0]
    source_ref[:, ny - 1, :] += y_flow_ref[1]
    source = source_ref[...].reshape(nz * ny, nx).T
    part_ref[...] = reduce_source(source, 0, left_ref, right_ref, inverse_ref[...])


def end_bands(link, first, last, axis, high, own):
    length = high.shape[axis]
    at = lambda values, i: lax.index_in_dim(values, i, axis, keepdims=False)
    return (
        1.0 + first * at(own, 1),
        1.0 + last * at(own, length - 2),
        first * at(high, 1),
    )


def yz_bands_kernel(
    halo_counts, conduct_ref, edge_ref, *refs
):
    z_halo, y_halo = split_halos(halo_counts, refs)
    (
        yl_ref, yr_ref, ylow_ref, yhigh_ref, yinv_ref, yends_ref, *y_two_refs,
        zl_ref, zr_ref, zlow_ref, zhigh_ref, zinv_ref, zends_ref,
    ) = refs[sum(halo_counts) :]
    nz, ny, nx = conduct_ref.shape
    index_z, index_y = lax.axis_index("gz"), lax.axis_index("gy")
    conduct = conduct_ref[...]
    row = lax.broadcasted_iota(jnp.int32, conduct.shape, 1)
    link = jnp.where(row > 0, link_of(FLAT_SCALE, conduct, roll(conduct, 1, 1)), 0.0)
    low, high, inverse, own = reduce_interior(link, 1, yl_ref, yr_ref)
    ylow_ref[...], yhigh_ref[...], yinv_ref[...] = low, high, inverse
    below, above = pick_halo("gy", y_halo, index_y % 2 == 1)
    first = link_of(FLAT_SCALE, conduct_ref[:, 0, :], conduct_ref[:, 1, :])
    last = link_of(FLAT_SCALE, conduct_ref[:, ny - 1, :], conduct_ref[:, ny - 2, :])
    own_first, own_last, between = end_bands(link, first, last, 1, high, own)
    outer_low = link_of(FLAT_SCALE, conduct_ref[:, 0, :], below[1])
    outer_high = link_of(FLAT_SCALE, conduct_ref[:, ny - 1, :], above[1])
    for i, value in enumerate((first, last, own_first, own_last, between, outer_low, outer_high)):
        yends_ref[i] = value
    if y_two_refs:
        ysum_ref, yshare_ref = y_two_refs
        odd = index_y % 2 == 1
        near_own, far_own = jnp.where(odd, own_first, own_last), jnp.where(odd, own_last, own_first)
        share = between / (far_own + between)
        ysum_ref[0] = near_own + share * far_own
        ysum_ref[1] = share
        for k in range(nz):
            near, far = jnp.where(odd, low[k], high[k]), jnp.where(odd, high[k], low[k])
            yshare_ref[k] = near + ysum_ref[1, pl.ds(k, 1), :] * far
    link = link_of(UPWARD_SCALE, conduct[1:], conduct[:-1])
    link = jnp.concatenate([jnp.zeros_like(conduct[:1]), link], 0)
    low, high, inverse, own = reduce_interior(link, 0, zl_ref, zr_ref)
    zlow_ref[...], zhigh_ref[...], zinv_ref[...] = low, high, inverse
    below, above = pick_halo("gz", z_halo, index_z % 2 == 1)
    own_first, own_last, between = end_bands(link, link[1], link[nz - 1], 0, high, own)
    ground = UPWARD_SCALE * conduct[0] * edge_ref[...]
    own_first = own_first + jnp.where(index_z == 0, ground, 0.0)
    outer = link_of(UPWARD_SCALE, conduct[0], below[1])
    for i, value in enumerate((link[1], link[nz - 1], own_first, own_last, between, outer)):
        zends_ref[i] = value


def chain_message(ends_ref, source_first, source_last, message_ref):
    own_first, own_last, between, outer = (ends_ref[i] for i in range(2, 6))
    inverse = 1.0 / (own_first + between + outer)
    message_ref[0] = outer * between * inverse
    message_ref[1] = outer * own_first * inverse
    message_ref[2] = outer * inverse * source_first
    message_ref[3] = own_last + between * own_first * inverse
    message_ref[4] = source_last + between * inverse * source_first


def chain_ends(name, messages, ends_ref, source_first, blocks_ref, state_ref):
    count, index = lax.axis_size(name), lax.axis_index(name)
    for shift, message in enumerate(messages):
        blocks_ref[lax.rem(index - shift + count, count)] = message[...]
    blocks = [tuple(blocks_ref[k, i] for i in range(5)) for k in range(count)]
    below, last = chain(blocks, count, index, state_ref)
    own_first, between, outer = ends_ref[2], ends_ref[4], ends_ref[5]
    first = (source_first + outer * below + between * last) / (own_first + between + outer)
    return first, last


def y_message_kernel(
    count_x, count_y, heat_ref, part_ref, low_ref, high_ref, yends_ref, *refs
):
    messages, refs = refs[:count_x], refs[count_x:]
    shares, refs = (refs[:2], refs[2:]) if count_y > 2 else (refs[:1], refs[1:])
    sums_ref, refs = (None, refs) if count_y > 2 else (refs[0], refs[1:])
    source_ref, message_ref, blocks_ref, rows_ref, state_ref = refs
    nz, ny, nx = heat_ref.shape
    index = lax.axis_index("gx") // 2
    for shift, message in enumerate(messages):
        blocks_ref[lax.rem(index - shift + count_x, count_x)] = message[...]
    first, last, own_first, own_last, between, c_first, c_last = (
        blocks_ref[:, i, :] for i in range(7)
    )
    before = jnp.concatenate([jnp.zeros_like(c_last[:1]), c_last[:-1]], 0)
    outer = link_of(FLAT_SCALE, c_first, before)
    inverse = 1.0 / (own_first + between + outer)
    rows = (
        outer * between * inverse,
        outer * own_first * inverse,
        outer * inverse * first,
        own_last + between * own_first * inverse,
        last + between * inverse * first,
        first * inverse,
        outer * inverse,
        between * inverse,
    )
    for i, value in enumerate(rows):
        rows_ref[i] = value
    whole = lambda i, k: jnp.broadcast_to(rows_ref[i, pl.ds(k, 1), :], (8, rows_ref.shape[2]))
    blocks = [tuple(whole(i, k) for i in range(5)) for k in range(count_x)]
    below, last = chain(blocks, count_x, index, state_ref)
    first = whole(5, index) + whole(6, index) * below + whole(7, index) * last
    lines = part_ref[...] + low_ref[...] * first[:1] + high_ref[...] * last[:1]
    source = lines.T.reshape(nz, ny, nx) - 2.0 * heat_ref[...]
    source_ref[...] = source
    sums = [jnp.sum(share[...] * source, 1) for share in shares]
    if count_y > 2:
        chain_message(yends_ref, *sums, message_ref)
    else:
        message_ref[0], message_ref[1] = sums_ref[0], sums[0]


def y_source_kernel(
    source_ref, yl_ref, yr_ref, yinv_ref, yends_ref, ypart_ref, ysource_ref
):
    ny = source_ref.shape[1]
    part = reduce_source(source_ref[...], 1, yl_ref, yr_ref, yinv_ref[...])
    ypart_ref[...] = part
    ysource_ref[0] = source_ref[:, 0, :] + yends_ref[0] * ypart_ref[:, 1, :]
    ysource_ref[1] = source_ref[:, ny - 1, :] + yends_ref[1] * ypart_ref[:, ny - 2, :]


def z_message_kernel(
    count_y, ypart_ref, ylow_ref, yhigh_ref, yends_ref, ysource_ref, zlow_ref, zhigh_ref,
    zends_ref, *refs
):
    messages, refs = refs[:count_y], refs[count_y:]
    source_ref, zsource_ref, message_ref, ends_ref, *state = refs
    nz, ny, nx = ypart_ref.shape
    if count_y > 2:
        first, last = chain_ends("gy", messages, yends_ref, ysource_ref[0], *state)
    else:
        odd = lax.axis_index("gy") % 2 == 1
        mine, other = messages
        outer = jnp.where(odd, yends_ref[5], yends_ref[6])
        between = yends_ref[4]
        factor = outer / (other[0] + outer)
        near = (mine[1] + factor * other[1]) / (mine[0] + factor * other[0])
        far_own = jnp.where(odd, yends_ref[3], yends_ref[2])
        far_source = jnp.where(odd, ysource_ref[1], ysource_ref[0])
        far = (far_source + between * near) / (far_own + between)
        first, last = jnp.where(odd, near, far), jnp.where(odd, far, near)
    ends_ref[0], ends_ref[1] = first, last
    source_first, source_last = jnp.zeros((ny, nx), F32), jnp.zeros((ny, nx), F32)
    for k in range(nz):
        source = (
            ypart_ref[k]
            + ylow_ref[k] * ends_ref[0, pl.ds(k, 1), :]
            + yhigh_ref[k] * ends_ref[1, pl.ds(k, 1), :]
        )
        source_ref[k] = source
        source_first = source_first + zlow_ref[k] * source
        source_last = source_last + zhigh_ref[k] * source
    zsource_ref[...] = source_first
    chain_message(zends_ref, source_first, source_last, message_ref)


def z_source_kernel(source_ref, zl_ref, zr_ref, zinv_ref, zpart_ref):
    zpart_ref[...] = reduce_source(source_ref[...], 0, zl_ref, zr_ref, zinv_ref[...])


def finish_kernel(
    count_z, heat_ref, zpart_ref, zlow_ref, zhigh_ref, zends_ref, zsource_ref, *refs
):
    messages, (theirs_ref, mine_ref, blocks_ref, state_ref) = refs[:count_z], refs[count_z:]
    first, last = chain_ends("gz", messages, zends_ref, zsource_ref[...], blocks_ref, state_ref)
    nx = theirs_ref.shape[-1]
    heated = heat_ref[...] + zpart_ref[...] + zlow_ref[...] * first + zhigh_ref[...] * last
    theirs_ref[...], mine_ref[...] = heated[:, :, :nx], heated[:, :, nx:]


VMEM = pl.BlockSpec(memory_space=pltpu.VMEM)
HBM = pl.BlockSpec(memory_space=pltpu.HBM)


def call(kernel, outs, operands, scratch=(), specs=None, ops=200_000, vmem=32):
    return pl.pallas_call(
        kernel,
        out_shape=[jax.ShapeDtypeStruct(out, F32) if isinstance(out, tuple) else out for out in outs],
        in_specs=specs or [VMEM] * len(operands),
        out_specs=[VMEM] * len(outs),
        scratch_shapes=[pltpu.VMEM(item, F32) if isinstance(item, tuple) else item for item in scratch],
        compiler_params=pltpu.CompilerParams(vmem_limit_bytes=vmem * 1024 * 1024),
        cost_estimate=pl.CostEstimate(flops=ops, bytes_accessed=ops, transcendentals=0),
    )(*operands)


def neighbour_swaps(name, other, faces):
    count, width = lax.axis_size(name), lax.axis_size(other)
    received = [lax.ppermute(faces[0], name, [(i, i ^ 1) for i in range(count)])]
    if count > 2:
        pairs = []
        for j in range(width):
            for i in range(count):
                at = (j ^ 1, i) if i in (0, count - 1) else (j, ((i + 1) ^ 1) - 1)
                pairs.append(((j, i), at))
        if (other, name) == ("gy", "gz"):
            axes, place = (other, name), lambda at: at[0] * count + at[1]
        else:
            axes, place = (name, other), lambda at: at[1] * width + at[0]
        pairs = [(place(source), place(target)) for source, target in pairs]
        received.append(lax.ppermute(faces[1], axes, pairs))
    return received


def swap_all(name, message, stride=1):
    count = lax.axis_size(name)
    return [message] + [
        lax.ppermute(message, name, [(i, (i + shift) % count) for i in range(count)])
        for shift in range(stride, count, stride)
    ]


def other_core(values):
    count = lax.axis_size("gx")
    return lax.ppermute(values, "gx", [(i, i ^ 1) for i in range(count)])


def chip_step(heat_a, label_a, edge_a, heat_b, conduct_b, edge_b, table):
    nz, ny, half = heat_a.shape
    nx = 2 * half
    block, lines, layer, rows = (nz, ny, nx), (nx, nz * ny), (ny, nx), (nz, nx)
    count_x, count_y, count_z = (lax.axis_size(name) for name in ("gx", "gy", "gz"))
    count_x = count_x // 2
    x_steps, y_steps, z_steps = (len(steps_of(length)) for length in (nx, ny, nz))

    halo_counts = swaps_along("gz"), swaps_along("gy")
    heat, conduct, edge, *faces = call(
        start_kernel,
        [block, block, layer] + [(2, *layer)] * halo_counts[0] + [(2, *rows)] * halo_counts[1],
        [heat_a, label_a, edge_a, heat_b, conduct_b, edge_b, table],
    )
    z_halo = neighbour_swaps("gz", "gy", faces[: halo_counts[0]])
    y_halo = neighbour_swaps("gy", "gz", faces[halo_counts[0] :])

    x_left, x_right, x_low, x_high, x_inverse, x_ends, x_local, x_low_block, x_high_block = call(
        x_bands_kernel,
        [(x_steps, *lines)] * 2 + [lines] * 3 + [(8, lines[1])] + [block] * 3,
        [heat, conduct],
    )
    x_message, z_flow, y_flow = call(
        functools.partial(x_message_kernel, halo_counts),
        [(8, lines[1]), (2, *layer), (2, *rows)],
        [heat, conduct, edge, x_low_block, x_high_block, x_ends, *join_halos(z_halo, y_halo)],
    )
    x_messages = swap_all("gx", x_message, 2)
    two = count_y == 2
    (
        y_left, y_right, y_low, y_high, y_inverse, y_ends, *y_two,
        z_left, z_right, z_low, z_high, z_inverse, z_ends,
    ) = call(
        functools.partial(yz_bands_kernel, halo_counts),
        [(y_steps, *block)] * 2 + [block] * 3 + [(7, *rows)] + [(2, *rows), block] * two
        + [(z_steps, *block)] * 2 + [block] * 3 + [(6, *layer)],
        [conduct, edge, *join_halos(z_halo, y_halo)],
    )
    y_sum, y_share = y_two[:1], y_two[1:]
    (x_part,) = call(
        x_source_kernel,
        [lines],
        [x_local, z_flow, y_flow, x_left, x_right, x_inverse],
        [block],
    )
    y_rows = 2 if two else 5
    y_source, y_message = call(
        functools.partial(y_message_kernel, count_x, count_y),
        [block, (y_rows, *rows)],
        [heat, x_part, x_low, x_high, y_ends, *x_messages, *(y_share or (y_low, y_high)), *y_sum],
        [(count_x, 8, lines[1]), (8, count_x, lines[1]), (5, count_x, 8, lines[1])],
    )
    y_messages = swap_all("gy", y_message)
    y_part, y_end_sources = call(
        y_source_kernel,
        [block, (2, *rows)],
        [y_source, y_left, y_right, y_inverse, y_ends],
    )
    z_source, z_first, z_message = call(
        functools.partial(z_message_kernel, count_y),
        [block, layer, (5, *layer)],
        [y_part, y_low, y_high, y_ends, y_end_sources, z_low, z_high, z_ends, *y_messages],
        [(2, *rows)] + ([] if two else [(count_y, y_rows, *rows), (5, count_y, *rows)]),
    )
    z_messages = swap_all("gz", z_message)
    (z_part,) = call(z_source_kernel, [block], [z_source, z_left, z_right, z_inverse])
    return call(
        functools.partial(finish_kernel, count_z),
        [heat_a.shape] * 2,
        [heat, z_part, z_low, z_high, z_ends, z_first, *z_messages],
        [(count_z, 5, *layer), (5, count_z, *layer)],
    )


def local(heat, label, table, edge):
    label_a, heat_a, edge_a = (other_core(values) for values in (label, heat, edge))
    entries = table.shape[0]
    own_heat, own_conduct, rows, own_edge = call(
        stage_kernel,
        [heat.shape, heat.shape, (entries, 8, heat.shape[-1]),
         jax.ShapeDtypeStruct(edge.shape, edge.dtype)],
        [heat, label, table, edge],
        [pltpu.VMEM(label.shape, label.dtype), pltpu.SMEM(table.shape, F32),
         pltpu.SemaphoreType.DMA((4,))],
        [HBM] * 4,
        vmem=60,
    )
    second = lax.axis_index("gx") % 2 == 1
    theirs, mine = lax.cond(
        second,
        chip_step,
        lambda heat_a, label_a, edge_a, heat_b, *rest: (heat_a, heat_b),
        heat_a, label_a, edge_a, own_heat, own_conduct, own_edge, rows,
    )
    return jnp.where(second, mine, other_core(theirs))


def solution(mesh):
    return jax.shard_map(
        local,
        mesh=mesh,
        in_specs=(P("gz", "gy", "gx"), P("gz", "gy", "gx"), P(), P("gy", "gx")),
        out_specs=P("gz", "gy", "gx"),
        check_vma=False,
    )
```

```python
import functools

import jax
import jax.numpy as jnp
from jax import lax
from jax.experimental import pallas as pl
from jax.experimental.pallas import tpu as pltpu
from jax.sharding import PartitionSpec as P

FLAT_SCALE = 1000.0
UPWARD_SCALE = 200.0
F32 = jnp.float32


def link_of(scale, one, other):
    return scale * one * other / (one + other)


def roll(values, offset, axis):
    if axis == 0 and values.ndim == 3:
        offset = offset % values.shape[0]
        return jnp.concatenate([values[-offset:], values[:-offset]], 0)
    return pltpu.roll(values, offset % values.shape[axis], axis)


def steps_of(length):
    steps, distance = [], 1
    while distance < length - 1:
        steps.append(distance)
        distance *= 2
    return steps


def reduce_interior(link, axis, left_ref, right_ref):
    length = link.shape[axis]
    row = lax.broadcasted_iota(jnp.int32, link.shape, axis)
    low, high, own = link, roll(link, -1, axis), jnp.ones_like(link)
    high = jnp.where(row == length - 1, 0.0, high)
    for step, distance in enumerate(steps_of(length)):
        inverse = 1.0 / (own + low + high)
        open_low, open_high = row > distance, row < length - 1 - distance
        left = jnp.where(open_low, low * roll(inverse, distance, axis), 0.0)
        right = jnp.where(open_high, high * roll(inverse, -distance, axis), 0.0)
        left_ref[step], right_ref[step] = left, right
        own = own + left * roll(own, distance, axis) + right * roll(own, -distance, axis)
        low = jnp.where(open_low, left * roll(low, distance, axis), low)
        high = jnp.where(open_high, right * roll(high, -distance, axis), high)
    inverse = 1.0 / (own + low + high)
    inner = (row > 0) & (row < length - 1)
    share_low = jnp.where(inner, low * inverse, jnp.where(row == 0, 1.0, 0.0))
    share_high = jnp.where(inner, high * inverse, jnp.where(row == 0, 0.0, 1.0))
    return share_low, share_high, jnp.where(inner, inverse, 0.0), own * inverse


def reduce_source(source, axis, left_ref, right_ref, inverse):
    length = source.shape[axis]
    for step, distance in enumerate(steps_of(length)):
        source = (
            source
            + left_ref[step] * roll(source, distance, axis)
            + right_ref[step] * roll(source, -distance, axis)
        )
    return source * inverse


def chain(blocks, count, index, state):
    own = [blocks[k][3] + (blocks[k + 1][1] if k + 1 < count else 0.0) for k in range(count)]
    source = [blocks[k][4] + (blocks[k + 1][2] if k + 1 < count else 0.0) for k in range(count)]
    shape = own[0].shape
    state[0, 0], state[1, 0] = jnp.ones(shape, F32), jnp.zeros(shape, F32)
    up_own, up_source = own[0], source[0]
    for k in range(1, count):
        state[0, k], state[1, k] = up_own, up_source
        factor = blocks[k][0] / (up_own + blocks[k][0])
        up_own, up_source = own[k] + factor * up_own, source[k] + factor * up_source
    down_own, down_source = own[count - 1], source[count - 1]
    state[2, count - 1], state[3, count - 1] = down_own, down_source
    for k in range(count - 2, -1, -1):
        factor = blocks[k + 1][0] / (down_own + blocks[k + 1][0])
        down_own, down_source = own[k] + factor * down_own, source[k] + factor * down_source
        state[2, k], state[3, k] = down_own, down_source
    for k in range(count):
        state[4, k] = blocks[k][0]
    up_own, up_source, down_own, down_source, link = (state[i, index] for i in range(5))
    inverse = 1.0 / (up_own * down_own + link * (up_own + down_own))
    below = ((down_own + link) * up_source + link * down_source) * inverse
    here = ((up_own + link) * down_source + link * up_source) * inverse
    return below, here


def pick_halo(name, received, odd):
    first = received[0][...]
    second = received[1][...] if len(received) > 1 else jnp.zeros_like(first)
    index, count = lax.axis_index(name), lax.axis_size(name)
    below = jnp.where(odd, first, second)
    above = jnp.where(odd, second, first)
    return jnp.where(index > 0, below, 0.0), jnp.where(index < count - 1, above, 0.0)


def swaps_along(name):
    return min(lax.axis_size(name) - 1, 2)


def look_up(label, table_ref):
    conduct = jnp.broadcast_to(table_ref[0], label.shape)
    for entry in range(1, table_ref.shape[0]):
        conduct = jnp.where(label == entry, table_ref[entry], conduct)
    return conduct


def stage_kernel(
    heat_in, label_in, table_in, edge_in, heat_ref, conduct_ref, table_ref, edge_ref, label_ref,
    entries_ref, sems
):
    copies = [
        pltpu.make_async_copy(source, target, sems.at[i])
        for i, (source, target) in enumerate(
            (
                (table_in, entries_ref), (label_in, label_ref), (heat_in, heat_ref),
                (edge_in, edge_ref),
            )
        )
    ]
    for copy in copies:
        copy.start()
    copies[0].wait()
    for entry in range(table_ref.shape[0]):
        table_ref[entry] = jnp.full(table_ref.shape[1:], entries_ref[entry], F32)
    copies[1].wait()
    conduct_ref[...] = look_up(label_ref[...], table_ref)
    copies[2].wait()
    copies[3].wait()


def join_halos(z_halo, y_halo):
    return [*z_halo[1:], z_halo[0], *y_halo]


def split_halos(counts, refs):
    halos = refs[: sum(counts)]
    return [halos[counts[0] - 1], *halos[: counts[0] - 1]], halos[counts[0] :]


def start_kernel(
    heat_a_ref, label_a_ref, edge_a_ref, heat_b_ref, conduct_b_ref, edge_b_ref, table_ref,
    heat_ref, conduct_ref, edge_ref, *faces
):
    nx = heat_a_ref.shape[-1]
    heat_ref[:, :, :nx], heat_ref[:, :, nx:] = heat_a_ref[...], heat_b_ref[...]
    conduct_ref[:, :, :nx] = look_up(label_a_ref[...], table_ref)
    conduct_ref[:, :, nx:] = conduct_b_ref[...]
    edge_ref[:, :nx] = edge_a_ref[...].astype(F32)
    edge_ref[:, nx:] = edge_b_ref[...].astype(F32)
    z_faces, y_faces = faces[: swaps_along("gz")], faces[swaps_along("gz") :]
    odd_z = lax.axis_index("gz") % 2 == 1
    odd_y = lax.axis_index("gy") % 2 == 1
    for i, ref in enumerate((heat_ref, conduct_ref)):
        low, high = ref[0], ref[ref.shape[0] - 1]
        for face_ref, pick in zip(z_faces, (odd_z, ~odd_z)):
            face_ref[i] = jnp.where(pick, low, high)
        low, high = ref[:, 0, :], ref[:, ref.shape[1] - 1, :]
        for face_ref, pick in zip(y_faces, (odd_y, ~odd_y)):
            face_ref[i] = jnp.where(pick, low, high)


def end_bands(link, first, last, axis, high, own):
    length = high.shape[axis]
    at = lambda values, i: lax.index_in_dim(values, i, axis, keepdims=False)
    return (
        1.0 + first * at(own, 1),
        1.0 + last * at(own, length - 2),
        first * at(high, 1),
    )


def x_bands_kernel(
    heat_ref, conduct_ref, left_ref, right_ref, low_ref, high_ref, inverse_ref, ends_ref, local_ref,
    low_block_ref, high_block_ref, zl_ref, zr_ref, zlow_ref, zhigh_ref, zinv_ref, zinner_ref
):
    nz, ny, nx = conduct_ref.shape
    conduct = conduct_ref[...]
    link = link_of(UPWARD_SCALE, conduct[1:], conduct[:-1])
    link = jnp.concatenate([jnp.zeros_like(conduct[:1]), link], 0)
    low, high, inverse, own = reduce_interior(link, 0, zl_ref, zr_ref)
    zlow_ref[...], zhigh_ref[...], zinv_ref[...] = low, high, inverse
    for i, value in enumerate(end_bands(link, link[1], link[nz - 1], 0, high, own)):
        zinner_ref[i] = value
    heat = heat_ref[...]
    local = 2.0 * heat
    across = 2.0 * link_of(UPWARD_SCALE, conduct[1:], conduct[:-1]) * (heat[1:] - heat[:-1])
    nothing = jnp.zeros_like(heat[:1])
    local = local + jnp.concatenate([across, nothing], 0) - jnp.concatenate([nothing, across], 0)
    row = lax.broadcasted_iota(jnp.int32, conduct.shape, 1)
    across = 2.0 * link_of(FLAT_SCALE, conduct, roll(conduct, 1, 1)) * (heat - roll(heat, 1, 1))
    across = jnp.where(row > 0, across, 0.0)
    local = local - across + roll(across, -1, 1)
    local_ref[...] = local
    lines = conduct.reshape(nz * ny, nx).T
    row = lax.broadcasted_iota(jnp.int32, lines.shape, 0)
    link = jnp.where(row > 0, link_of(FLAT_SCALE, lines, roll(lines, 1, 0)), 0.0)
    low, high, inverse, own = reduce_interior(link, 0, left_ref, right_ref)
    low_ref[...], high_ref[...], inverse_ref[...] = low, high, inverse
    low_block_ref[...] = low.T.reshape(nz, ny, nx)
    high_block_ref[...] = high.T.reshape(nz, ny, nx)
    local = local.reshape(nz * ny, nx).T
    first, last = link[1:2], link[nx - 1 :]
    ends_ref[...] = jnp.concatenate(
        [
            jnp.sum(low * local, 0, keepdims=True),
            jnp.sum(high * local, 0, keepdims=True),
            1.0 + first * own[1:2],
            1.0 + last * own[nx - 2 : nx - 1],
            first * high[1:2],
            lines[:1],
            lines[nx - 1 :],
            jnp.zeros_like(first),
        ],
        0,
    )


def x_message_kernel(
    halo_counts, heat_ref, conduct_ref, edge_ref, low_ref, high_ref, ends_ref, zinner_ref, *refs
):
    z_halo, y_halo = split_halos(halo_counts, refs)
    message_ref, z_flow_ref, y_flow_ref, zends_ref = refs[sum(halo_counts) :]
    nz, ny, nx = conduct_ref.shape
    lanes = nz * ny
    index_z, index_y = lax.axis_index("gz"), lax.axis_index("gy")
    below, above = pick_halo("gz", z_halo, index_z % 2 == 1)
    ground = jnp.where(index_z == 0, UPWARD_SCALE * conduct_ref[0] * edge_ref[...], 0.0)
    outer = link_of(UPWARD_SCALE, conduct_ref[0], below[1])
    z_flow_ref[0] = 2.0 * (outer * (below[0] - heat_ref[0]) - ground * heat_ref[0])
    own_first, own_last, between = zinner_ref[0] + ground, zinner_ref[1], zinner_ref[2]
    inverse = 1.0 / (own_first + between + outer)
    for i, value in enumerate((outer, between, inverse)):
        zends_ref[i] = value
    zends_ref[3] = outer * between * inverse
    zends_ref[4] = outer * own_first * inverse
    zends_ref[5] = own_last + between * own_first * inverse
    flow = link_of(UPWARD_SCALE, conduct_ref[nz - 1], above[1]) * (above[0] - heat_ref[nz - 1])
    z_flow_ref[1] = 2.0 * flow
    below, above = pick_halo("gy", y_halo, index_y % 2 == 1)
    flow = link_of(FLAT_SCALE, conduct_ref[:, 0, :], below[1]) * (below[0] - heat_ref[:, 0, :])
    y_flow_ref[0] = 2.0 * flow
    flow = link_of(FLAT_SCALE, conduct_ref[:, ny - 1, :], above[1])
    y_flow_ref[1] = 2.0 * flow * (above[0] - heat_ref[:, ny - 1, :])

    def spread(values, first, step):
        shape = (values.shape[0], lanes)
        row = lax.broadcasted_iota(jnp.int32, shape, 0)
        lane = lax.broadcasted_iota(jnp.int32, shape, 1)
        return jnp.where(lane == first + step * row, jnp.sum(values, 1, keepdims=True), 0.0)

    sums = []
    for share in (low_ref, high_ref):
        layers = spread(share[0] * z_flow_ref[0], 0, 1)
        layers = layers + spread(share[nz - 1] * z_flow_ref[1], lanes - ny, 1)
        rows = spread(share[:, 0, :] * y_flow_ref[0], 0, ny)
        rows = rows + spread(share[:, ny - 1, :] * y_flow_ref[1], ny - 1, ny)
        sums.append(jnp.sum(layers, 0, keepdims=True) + jnp.sum(rows, 0, keepdims=True))
    ends = ends_ref[...]
    message_ref[...] = jnp.concatenate([ends[0:1] + sums[0], ends[1:2] + sums[1], ends[2:8]], 0)


def x_source_kernel(
    local_ref, z_flow_ref, y_flow_ref, left_ref, right_ref, inverse_ref, part_ref, source_ref
):
    nz, ny, nx = local_ref.shape
    source_ref[...] = local_ref[...]
    source_ref[0] += z_flow_ref[0]
    source_ref[nz - 1] += z_flow_ref[1]
    source_ref[:, 0, :] += y_flow_ref[0]
    source_ref[:, ny - 1, :] += y_flow_ref[1]
    source = source_ref[...].reshape(nz * ny, nx).T
    part_ref[...] = reduce_source(source, 0, left_ref, right_ref, inverse_ref[...])


def y_bands_kernel(halo_count, conduct_ref, *refs):
    y_halo = refs[:halo_count]
    yl_ref, yr_ref, ylow_ref, yhigh_ref, yinv_ref, yends_ref, *y_two_refs = refs[halo_count:]
    nz, ny, nx = conduct_ref.shape
    index_y = lax.axis_index("gy")
    conduct = conduct_ref[...]
    row = lax.broadcasted_iota(jnp.int32, conduct.shape, 1)
    link = jnp.where(row > 0, link_of(FLAT_SCALE, conduct, roll(conduct, 1, 1)), 0.0)
    low, high, inverse, own = reduce_interior(link, 1, yl_ref, yr_ref)
    ylow_ref[...], yhigh_ref[...], yinv_ref[...] = low, high, inverse
    below, above = pick_halo("gy", y_halo, index_y % 2 == 1)
    first = link_of(FLAT_SCALE, conduct_ref[:, 0, :], conduct_ref[:, 1, :])
    last = link_of(FLAT_SCALE, conduct_ref[:, ny - 1, :], conduct_ref[:, ny - 2, :])
    own_first, own_last, between = end_bands(link, first, last, 1, high, own)
    outer_low = link_of(FLAT_SCALE, conduct_ref[:, 0, :], below[1])
    outer_high = link_of(FLAT_SCALE, conduct_ref[:, ny - 1, :], above[1])
    for i, value in enumerate((first, last, own_first, own_last, between, outer_low, outer_high)):
        yends_ref[i] = value
    if y_two_refs:
        ysum_ref, yshare_ref = y_two_refs
        odd = index_y % 2 == 1
        near_own, far_own = jnp.where(odd, own_first, own_last), jnp.where(odd, own_last, own_first)
        share = between / (far_own + between)
        ysum_ref[0] = near_own + share * far_own
        ysum_ref[1] = share
        for k in range(nz):
            near, far = jnp.where(odd, low[k], high[k]), jnp.where(odd, high[k], low[k])
            yshare_ref[k] = near + ysum_ref[1, pl.ds(k, 1), :] * far


def chain_message(ends_ref, source_first, source_last, message_ref):
    own_first, own_last, between, outer = (ends_ref[i] for i in range(2, 6))
    inverse = 1.0 / (own_first + between + outer)
    message_ref[0] = outer * between * inverse
    message_ref[1] = outer * own_first * inverse
    message_ref[2] = outer * inverse * source_first
    message_ref[3] = own_last + between * own_first * inverse
    message_ref[4] = source_last + between * inverse * source_first


def chain_ends(name, messages, ends_ref, source_first, blocks_ref, state_ref):
    count, index = lax.axis_size(name), lax.axis_index(name)
    for shift, message in enumerate(messages):
        blocks_ref[lax.rem(index - shift + count, count)] = message[...]
    blocks = [tuple(blocks_ref[k, i] for i in range(5)) for k in range(count)]
    below, last = chain(blocks, count, index, state_ref)
    own_first, between, outer = ends_ref[2], ends_ref[4], ends_ref[5]
    first = (source_first + outer * below + between * last) / (own_first + between + outer)
    return first, last


def y_message_kernel(
    count_x, count_y, heat_ref, part_ref, low_ref, high_ref, yends_ref, *refs
):
    messages, refs = refs[:count_x], refs[count_x:]
    shares, refs = (refs[:2], refs[2:]) if count_y > 2 else (refs[:1], refs[1:])
    sums_ref, refs = (None, refs) if count_y > 2 else (refs[0], refs[1:])
    source_ref, message_ref, blocks_ref, rows_ref, state_ref = refs
    nz, ny, nx = heat_ref.shape
    index = lax.axis_index("gx") // 2
    for shift, message in enumerate(messages):
        blocks_ref[lax.rem(index - shift + count_x, count_x)] = message[...]
    first, last, own_first, own_last, between, c_first, c_last = (
        blocks_ref[:, i, :] for i in range(7)
    )
    before = jnp.zeros_like(c_last[:1])
    if count_x > 1:
        before = jnp.concatenate([before, c_last[:-1]], 0)
    outer = link_of(FLAT_SCALE, c_first, before)
    inverse = 1.0 / (own_first + between + outer)
    rows = (
        outer * between * inverse,
        outer * own_first * inverse,
        outer * inverse * first,
        own_last + between * own_first * inverse,
        last + between * inverse * first,
        first * inverse,
        outer * inverse,
        between * inverse,
    )
    for i, value in enumerate(rows):
        rows_ref[i] = value
    whole = lambda i, k: jnp.broadcast_to(rows_ref[i, pl.ds(k, 1), :], (8, rows_ref.shape[2]))
    blocks = [tuple(whole(i, k) for i in range(5)) for k in range(count_x)]
    below, last = chain(blocks, count_x, index, state_ref)
    first = whole(5, index) + whole(6, index) * below + whole(7, index) * last
    lines = part_ref[...] + low_ref[...] * first[:1] + high_ref[...] * last[:1]
    source = lines.T.reshape(nz, ny, nx) - 2.0 * heat_ref[...]
    source_ref[...] = source
    sums = [jnp.sum(share[...] * source, 1) for share in shares]
    if count_y > 2:
        chain_message(yends_ref, *sums, message_ref)
    else:
        message_ref[0], message_ref[1] = sums_ref[0], sums[0]


def y_source_kernel(
    source_ref, yl_ref, yr_ref, yinv_ref, yends_ref, ypart_ref, ysource_ref
):
    ny = source_ref.shape[1]
    part = reduce_source(source_ref[...], 1, yl_ref, yr_ref, yinv_ref[...])
    ypart_ref[...] = part
    ysource_ref[0] = source_ref[:, 0, :] + yends_ref[0] * ypart_ref[:, 1, :]
    ysource_ref[1] = source_ref[:, ny - 1, :] + yends_ref[1] * ypart_ref[:, ny - 2, :]


def z_message_kernel(
    count_y, ypart_ref, ylow_ref, yhigh_ref, yends_ref, ysource_ref, zlow_ref, zhigh_ref,
    zends_ref, *refs
):
    messages, refs = refs[:count_y], refs[count_y:]
    source_ref, zsource_ref, message_ref, ends_ref, *state = refs
    nz, ny, nx = ypart_ref.shape
    if count_y > 2:
        first, last = chain_ends("gy", messages, yends_ref, ysource_ref[0], *state)
    else:
        odd = lax.axis_index("gy") % 2 == 1
        mine, other = messages
        outer = jnp.where(odd, yends_ref[5], yends_ref[6])
        between = yends_ref[4]
        factor = outer / (other[0] + outer)
        near = (mine[1] + factor * other[1]) / (mine[0] + factor * other[0])
        far_own = jnp.where(odd, yends_ref[3], yends_ref[2])
        far_source = jnp.where(odd, ysource_ref[1], ysource_ref[0])
        far = (far_source + between * near) / (far_own + between)
        first, last = jnp.where(odd, near, far), jnp.where(odd, far, near)
    ends_ref[0], ends_ref[1] = first, last
    source_first, source_last = jnp.zeros((ny, nx), F32), jnp.zeros((ny, nx), F32)
    for k in range(nz):
        source = (
            ypart_ref[k]
            + ylow_ref[k] * ends_ref[0, pl.ds(k, 1), :]
            + yhigh_ref[k] * ends_ref[1, pl.ds(k, 1), :]
        )
        source_ref[k] = source
        source_first = source_first + zlow_ref[k] * source
        source_last = source_last + zhigh_ref[k] * source
    zsource_ref[...] = source_first
    outer, between, inverse = (zends_ref[i] for i in range(3))
    message_ref[0], message_ref[1], message_ref[3] = (zends_ref[i] for i in range(3, 6))
    message_ref[2] = outer * inverse * source_first
    message_ref[4] = source_last + between * inverse * source_first


def z_source_kernel(source_ref, zl_ref, zr_ref, zinv_ref, zpart_ref):
    zpart_ref[...] = reduce_source(source_ref[...], 0, zl_ref, zr_ref, zinv_ref[...])


def finish_kernel(
    count_z, heat_ref, zpart_ref, zlow_ref, zhigh_ref, zends_ref, zsource_ref, *refs
):
    messages, (theirs_ref, mine_ref, blocks_ref, state_ref) = refs[:count_z], refs[count_z:]
    index = lax.axis_index("gz")
    for shift, message in enumerate(messages):
        blocks_ref[lax.rem(index - shift + count_z, count_z)] = message[...]
    blocks = [tuple(blocks_ref[k, i] for i in range(5)) for k in range(count_z)]
    below, last = chain(blocks, count_z, index, state_ref)
    outer, between, inverse = (zends_ref[i] for i in range(3))
    first = (zsource_ref[...] + outer * below + between * last) * inverse
    nx = theirs_ref.shape[-1]
    heated = heat_ref[...] + zpart_ref[...] + zlow_ref[...] * first + zhigh_ref[...] * last
    theirs_ref[...], mine_ref[...] = heated[:, :, :nx], heated[:, :, nx:]


VMEM = pl.BlockSpec(memory_space=pltpu.VMEM)
HBM = pl.BlockSpec(memory_space=pltpu.HBM)


def call(kernel, outs, operands, scratch=(), specs=None, ops=200_000, vmem=32):
    return pl.pallas_call(
        kernel,
        out_shape=[jax.ShapeDtypeStruct(out, F32) if isinstance(out, tuple) else out for out in outs],
        in_specs=specs or [VMEM] * len(operands),
        out_specs=[VMEM] * len(outs),
        scratch_shapes=[pltpu.VMEM(item, F32) if isinstance(item, tuple) else item for item in scratch],
        compiler_params=pltpu.CompilerParams(vmem_limit_bytes=vmem * 1024 * 1024),
        cost_estimate=pl.CostEstimate(flops=ops, bytes_accessed=ops, transcendentals=0),
    )(*operands)


def neighbour_swaps(name, other, faces):
    count, width = lax.axis_size(name), lax.axis_size(other)
    received = [lax.ppermute(faces[0], name, [(i, i ^ 1) for i in range(count)])]
    if count > 2:
        pairs = []
        for j in range(width):
            for i in range(count):
                at = (j ^ 1, i) if i in (0, count - 1) else (j, ((i + 1) ^ 1) - 1)
                pairs.append(((j, i), at))
        if (other, name) == ("gy", "gz"):
            axes, place = (other, name), lambda at: at[0] * count + at[1]
        else:
            axes, place = (name, other), lambda at: at[1] * width + at[0]
        pairs = [(place(source), place(target)) for source, target in pairs]
        received.append(lax.ppermute(faces[1], axes, pairs))
    return received


def swap_all(name, message, stride=1):
    count = lax.axis_size(name)
    return [message] + [
        lax.ppermute(message, name, [(i, (i + shift) % count) for i in range(count)])
        for shift in range(stride, count, stride)
    ]


def other_core(values):
    count = lax.axis_size("gx")
    return lax.ppermute(values, "gx", [(i, i ^ 1) for i in range(count)])


def chip_step(heat_a, label_a, edge_a, heat_b, conduct_b, edge_b, table):
    nz, ny, half = heat_a.shape
    nx = 2 * half
    block, lines, layer, rows = (nz, ny, nx), (nx, nz * ny), (ny, nx), (nz, nx)
    count_x, count_y, count_z = (lax.axis_size(name) for name in ("gx", "gy", "gz"))
    count_x = count_x // 2
    x_steps, y_steps, z_steps = (len(steps_of(length)) for length in (nx, ny, nz))

    halo_counts = swaps_along("gz"), swaps_along("gy")
    heat, conduct, edge, *faces = call(
        start_kernel,
        [block, block, layer] + [(2, *layer)] * halo_counts[0] + [(2, *rows)] * halo_counts[1],
        [heat_a, label_a, edge_a, heat_b, conduct_b, edge_b, table],
    )
    z_halo = neighbour_swaps("gz", "gy", faces[: halo_counts[0]])
    y_halo = neighbour_swaps("gy", "gz", faces[halo_counts[0] :])

    (
        x_left, x_right, x_low, x_high, x_inverse, x_ends, x_local, x_low_block, x_high_block,
        z_left, z_right, z_low, z_high, z_inverse, z_inner,
    ) = call(
        x_bands_kernel,
        [(x_steps, *lines)] * 2 + [lines] * 3 + [(8, lines[1])] + [block] * 3
        + [(z_steps, *block)] * 2 + [block] * 3 + [(3, *layer)],
        [heat, conduct],
    )
    x_message, z_flow, y_flow, z_ends = call(
        functools.partial(x_message_kernel, halo_counts),
        [(8, lines[1]), (2, *layer), (2, *rows), (6, *layer)],
        [heat, conduct, edge, x_low_block, x_high_block, x_ends, z_inner,
         *join_halos(z_halo, y_halo)],
    )
    x_messages = swap_all("gx", x_message, 2)
    two = count_y == 2
    y_left, y_right, y_low, y_high, y_inverse, y_ends, *y_two = call(
        functools.partial(y_bands_kernel, len(y_halo)),
        [(y_steps, *block)] * 2 + [block] * 3 + [(7, *rows)] + [(2, *rows), block] * two,
        [conduct, *y_halo],
    )
    y_sum, y_share = y_two[:1], y_two[1:]
    (x_part,) = call(
        x_source_kernel,
        [lines],
        [x_local, z_flow, y_flow, x_left, x_right, x_inverse],
        [block],
    )
    y_rows = 2 if two else 5
    y_source, y_message = call(
        functools.partial(y_message_kernel, count_x, count_y),
        [block, (y_rows, *rows)],
        [heat, x_part, x_low, x_high, y_ends, *x_messages, *(y_share or (y_low, y_high)), *y_sum],
        [(count_x, 8, lines[1]), (8, count_x, lines[1]), (5, count_x, 8, lines[1])],
    )
    y_messages = swap_all("gy", y_message)
    y_part, y_end_sources = call(
        y_source_kernel,
        [block, (2, *rows)],
        [y_source, y_left, y_right, y_inverse, y_ends],
    )
    z_source, z_first, z_message = call(
        functools.partial(z_message_kernel, count_y),
        [block, layer, (5, *layer)],
        [y_part, y_low, y_high, y_ends, y_end_sources, z_low, z_high, z_ends, *y_messages],
        [(2, *rows)] + ([] if two else [(count_y, y_rows, *rows), (5, count_y, *rows)]),
    )
    z_messages = swap_all("gz", z_message)
    (z_part,) = call(z_source_kernel, [block], [z_source, z_left, z_right, z_inverse])
    return call(
        functools.partial(finish_kernel, count_z),
        [heat_a.shape] * 2,
        [heat, z_part, z_low, z_high, z_ends, z_first, *z_messages],
        [(count_z, 5, *layer), (5, count_z, *layer)],
    )


def local(heat, label, table, edge):
    label_a, heat_a, edge_a = (other_core(values) for values in (label, heat, edge))
    entries = table.shape[0]
    own_heat, own_conduct, rows, own_edge = call(
        stage_kernel,
        [heat.shape, heat.shape, (entries, 8, heat.shape[-1]),
         jax.ShapeDtypeStruct(edge.shape, edge.dtype)],
        [heat, label, table, edge],
        [pltpu.VMEM(label.shape, label.dtype), pltpu.SMEM(table.shape, F32),
         pltpu.SemaphoreType.DMA((4,))],
        [HBM] * 4,
        vmem=60,
    )
    second = lax.axis_index("gx") % 2 == 1
    theirs, mine = lax.cond(
        second,
        chip_step,
        lambda heat_a, label_a, edge_a, heat_b, *rest: (heat_a, heat_b),
        heat_a, label_a, edge_a, own_heat, own_conduct, own_edge, rows,
    )
    return jnp.where(second, mine, other_core(theirs))


def solution(mesh):
    return jax.shard_map(
        local,
        mesh=mesh,
        in_specs=(P("gz", "gy", "gx"), P("gz", "gy", "gx"), P(), P("gy", "gx")),
        out_specs=P("gz", "gy", "gx"),
        check_vma=False,
    )
```

```python
import functools

import jax
import jax.numpy as jnp
from jax import lax
from jax.experimental import pallas as pl
from jax.experimental.pallas import tpu as pltpu
from jax.sharding import PartitionSpec as P

FLAT_SCALE = 1000.0
UPWARD_SCALE = 200.0
F32 = jnp.float32


def link_of(scale, one, other):
    return scale * one * other / (one + other)


def roll(values, offset, axis):
    if axis == 0 and values.ndim == 3:
        offset = offset % values.shape[0]
        return jnp.concatenate([values[-offset:], values[:-offset]], 0)
    return pltpu.roll(values, offset % values.shape[axis], axis)


def steps_of(length):
    steps, distance = [], 1
    while distance < length - 1:
        steps.append(distance)
        distance *= 2
    return steps


def reduce_interior(link, axis, left_ref, right_ref):
    length = link.shape[axis]
    row = lax.broadcasted_iota(jnp.int32, link.shape, axis)
    low, high, own = link, roll(link, -1, axis), jnp.ones_like(link)
    high = jnp.where(row == length - 1, 0.0, high)
    for step, distance in enumerate(steps_of(length)):
        inverse = 1.0 / (own + low + high)
        open_low, open_high = row > distance, row < length - 1 - distance
        left = jnp.where(open_low, low * roll(inverse, distance, axis), 0.0)
        right = jnp.where(open_high, high * roll(inverse, -distance, axis), 0.0)
        left_ref[step], right_ref[step] = left, right
        own = own + left * roll(own, distance, axis) + right * roll(own, -distance, axis)
        low = jnp.where(open_low, left * roll(low, distance, axis), low)
        high = jnp.where(open_high, right * roll(high, -distance, axis), high)
    inverse = 1.0 / (own + low + high)
    inner = (row > 0) & (row < length - 1)
    share_low = jnp.where(inner, low * inverse, jnp.where(row == 0, 1.0, 0.0))
    share_high = jnp.where(inner, high * inverse, jnp.where(row == 0, 0.0, 1.0))
    return share_low, share_high, jnp.where(inner, inverse, 0.0), own * inverse


def reduce_source(source, axis, left_ref, right_ref, inverse):
    length = source.shape[axis]
    for step, distance in enumerate(steps_of(length)):
        source = (
            source
            + left_ref[step] * roll(source, distance, axis)
            + right_ref[step] * roll(source, -distance, axis)
        )
    return source * inverse


def chain(blocks, count, index, state):
    own = [blocks[k][3] + (blocks[k + 1][1] if k + 1 < count else 0.0) for k in range(count)]
    source = [blocks[k][4] + (blocks[k + 1][2] if k + 1 < count else 0.0) for k in range(count)]
    shape = own[0].shape
    state[0, 0], state[1, 0] = jnp.ones(shape, F32), jnp.zeros(shape, F32)
    up_own, up_source = own[0], source[0]
    for k in range(1, count):
        state[0, k], state[1, k] = up_own, up_source
        factor = blocks[k][0] / (up_own + blocks[k][0])
        up_own, up_source = own[k] + factor * up_own, source[k] + factor * up_source
    down_own, down_source = own[count - 1], source[count - 1]
    state[2, count - 1], state[3, count - 1] = down_own, down_source
    for k in range(count - 2, -1, -1):
        factor = blocks[k + 1][0] / (down_own + blocks[k + 1][0])
        down_own, down_source = own[k] + factor * down_own, source[k] + factor * down_source
        state[2, k], state[3, k] = down_own, down_source
    for k in range(count):
        state[4, k] = blocks[k][0]
    up_own, up_source, down_own, down_source, link = (state[i, index] for i in range(5))
    inverse = 1.0 / (up_own * down_own + link * (up_own + down_own))
    below = ((down_own + link) * up_source + link * down_source) * inverse
    here = ((up_own + link) * down_source + link * up_source) * inverse
    return below, here


def pick_halo(name, received, odd):
    first = received[0][...]
    second = received[1][...] if len(received) > 1 else jnp.zeros_like(first)
    index, count = lax.axis_index(name), lax.axis_size(name)
    below = jnp.where(odd, first, second)
    above = jnp.where(odd, second, first)
    return jnp.where(index > 0, below, 0.0), jnp.where(index < count - 1, above, 0.0)


def swaps_along(name):
    return min(lax.axis_size(name) - 1, 2)


def look_up(label, table_ref):
    conduct = jnp.broadcast_to(table_ref[0], label.shape)
    for entry in range(1, table_ref.shape[0]):
        conduct = jnp.where(label == entry, table_ref[entry], conduct)
    return conduct


def stage_kernel(
    heat_in, label_in, table_in, edge_in, heat_ref, conduct_ref, table_ref, edge_ref, label_ref,
    entries_ref, sems
):
    copies = [
        pltpu.make_async_copy(source, target, sems.at[i])
        for i, (source, target) in enumerate(
            (
                (table_in, entries_ref), (label_in, label_ref), (heat_in, heat_ref),
                (edge_in, edge_ref),
            )
        )
    ]
    for copy in copies:
        copy.start()
    copies[0].wait()
    for entry in range(table_ref.shape[0]):
        table_ref[entry] = jnp.full(table_ref.shape[1:], entries_ref[entry], F32)
    copies[1].wait()
    conduct_ref[...] = look_up(label_ref[...], table_ref)
    copies[2].wait()
    copies[3].wait()


def join_halos(z_halo, y_halo):
    return [*z_halo[1:], z_halo[0], *y_halo]


def split_halos(counts, refs):
    halos = refs[: sum(counts)]
    return [halos[counts[0] - 1], *halos[: counts[0] - 1]], halos[counts[0] :]


def start_kernel(
    heat_a_ref, label_a_ref, edge_a_ref, heat_b_ref, conduct_b_ref, edge_b_ref, table_ref,
    heat_ref, conduct_ref, edge_ref, *faces
):
    nx = heat_a_ref.shape[-1]
    heat_ref[:, :, :nx], heat_ref[:, :, nx:] = heat_a_ref[...], heat_b_ref[...]
    conduct_ref[:, :, :nx] = look_up(label_a_ref[...], table_ref)
    conduct_ref[:, :, nx:] = conduct_b_ref[...]
    edge_ref[:, :nx] = edge_a_ref[...].astype(F32)
    edge_ref[:, nx:] = edge_b_ref[...].astype(F32)
    z_faces, y_faces = faces[: swaps_along("gz")], faces[swaps_along("gz") :]
    odd_z = lax.axis_index("gz") % 2 == 1
    odd_y = lax.axis_index("gy") % 2 == 1
    for i, ref in enumerate((heat_ref, conduct_ref)):
        low, high = ref[0], ref[ref.shape[0] - 1]
        for face_ref, pick in zip(z_faces, (odd_z, ~odd_z)):
            face_ref[i] = jnp.where(pick, low, high)
        low, high = ref[:, 0, :], ref[:, ref.shape[1] - 1, :]
        for face_ref, pick in zip(y_faces, (odd_y, ~odd_y)):
            face_ref[i] = jnp.where(pick, low, high)


def end_bands(link, first, last, axis, high, own):
    length = high.shape[axis]
    at = lambda values, i: lax.index_in_dim(values, i, axis, keepdims=False)
    return (
        1.0 + first * at(own, 1),
        1.0 + last * at(own, length - 2),
        first * at(high, 1),
    )


def x_bands_kernel(
    heat_ref, conduct_ref, left_ref, right_ref, low_ref, high_ref, inverse_ref, ends_ref, local_ref,
    low_block_ref, high_block_ref, zl_ref, zr_ref, zlow_ref, zhigh_ref, zinv_ref, zinner_ref,
    yl_ref, yr_ref, ylow_ref, yhigh_ref, yinv_ref, yends_ref, *y_two_refs
):
    nz, ny, nx = conduct_ref.shape
    conduct = conduct_ref[...]
    link = link_of(UPWARD_SCALE, conduct[1:], conduct[:-1])
    link = jnp.concatenate([jnp.zeros_like(conduct[:1]), link], 0)
    low, high, inverse, own = reduce_interior(link, 0, zl_ref, zr_ref)
    zlow_ref[...], zhigh_ref[...], zinv_ref[...] = low, high, inverse
    for i, value in enumerate(end_bands(link, link[1], link[nz - 1], 0, high, own)):
        zinner_ref[i] = value
    row = lax.broadcasted_iota(jnp.int32, conduct.shape, 1)
    link = jnp.where(row > 0, link_of(FLAT_SCALE, conduct, roll(conduct, 1, 1)), 0.0)
    link_y = link
    low, high, inverse, own = reduce_interior(link, 1, yl_ref, yr_ref)
    ylow_ref[...], yhigh_ref[...], yinv_ref[...] = low, high, inverse
    first = link_of(FLAT_SCALE, conduct_ref[:, 0, :], conduct_ref[:, 1, :])
    last = link_of(FLAT_SCALE, conduct_ref[:, ny - 1, :], conduct_ref[:, ny - 2, :])
    own_first, own_last, between = end_bands(link, first, last, 1, high, own)
    for i, value in enumerate((first, last, own_first, own_last, between)):
        yends_ref[i] = value
    if y_two_refs:
        ysum_ref, yshare_ref, factor_ref = y_two_refs
        odd = lax.axis_index("gy") % 2 == 1
        near_own, far_own = jnp.where(odd, own_first, own_last), jnp.where(odd, own_last, own_first)
        share = between / (far_own + between)
        ysum_ref[...] = near_own + share * far_own
        factor_ref[...] = share
        for k in range(nz):
            near, far = jnp.where(odd, low[k], high[k]), jnp.where(odd, high[k], low[k])
            yshare_ref[k] = near + factor_ref[pl.ds(k, 1), :] * far
    heat = heat_ref[...]
    local = 2.0 * heat
    across = 2.0 * link_of(UPWARD_SCALE, conduct[1:], conduct[:-1]) * (heat[1:] - heat[:-1])
    nothing = jnp.zeros_like(heat[:1])
    local = local + jnp.concatenate([across, nothing], 0) - jnp.concatenate([nothing, across], 0)
    across = 2.0 * link_y * (heat - roll(heat, 1, 1))
    local = local - across + roll(across, -1, 1)
    local_ref[...] = local
    lines = conduct.reshape(nz * ny, nx).T
    row = lax.broadcasted_iota(jnp.int32, lines.shape, 0)
    link = jnp.where(row > 0, link_of(FLAT_SCALE, lines, roll(lines, 1, 0)), 0.0)
    low, high, inverse, own = reduce_interior(link, 0, left_ref, right_ref)
    low_ref[...], high_ref[...], inverse_ref[...] = low, high, inverse
    low_block_ref[...] = low.T.reshape(nz, ny, nx)
    high_block_ref[...] = high.T.reshape(nz, ny, nx)
    local = local.reshape(nz * ny, nx).T
    first, last = link[1:2], link[nx - 1 :]
    ends_ref[...] = jnp.concatenate(
        [
            jnp.sum(low * local, 0, keepdims=True),
            jnp.sum(high * local, 0, keepdims=True),
            1.0 + first * own[1:2],
            1.0 + last * own[nx - 2 : nx - 1],
            first * high[1:2],
            lines[:1],
            lines[nx - 1 :],
            jnp.zeros_like(first),
        ],
        0,
    )


def x_message_kernel(
    halo_counts, heat_ref, conduct_ref, edge_ref, low_ref, high_ref, ends_ref, zinner_ref, *refs
):
    z_halo, y_halo = split_halos(halo_counts, refs)
    message_ref, z_flow_ref, y_flow_ref, zends_ref, youter_ref = refs[sum(halo_counts) :]
    nz, ny, nx = conduct_ref.shape
    lanes = nz * ny
    index_z, index_y = lax.axis_index("gz"), lax.axis_index("gy")
    below, above = pick_halo("gz", z_halo, index_z % 2 == 1)
    ground = jnp.where(index_z == 0, UPWARD_SCALE * conduct_ref[0] * edge_ref[...], 0.0)
    outer = link_of(UPWARD_SCALE, conduct_ref[0], below[1])
    z_flow_ref[0] = 2.0 * (outer * (below[0] - heat_ref[0]) - ground * heat_ref[0])
    own_first, own_last, between = zinner_ref[0] + ground, zinner_ref[1], zinner_ref[2]
    inverse = 1.0 / (own_first + between + outer)
    for i, value in enumerate((outer, between, inverse)):
        zends_ref[i] = value
    zends_ref[3] = outer * between * inverse
    zends_ref[4] = outer * own_first * inverse
    zends_ref[5] = own_last + between * own_first * inverse
    flow = link_of(UPWARD_SCALE, conduct_ref[nz - 1], above[1]) * (above[0] - heat_ref[nz - 1])
    z_flow_ref[1] = 2.0 * flow
    below, above = pick_halo("gy", y_halo, index_y % 2 == 1)
    youter_ref[0] = link_of(FLAT_SCALE, conduct_ref[:, 0, :], below[1])
    youter_ref[1] = link_of(FLAT_SCALE, conduct_ref[:, ny - 1, :], above[1])
    y_flow_ref[0] = 2.0 * youter_ref[0] * (below[0] - heat_ref[:, 0, :])
    y_flow_ref[1] = 2.0 * youter_ref[1] * (above[0] - heat_ref[:, ny - 1, :])

    def spread(values, first, step):
        shape = (values.shape[0], lanes)
        row = lax.broadcasted_iota(jnp.int32, shape, 0)
        lane = lax.broadcasted_iota(jnp.int32, shape, 1)
        return jnp.where(lane == first + step * row, jnp.sum(values, 1, keepdims=True), 0.0)

    sums = []
    for share in (low_ref, high_ref):
        layers = spread(share[0] * z_flow_ref[0], 0, 1)
        layers = layers + spread(share[nz - 1] * z_flow_ref[1], lanes - ny, 1)
        rows = spread(share[:, 0, :] * y_flow_ref[0], 0, ny)
        rows = rows + spread(share[:, ny - 1, :] * y_flow_ref[1], ny - 1, ny)
        sums.append(jnp.sum(layers, 0, keepdims=True) + jnp.sum(rows, 0, keepdims=True))
    ends = ends_ref[...]
    message_ref[...] = jnp.concatenate([ends[0:1] + sums[0], ends[1:2] + sums[1], ends[2:8]], 0)


def x_source_kernel(
    local_ref, z_flow_ref, y_flow_ref, left_ref, right_ref, inverse_ref, part_ref, source_ref
):
    nz, ny, nx = local_ref.shape
    source_ref[...] = local_ref[...]
    source_ref[0] += z_flow_ref[0]
    source_ref[nz - 1] += z_flow_ref[1]
    source_ref[:, 0, :] += y_flow_ref[0]
    source_ref[:, ny - 1, :] += y_flow_ref[1]
    source = source_ref[...].reshape(nz * ny, nx).T
    part_ref[...] = reduce_source(source, 0, left_ref, right_ref, inverse_ref[...])


def chain_message(ends_ref, outer_ref, source_first, source_last, message_ref):
    own_first, own_last, between = (ends_ref[i] for i in range(2, 5))
    outer = outer_ref[0]
    inverse = 1.0 / (own_first + between + outer)
    message_ref[0] = outer * between * inverse
    message_ref[1] = outer * own_first * inverse
    message_ref[2] = outer * inverse * source_first
    message_ref[3] = own_last + between * own_first * inverse
    message_ref[4] = source_last + between * inverse * source_first


def chain_ends(name, messages, ends_ref, outer_ref, source_first, blocks_ref, state_ref):
    count, index = lax.axis_size(name), lax.axis_index(name)
    for shift, message in enumerate(messages):
        blocks_ref[lax.rem(index - shift + count, count)] = message[...]
    blocks = [tuple(blocks_ref[k, i] for i in range(5)) for k in range(count)]
    below, last = chain(blocks, count, index, state_ref)
    own_first, between, outer = ends_ref[2], ends_ref[4], outer_ref[0]
    first = (source_first + outer * below + between * last) / (own_first + between + outer)
    return first, last


def y_message_kernel(
    count_x, count_y, heat_ref, part_ref, low_ref, high_ref, yends_ref, youter_ref, *refs
):
    messages, refs = refs[:count_x], refs[count_x:]
    shares, refs = (refs[:2], refs[2:]) if count_y > 2 else (refs[:1], refs[1:])
    source_ref, message_ref, blocks_ref, rows_ref, state_ref = refs
    nz, ny, nx = heat_ref.shape
    index = lax.axis_index("gx") // 2
    for shift, message in enumerate(messages):
        blocks_ref[lax.rem(index - shift + count_x, count_x)] = message[...]
    first, last, own_first, own_last, between, c_first, c_last = (
        blocks_ref[:, i, :] for i in range(7)
    )
    before = jnp.zeros_like(c_last[:1])
    if count_x > 1:
        before = jnp.concatenate([before, c_last[:-1]], 0)
    outer = link_of(FLAT_SCALE, c_first, before)
    inverse = 1.0 / (own_first + between + outer)
    rows = (
        outer * between * inverse,
        outer * own_first * inverse,
        outer * inverse * first,
        own_last + between * own_first * inverse,
        last + between * inverse * first,
        first * inverse,
        outer * inverse,
        between * inverse,
    )
    for i, value in enumerate(rows):
        rows_ref[i] = value
    whole = lambda i, k: jnp.broadcast_to(rows_ref[i, pl.ds(k, 1), :], (8, rows_ref.shape[2]))
    blocks = [tuple(whole(i, k) for i in range(5)) for k in range(count_x)]
    below, last = chain(blocks, count_x, index, state_ref)
    first = whole(5, index) + whole(6, index) * below + whole(7, index) * last
    lines = part_ref[...] + low_ref[...] * first[:1] + high_ref[...] * last[:1]
    source = lines.T.reshape(nz, ny, nx) - 2.0 * heat_ref[...]
    source_ref[...] = source
    sums = [jnp.sum(share[...] * source, 1) for share in shares]
    if count_y > 2:
        chain_message(yends_ref, youter_ref, *sums, message_ref)
    else:
        message_ref[0] = sums[0]


def y_source_kernel(
    source_ref, yl_ref, yr_ref, yinv_ref, yends_ref, ypart_ref, ysource_ref
):
    ny = source_ref.shape[1]
    part = reduce_source(source_ref[...], 1, yl_ref, yr_ref, yinv_ref[...])
    ypart_ref[...] = part
    ysource_ref[0] = source_ref[:, 0, :] + yends_ref[0] * ypart_ref[:, 1, :]
    ysource_ref[1] = source_ref[:, ny - 1, :] + yends_ref[1] * ypart_ref[:, ny - 2, :]


def z_message_kernel(
    count_y, ypart_ref, ylow_ref, yhigh_ref, yends_ref, youter_ref, ysource_ref, zlow_ref,
    zhigh_ref, zends_ref, *refs
):
    messages, refs = refs[:count_y], refs[count_y:]
    owns, refs = ((), refs) if count_y > 2 else (refs[:2], refs[2:])
    source_ref, zsource_ref, message_ref, ends_ref, *state = refs
    nz, ny, nx = ypart_ref.shape
    if count_y > 2:
        first, last = chain_ends(
            "gy", messages, yends_ref, youter_ref, ysource_ref[0], *state
        )
    else:
        odd = lax.axis_index("gy") % 2 == 1
        mine, other = messages
        outer = jnp.where(odd, youter_ref[0], youter_ref[1])
        between = yends_ref[4]
        mine_own, other_own = (own[...] for own in owns)
        factor = outer / (other_own + outer)
        near = (mine[0] + factor * other[0]) / (mine_own + factor * other_own)
        far_own = jnp.where(odd, yends_ref[3], yends_ref[2])
        far_source = jnp.where(odd, ysource_ref[1], ysource_ref[0])
        far = (far_source + between * near) / (far_own + between)
        first, last = jnp.where(odd, near, far), jnp.where(odd, far, near)
    ends_ref[0], ends_ref[1] = first, last
    source_first, source_last = jnp.zeros((ny, nx), F32), jnp.zeros((ny, nx), F32)
    for k in range(nz):
        source = (
            ypart_ref[k]
            + ylow_ref[k] * ends_ref[0, pl.ds(k, 1), :]
            + yhigh_ref[k] * ends_ref[1, pl.ds(k, 1), :]
        )
        source_ref[k] = source
        source_first = source_first + zlow_ref[k] * source
        source_last = source_last + zhigh_ref[k] * source
    zsource_ref[...] = source_first
    outer, between, inverse = (zends_ref[i] for i in range(3))
    message_ref[0], message_ref[1], message_ref[3] = (zends_ref[i] for i in range(3, 6))
    message_ref[2] = outer * inverse * source_first
    message_ref[4] = source_last + between * inverse * source_first


def z_source_kernel(source_ref, zl_ref, zr_ref, zinv_ref, zpart_ref):
    zpart_ref[...] = reduce_source(source_ref[...], 0, zl_ref, zr_ref, zinv_ref[...])


def finish_kernel(
    count_z, heat_ref, zpart_ref, zlow_ref, zhigh_ref, zends_ref, zsource_ref, *refs
):
    messages, (theirs_ref, mine_ref, blocks_ref, state_ref) = refs[:count_z][::-1], refs[count_z:]
    index = lax.axis_index("gz")
    for shift, message in enumerate(messages):
        blocks_ref[lax.rem(index - shift + count_z, count_z)] = message[...]
    blocks = [tuple(blocks_ref[k, i] for i in range(5)) for k in range(count_z)]
    below, last = chain(blocks, count_z, index, state_ref)
    outer, between, inverse = (zends_ref[i] for i in range(3))
    first = (zsource_ref[...] + outer * below + between * last) * inverse
    nx = theirs_ref.shape[-1]
    heated = heat_ref[...] + zpart_ref[...] + zlow_ref[...] * first + zhigh_ref[...] * last
    theirs_ref[...], mine_ref[...] = heated[:, :, :nx], heated[:, :, nx:]


VMEM = pl.BlockSpec(memory_space=pltpu.VMEM)
HBM = pl.BlockSpec(memory_space=pltpu.HBM)


def call(kernel, outs, operands, scratch=(), specs=None, ops=200_000, vmem=32):
    return pl.pallas_call(
        kernel,
        out_shape=[jax.ShapeDtypeStruct(out, F32) if isinstance(out, tuple) else out for out in outs],
        in_specs=specs or [VMEM] * len(operands),
        out_specs=[VMEM] * len(outs),
        scratch_shapes=[pltpu.VMEM(item, F32) if isinstance(item, tuple) else item for item in scratch],
        compiler_params=pltpu.CompilerParams(vmem_limit_bytes=vmem * 1024 * 1024),
        cost_estimate=pl.CostEstimate(flops=ops, bytes_accessed=ops, transcendentals=0),
    )(*operands)


def neighbour_swaps(name, other, faces):
    count, width = lax.axis_size(name), lax.axis_size(other)
    received = [lax.ppermute(faces[0], name, [(i, i ^ 1) for i in range(count)])]
    if count > 2:
        pairs = []
        for j in range(width):
            for i in range(count):
                at = (j ^ 1, i) if i in (0, count - 1) else (j, ((i + 1) ^ 1) - 1)
                pairs.append(((j, i), at))
        if (other, name) == ("gy", "gz"):
            axes, place = (other, name), lambda at: at[0] * count + at[1]
        else:
            axes, place = (name, other), lambda at: at[1] * width + at[0]
        pairs = [(place(source), place(target)) for source, target in pairs]
        received.append(lax.ppermute(faces[1], axes, pairs))
    return received


def swap_all(name, message, stride=1):
    count = lax.axis_size(name)
    return [message] + [
        lax.ppermute(message, name, [(i, (i + shift) % count) for i in range(count)])
        for shift in range(stride, count, stride)
    ]


def other_core(values):
    count = lax.axis_size("gx")
    return lax.ppermute(values, "gx", [(i, i ^ 1) for i in range(count)])


def chip_step(heat_a, label_a, edge_a, heat_b, conduct_b, edge_b, table):
    nz, ny, half = heat_a.shape
    nx = 2 * half
    block, lines, layer, rows = (nz, ny, nx), (nx, nz * ny), (ny, nx), (nz, nx)
    count_x, count_y, count_z = (lax.axis_size(name) for name in ("gx", "gy", "gz"))
    count_x = count_x // 2
    x_steps, y_steps, z_steps = (len(steps_of(length)) for length in (nx, ny, nz))

    halo_counts = swaps_along("gz"), swaps_along("gy")
    two = count_y == 2
    heat, conduct, edge, *faces = call(
        start_kernel,
        [block, block, layer] + [(2, *layer)] * halo_counts[0] + [(2, *rows)] * halo_counts[1],
        [heat_a, label_a, edge_a, heat_b, conduct_b, edge_b, table],
    )
    z_halo = neighbour_swaps("gz", "gy", faces[: halo_counts[0]])
    y_halo = neighbour_swaps("gy", "gz", faces[halo_counts[0] :])

    (
        x_left, x_right, x_low, x_high, x_inverse, x_ends, x_local, x_low_block, x_high_block,
        z_left, z_right, z_low, z_high, z_inverse, z_inner,
        y_left, y_right, y_low, y_high, y_inverse, y_ends, *y_two,
    ) = call(
        x_bands_kernel,
        [(x_steps, *lines)] * 2 + [lines] * 3 + [(8, lines[1])] + [block] * 3
        + [(z_steps, *block)] * 2 + [block] * 3 + [(3, *layer)]
        + [(y_steps, *block)] * 2 + [block] * 3 + [(5, *rows)] + [rows, block] * two,
        [heat, conduct],
        [rows] * two,
    )
    y_sum, y_share = y_two[:1], y_two[1:]
    y_sums = swap_all("gy", y_sum[0]) if two else []
    x_message, z_flow, y_flow, z_ends, y_outer = call(
        functools.partial(x_message_kernel, halo_counts),
        [(8, lines[1]), (2, *layer), (2, *rows), (6, *layer), (2, *rows)],
        [heat, conduct, edge, x_low_block, x_high_block, x_ends, z_inner,
         *join_halos(z_halo, y_halo)],
    )
    x_messages = swap_all("gx", x_message, 2)
    (x_part,) = call(
        x_source_kernel,
        [lines],
        [x_local, z_flow, y_flow, x_left, x_right, x_inverse],
        [block],
    )
    y_rows = 1 if two else 5
    y_source, y_message = call(
        functools.partial(y_message_kernel, count_x, count_y),
        [block, (y_rows, *rows)],
        [heat, x_part, x_low, x_high, y_ends, y_outer, *x_messages, *(y_share or (y_low, y_high))],
        [(count_x, 8, lines[1]), (8, count_x, lines[1]), (5, count_x, 8, lines[1])],
    )
    y_messages = swap_all("gy", y_message)
    y_part, y_end_sources = call(
        y_source_kernel,
        [block, (2, *rows)],
        [y_source, y_left, y_right, y_inverse, y_ends],
    )
    z_source, z_first, z_message = call(
        functools.partial(z_message_kernel, count_y),
        [block, layer, (5, *layer)],
        [y_part, y_low, y_high, y_ends, y_outer, y_end_sources, z_low, z_high, z_ends, *y_messages,
         *y_sums],
        [(2, *rows)] + ([] if two else [(count_y, y_rows, *rows), (5, count_y, *rows)]),
    )
    z_messages = swap_all("gz", z_message)
    (z_part,) = call(z_source_kernel, [block], [z_source, z_left, z_right, z_inverse])
    return call(
        functools.partial(finish_kernel, count_z),
        [heat_a.shape] * 2,
        [heat, z_part, z_low, z_high, z_ends, z_first, *z_messages[::-1]],
        [(count_z, 5, *layer), (5, count_z, *layer)],
    )


def local(heat, label, table, edge):
    label_a, heat_a, edge_a = (other_core(values) for values in (label, heat, edge))
    entries = table.shape[0]
    own_heat, own_conduct, rows, own_edge = call(
        stage_kernel,
        [heat.shape, heat.shape, (entries, 8, heat.shape[-1]),
         jax.ShapeDtypeStruct(edge.shape, edge.dtype)],
        [heat, label, table, edge],
        [pltpu.VMEM(label.shape, label.dtype), pltpu.SMEM(table.shape, F32),
         pltpu.SemaphoreType.DMA((4,))],
        [HBM] * 4,
        vmem=60,
    )
    second = lax.axis_index("gx") % 2 == 1
    theirs, mine = lax.cond(
        second,
        chip_step,
        lambda heat_a, label_a, edge_a, heat_b, *rest: (heat_a, heat_b),
        heat_a, label_a, edge_a, own_heat, own_conduct, own_edge, rows,
    )
    return jnp.where(second, mine, other_core(theirs))


def solution(mesh):
    return jax.shard_map(
        local,
        mesh=mesh,
        in_specs=(P("gz", "gy", "gx"), P("gz", "gy", "gx"), P(), P("gy", "gx")),
        out_specs=P("gz", "gy", "gx"),
        check_vma=False,
    )
```

```python
import functools

import jax
import jax.numpy as jnp
from jax import lax
from jax.experimental import pallas as pl
from jax.experimental.pallas import tpu as pltpu
from jax.sharding import PartitionSpec as P

FLAT_SCALE = 1000.0
UPWARD_SCALE = 200.0
F32 = jnp.float32


def link_of(scale, one, other):
    return scale * one * other / (one + other)


def roll(values, offset, axis):
    if axis == 0 and values.ndim == 3:
        offset = offset % values.shape[0]
        return jnp.concatenate([values[-offset:], values[:-offset]], 0)
    return pltpu.roll(values, offset % values.shape[axis], axis)


def steps_of(length):
    steps, distance = [], 1
    while distance < length - 1:
        steps.append(distance)
        distance *= 2
    return steps


def reduce_interior(link, axis, left_ref, right_ref):
    length = link.shape[axis]
    row = lax.broadcasted_iota(jnp.int32, link.shape, axis)
    low, high, own = link, roll(link, -1, axis), jnp.ones_like(link)
    high = jnp.where(row == length - 1, 0.0, high)
    for step, distance in enumerate(steps_of(length)):
        inverse = 1.0 / (own + low + high)
        open_low, open_high = row > distance, row < length - 1 - distance
        left = jnp.where(open_low, low * roll(inverse, distance, axis), 0.0)
        right = jnp.where(open_high, high * roll(inverse, -distance, axis), 0.0)
        left_ref[step], right_ref[step] = left, right
        own = own + left * roll(own, distance, axis) + right * roll(own, -distance, axis)
        low = jnp.where(open_low, left * roll(low, distance, axis), low)
        high = jnp.where(open_high, right * roll(high, -distance, axis), high)
    inverse = 1.0 / (own + low + high)
    inner = (row > 0) & (row < length - 1)
    share_low = jnp.where(inner, low * inverse, jnp.where(row == 0, 1.0, 0.0))
    share_high = jnp.where(inner, high * inverse, jnp.where(row == 0, 0.0, 1.0))
    return share_low, share_high, jnp.where(inner, inverse, 0.0), own * inverse


def reduce_source(source, axis, left_ref, right_ref, inverse):
    length = source.shape[axis]
    for step, distance in enumerate(steps_of(length)):
        source = (
            source
            + left_ref[step] * roll(source, distance, axis)
            + right_ref[step] * roll(source, -distance, axis)
        )
    return source * inverse


def halvings(count):
    rows, stages = list(range(count)), []
    while len(rows) > 1:
        near = [
            (row, rows[i - 1] if i else None, rows[i + 1] if i + 1 < len(rows) else None)
            for i, row in enumerate(rows)
        ]
        stages.append((near[0::2], near[1::2]))
        rows = rows[0::2]
    return stages


def reduce_lines(link, left_ref, right_ref, kept_ref, gone_ref):
    length = link.shape[0]
    count = length // 8
    row = lax.broadcasted_iota(jnp.int32, link.shape, 0)
    low, high, own = link, roll(link, -1, 0), jnp.ones_like(link)
    for step, distance in enumerate((1, 2, 4)):
        inverse = 1.0 / (own + low + high)
        open_low, open_high = row > distance, row < length - 1 - distance
        left = jnp.where(open_low, low * roll(inverse, distance, 0), 0.0)
        right = jnp.where(open_high, high * roll(inverse, -distance, 0), 0.0)
        left_ref[step], right_ref[step] = left, right
        own = own + left * roll(own, distance, 0) + right * roll(own, -distance, 0)
        low = jnp.where(open_low, left * roll(low, distance, 0), low)
        high = jnp.where(open_high, right * roll(high, -distance, 0), high)
    first, last = row == 0, row == length - 1
    own = jnp.where(first | last, 0.0, own)
    low = jnp.where(first, 1.0, jnp.where(last, 0.0, low))
    high = jnp.where(last, 1.0, jnp.where(first, 0.0, high))
    tiles = lambda values: [values[8 * k : 8 * k + 8] for k in range(count)]
    own, low, high = tiles(own), tiles(low), tiles(high)
    inverse, share_low, share_high, share_own = {}, {}, {}, {}

    def finish(k):
        inverse[k] = 1.0 / (own[k] + low[k] + high[k])
        gone_ref[0, k], gone_ref[1, k] = low[k] * inverse[k], high[k] * inverse[k]
        gone_ref[2, k] = inverse[k]

    slot = 0
    for kept, gone in halvings(count):
        for k, _, _ in gone:
            finish(k)
        for k, below, above in kept:
            new_low, new_high = low[k], high[k]
            if below is not None:
                factor = low[k] * inverse[below]
                kept_ref[0, slot] = factor
                own[k] = own[k] + factor * own[below]
                new_low = factor * low[below]
            if above is not None:
                factor = high[k] * inverse[above]
                kept_ref[1, slot] = factor
                own[k] = own[k] + factor * own[above]
                new_high = factor * high[above]
            low[k], high[k] = new_low, new_high
            slot += 1
    finish(0)
    share_low[0], share_high[0] = low[0] * inverse[0], high[0] * inverse[0]
    share_own[0] = own[0] * inverse[0]
    for _, gone in halvings(count)[::-1]:
        for k, below, above in gone:
            to_low, to_high = low[k] * inverse[k], high[k] * inverse[k]
            share_low[k] = to_low * share_low[below]
            share_high[k] = to_low * share_high[below]
            if above is None:
                share_high[k] = share_high[k] + to_high
                share_own[k] = own[k] * inverse[k] + to_low * share_own[below]
            else:
                share_low[k] = share_low[k] + to_high * share_low[above]
                share_high[k] = share_high[k] + to_high * share_high[above]
    whole = lambda shares: jnp.concatenate([shares[k] for k in range(count)], 0)
    return whole(share_low), whole(share_high), share_own[0][1:2], share_own[count - 1][6:7]


def solve_lines(source, left_ref, right_ref, kept_ref, gone_ref):
    length = source.shape[0]
    count = length // 8
    for step, distance in enumerate((1, 2, 4)):
        source = (
            source
            + left_ref[step] * roll(source, distance, 0)
            + right_ref[step] * roll(source, -distance, 0)
        )
    row = lax.broadcasted_iota(jnp.int32, source.shape, 0)
    source = jnp.where((row == 0) | (row == length - 1), 0.0, source)
    source = [source[8 * k : 8 * k + 8] for k in range(count)]
    slot, stages = 0, halvings(count)
    for kept, _ in stages:
        for k, below, above in kept:
            if below is not None:
                source[k] = source[k] + kept_ref[0, slot] * source[below]
            if above is not None:
                source[k] = source[k] + kept_ref[1, slot] * source[above]
            slot += 1
    solved = {0: source[0] * gone_ref[2, 0]}
    for _, gone in stages[::-1]:
        for k, below, above in gone:
            solved[k] = source[k] * gone_ref[2, k] + gone_ref[0, k] * solved[below]
            if above is not None:
                solved[k] = solved[k] + gone_ref[1, k] * solved[above]
    return jnp.concatenate([solved[k] for k in range(count)], 0)


def chain(blocks, count, index, state):
    own = [blocks[k][3] + (blocks[k + 1][1] if k + 1 < count else 0.0) for k in range(count)]
    source = [blocks[k][4] + (blocks[k + 1][2] if k + 1 < count else 0.0) for k in range(count)]
    shape = own[0].shape
    state[0, 0], state[1, 0] = jnp.ones(shape, F32), jnp.zeros(shape, F32)
    up_own, up_source = own[0], source[0]
    for k in range(1, count):
        state[0, k], state[1, k] = up_own, up_source
        factor = blocks[k][0] / (up_own + blocks[k][0])
        up_own, up_source = own[k] + factor * up_own, source[k] + factor * up_source
    down_own, down_source = own[count - 1], source[count - 1]
    state[2, count - 1], state[3, count - 1] = down_own, down_source
    for k in range(count - 2, -1, -1):
        factor = blocks[k + 1][0] / (down_own + blocks[k + 1][0])
        down_own, down_source = own[k] + factor * down_own, source[k] + factor * down_source
        state[2, k], state[3, k] = down_own, down_source
    for k in range(count):
        state[4, k] = blocks[k][0]
    up_own, up_source, down_own, down_source, link = (state[i, index] for i in range(5))
    inverse = 1.0 / (up_own * down_own + link * (up_own + down_own))
    below = ((down_own + link) * up_source + link * down_source) * inverse
    here = ((up_own + link) * down_source + link * up_source) * inverse
    return below, here


def pick_halo(name, received, odd):
    first = received[0][...]
    second = received[1][...] if len(received) > 1 else jnp.zeros_like(first)
    index, count = lax.axis_index(name), lax.axis_size(name)
    below = jnp.where(odd, first, second)
    above = jnp.where(odd, second, first)
    return jnp.where(index > 0, below, 0.0), jnp.where(index < count - 1, above, 0.0)


def swaps_along(name):
    return min(lax.axis_size(name) - 1, 2)


def look_up(label, table_ref):
    conduct = jnp.broadcast_to(table_ref[0], label.shape)
    for entry in range(1, table_ref.shape[0]):
        conduct = jnp.where(label == entry, table_ref[entry], conduct)
    return conduct


def stage_kernel(
    heat_in, label_in, table_in, edge_in, heat_ref, conduct_ref, table_ref, edge_ref, label_ref,
    entries_ref, sems
):
    copies = [
        pltpu.make_async_copy(source, target, sems.at[i])
        for i, (source, target) in enumerate(
            (
                (table_in, entries_ref), (label_in, label_ref), (heat_in, heat_ref),
                (edge_in, edge_ref),
            )
        )
    ]
    for copy in copies:
        copy.start()
    copies[0].wait()
    for entry in range(table_ref.shape[0]):
        table_ref[entry] = jnp.full(table_ref.shape[1:], entries_ref[entry], F32)
    copies[1].wait()
    conduct_ref[...] = look_up(label_ref[...], table_ref)
    copies[2].wait()
    copies[3].wait()


def join_halos(z_halo, y_halo):
    return [*z_halo[1:], z_halo[0], *y_halo]


def split_halos(counts, refs):
    halos = refs[: sum(counts)]
    return [halos[counts[0] - 1], *halos[: counts[0] - 1]], halos[counts[0] :]


def start_kernel(
    heat_a_ref, label_a_ref, edge_a_ref, heat_b_ref, conduct_b_ref, edge_b_ref, table_ref,
    heat_ref, conduct_ref, edge_ref, *faces
):
    nx = heat_a_ref.shape[-1]
    heat_ref[:, :, :nx], heat_ref[:, :, nx:] = heat_a_ref[...], heat_b_ref[...]
    conduct_ref[:, :, :nx] = look_up(label_a_ref[...], table_ref)
    conduct_ref[:, :, nx:] = conduct_b_ref[...]
    edge_ref[:, :nx] = edge_a_ref[...].astype(F32)
    edge_ref[:, nx:] = edge_b_ref[...].astype(F32)
    z_faces, y_faces = faces[: swaps_along("gz")], faces[swaps_along("gz") :]
    odd_z = lax.axis_index("gz") % 2 == 1
    odd_y = lax.axis_index("gy") % 2 == 1
    for i, ref in enumerate((heat_ref, conduct_ref)):
        low, high = ref[0], ref[ref.shape[0] - 1]
        for face_ref, pick in zip(z_faces, (odd_z, ~odd_z)):
            face_ref[i] = jnp.where(pick, low, high)
        low, high = ref[:, 0, :], ref[:, ref.shape[1] - 1, :]
        for face_ref, pick in zip(y_faces, (odd_y, ~odd_y)):
            face_ref[i] = jnp.where(pick, low, high)


def end_bands(link, first, last, axis, high, own):
    length = high.shape[axis]
    at = lambda values, i: lax.index_in_dim(values, i, axis, keepdims=False)
    return (
        1.0 + first * at(own, 1),
        1.0 + last * at(own, length - 2),
        first * at(high, 1),
    )


def x_bands_kernel(
    heat_ref, conduct_ref, left_ref, right_ref, low_ref, high_ref, kept_ref, gone_ref, ends_ref,
    local_ref, low_block_ref, high_block_ref, zl_ref, zr_ref, zlow_ref, zhigh_ref, zinv_ref, zinner_ref
):
    nz, ny, nx = conduct_ref.shape
    conduct = conduct_ref[...]
    link = link_of(UPWARD_SCALE, conduct[1:], conduct[:-1])
    link = jnp.concatenate([jnp.zeros_like(conduct[:1]), link], 0)
    low, high, inverse, own = reduce_interior(link, 0, zl_ref, zr_ref)
    zlow_ref[...], zhigh_ref[...], zinv_ref[...] = low, high, inverse
    for i, value in enumerate(end_bands(link, link[1], link[nz - 1], 0, high, own)):
        zinner_ref[i] = value
    heat = heat_ref[...]
    local = 2.0 * heat
    across = 2.0 * link_of(UPWARD_SCALE, conduct[1:], conduct[:-1]) * (heat[1:] - heat[:-1])
    nothing = jnp.zeros_like(heat[:1])
    local = local + jnp.concatenate([across, nothing], 0) - jnp.concatenate([nothing, across], 0)
    row = lax.broadcasted_iota(jnp.int32, conduct.shape, 1)
    across = 2.0 * link_of(FLAT_SCALE, conduct, roll(conduct, 1, 1)) * (heat - roll(heat, 1, 1))
    across = jnp.where(row > 0, across, 0.0)
    local = local - across + roll(across, -1, 1)
    local_ref[...] = local
    lines = conduct.reshape(nz * ny, nx).T
    row = lax.broadcasted_iota(jnp.int32, lines.shape, 0)
    link = jnp.where(row > 0, link_of(FLAT_SCALE, lines, roll(lines, 1, 0)), 0.0)
    low, high, own_low, own_high = reduce_lines(link, left_ref, right_ref, kept_ref, gone_ref)
    low_ref[...], high_ref[...] = low, high
    low_block_ref[...] = low.T.reshape(nz, ny, nx)
    high_block_ref[...] = high.T.reshape(nz, ny, nx)
    local = local.reshape(nz * ny, nx).T
    first, last = link[1:2], link[nx - 1 :]
    ends_ref[...] = jnp.concatenate(
        [
            jnp.sum(low * local, 0, keepdims=True),
            jnp.sum(high * local, 0, keepdims=True),
            1.0 + first * own_low,
            1.0 + last * own_high,
            first * high[1:2],
            lines[:1],
            lines[nx - 1 :],
            jnp.zeros_like(first),
        ],
        0,
    )


def x_message_kernel(
    halo_counts, heat_ref, conduct_ref, edge_ref, low_ref, high_ref, ends_ref, zinner_ref, *refs
):
    z_halo, y_halo = split_halos(halo_counts, refs)
    message_ref, z_flow_ref, y_flow_ref, zends_ref = refs[sum(halo_counts) :]
    nz, ny, nx = conduct_ref.shape
    lanes = nz * ny
    index_z, index_y = lax.axis_index("gz"), lax.axis_index("gy")
    below, above = pick_halo("gz", z_halo, index_z % 2 == 1)
    ground = jnp.where(index_z == 0, UPWARD_SCALE * conduct_ref[0] * edge_ref[...], 0.0)
    outer = link_of(UPWARD_SCALE, conduct_ref[0], below[1])
    z_flow_ref[0] = 2.0 * (outer * (below[0] - heat_ref[0]) - ground * heat_ref[0])
    own_first, own_last, between = zinner_ref[0] + ground, zinner_ref[1], zinner_ref[2]
    inverse = 1.0 / (own_first + between + outer)
    for i, value in enumerate((outer, between, inverse)):
        zends_ref[i] = value
    zends_ref[3] = outer * between * inverse
    zends_ref[4] = outer * own_first * inverse
    zends_ref[5] = own_last + between * own_first * inverse
    flow = link_of(UPWARD_SCALE, conduct_ref[nz - 1], above[1]) * (above[0] - heat_ref[nz - 1])
    z_flow_ref[1] = 2.0 * flow
    below, above = pick_halo("gy", y_halo, index_y % 2 == 1)
    flow = link_of(FLAT_SCALE, conduct_ref[:, 0, :], below[1]) * (below[0] - heat_ref[:, 0, :])
    y_flow_ref[0] = 2.0 * flow
    flow = link_of(FLAT_SCALE, conduct_ref[:, ny - 1, :], above[1])
    y_flow_ref[1] = 2.0 * flow * (above[0] - heat_ref[:, ny - 1, :])

    def spread(values, first, step):
        shape = (values.shape[0], lanes)
        row = lax.broadcasted_iota(jnp.int32, shape, 0)
        lane = lax.broadcasted_iota(jnp.int32, shape, 1)
        return jnp.where(lane == first + step * row, jnp.sum(values, 1, keepdims=True), 0.0)

    sums = []
    for share in (low_ref, high_ref):
        layers = spread(share[0] * z_flow_ref[0], 0, 1)
        layers = layers + spread(share[nz - 1] * z_flow_ref[1], lanes - ny, 1)
        rows = spread(share[:, 0, :] * y_flow_ref[0], 0, ny)
        rows = rows + spread(share[:, ny - 1, :] * y_flow_ref[1], ny - 1, ny)
        sums.append(jnp.sum(layers, 0, keepdims=True) + jnp.sum(rows, 0, keepdims=True))
    ends = ends_ref[...]
    message_ref[...] = jnp.concatenate([ends[0:1] + sums[0], ends[1:2] + sums[1], ends[2:8]], 0)


def x_source_kernel(
    local_ref, z_flow_ref, y_flow_ref, left_ref, right_ref, kept_ref, gone_ref, part_ref, source_ref
):
    nz, ny, nx = local_ref.shape
    source_ref[...] = local_ref[...]
    source_ref[0] += z_flow_ref[0]
    source_ref[nz - 1] += z_flow_ref[1]
    source_ref[:, 0, :] += y_flow_ref[0]
    source_ref[:, ny - 1, :] += y_flow_ref[1]
    source = source_ref[...].reshape(nz * ny, nx).T
    part_ref[...] = solve_lines(source, left_ref, right_ref, kept_ref, gone_ref)


def y_bands_kernel(halo_count, conduct_ref, *refs):
    y_halo = refs[:halo_count]
    yl_ref, yr_ref, ylow_ref, yhigh_ref, yinv_ref, yends_ref, *y_two_refs = refs[halo_count:]
    nz, ny, nx = conduct_ref.shape
    index_y = lax.axis_index("gy")
    conduct = conduct_ref[...]
    row = lax.broadcasted_iota(jnp.int32, conduct.shape, 1)
    link = jnp.where(row > 0, link_of(FLAT_SCALE, conduct, roll(conduct, 1, 1)), 0.0)
    low, high, inverse, own = reduce_interior(link, 1, yl_ref, yr_ref)
    ylow_ref[...], yhigh_ref[...], yinv_ref[...] = low, high, inverse
    below, above = pick_halo("gy", y_halo, index_y % 2 == 1)
    first = link_of(FLAT_SCALE, conduct_ref[:, 0, :], conduct_ref[:, 1, :])
    last = link_of(FLAT_SCALE, conduct_ref[:, ny - 1, :], conduct_ref[:, ny - 2, :])
    own_first, own_last, between = end_bands(link, first, last, 1, high, own)
    outer_low = link_of(FLAT_SCALE, conduct_ref[:, 0, :], below[1])
    outer_high = link_of(FLAT_SCALE, conduct_ref[:, ny - 1, :], above[1])
    for i, value in enumerate((first, last, own_first, own_last, between, outer_low, outer_high)):
        yends_ref[i] = value
    if y_two_refs:
        ysum_ref, yshare_ref = y_two_refs
        odd = index_y % 2 == 1
        near_own, far_own = jnp.where(odd, own_first, own_last), jnp.where(odd, own_last, own_first)
        share = between / (far_own + between)
        ysum_ref[0] = near_own + share * far_own
        ysum_ref[1] = share
        for k in range(nz):
            near, far = jnp.where(odd, low[k], high[k]), jnp.where(odd, high[k], low[k])
            yshare_ref[k] = near + ysum_ref[1, pl.ds(k, 1), :] * far


def chain_message(ends_ref, source_first, source_last, message_ref):
    own_first, own_last, between, outer = (ends_ref[i] for i in range(2, 6))
    inverse = 1.0 / (own_first + between + outer)
    message_ref[0] = outer * between * inverse
    message_ref[1] = outer * own_first * inverse
    message_ref[2] = outer * inverse * source_first
    message_ref[3] = own_last + between * own_first * inverse
    message_ref[4] = source_last + between * inverse * source_first


def chain_ends(name, messages, ends_ref, source_first, blocks_ref, state_ref):
    count, index = lax.axis_size(name), lax.axis_index(name)
    for shift, message in enumerate(messages):
        blocks_ref[lax.rem(index - shift + count, count)] = message[...]
    blocks = [tuple(blocks_ref[k, i] for i in range(5)) for k in range(count)]
    below, last = chain(blocks, count, index, state_ref)
    own_first, between, outer = ends_ref[2], ends_ref[4], ends_ref[5]
    first = (source_first + outer * below + between * last) / (own_first + between + outer)
    return first, last


def y_message_kernel(
    count_x, count_y, heat_ref, part_ref, low_ref, high_ref, yends_ref, *refs
):
    messages, refs = refs[:count_x], refs[count_x:]
    shares, refs = (refs[:2], refs[2:]) if count_y > 2 else (refs[:1], refs[1:])
    sums_ref, refs = (None, refs) if count_y > 2 else (refs[0], refs[1:])
    source_ref, message_ref, blocks_ref, rows_ref, state_ref = refs
    nz, ny, nx = heat_ref.shape
    index = lax.axis_index("gx") // 2
    for shift, message in enumerate(messages):
        blocks_ref[lax.rem(index - shift + count_x, count_x)] = message[...]
    first, last, own_first, own_last, between, c_first, c_last = (
        blocks_ref[:, i, :] for i in range(7)
    )
    before = jnp.zeros_like(c_last[:1])
    if count_x > 1:
        before = jnp.concatenate([before, c_last[:-1]], 0)
    outer = link_of(FLAT_SCALE, c_first, before)
    inverse = 1.0 / (own_first + between + outer)
    rows = (
        outer * between * inverse,
        outer * own_first * inverse,
        outer * inverse * first,
        own_last + between * own_first * inverse,
        last + between * inverse * first,
        first * inverse,
        outer * inverse,
        between * inverse,
    )
    for i, value in enumerate(rows):
        rows_ref[i] = value
    whole = lambda i, k: jnp.broadcast_to(rows_ref[i, pl.ds(k, 1), :], (8, rows_ref.shape[2]))
    blocks = [tuple(whole(i, k) for i in range(5)) for k in range(count_x)]
    below, last = chain(blocks, count_x, index, state_ref)
    first = whole(5, index) + whole(6, index) * below + whole(7, index) * last
    lines = part_ref[...] + low_ref[...] * first[:1] + high_ref[...] * last[:1]
    source = lines.T.reshape(nz, ny, nx) - 2.0 * heat_ref[...]
    source_ref[...] = source
    sums = [jnp.sum(share[...] * source, 1) for share in shares]
    if count_y > 2:
        chain_message(yends_ref, *sums, message_ref)
    else:
        message_ref[0], message_ref[1] = sums_ref[0], sums[0]


def y_source_kernel(
    source_ref, yl_ref, yr_ref, yinv_ref, yends_ref, ypart_ref, ysource_ref
):
    ny = source_ref.shape[1]
    part = reduce_source(source_ref[...], 1, yl_ref, yr_ref, yinv_ref[...])
    ypart_ref[...] = part
    ysource_ref[0] = source_ref[:, 0, :] + yends_ref[0] * ypart_ref[:, 1, :]
    ysource_ref[1] = source_ref[:, ny - 1, :] + yends_ref[1] * ypart_ref[:, ny - 2, :]


def z_message_kernel(
    count_y, ypart_ref, ylow_ref, yhigh_ref, yends_ref, ysource_ref, zlow_ref, zhigh_ref,
    zends_ref, *refs
):
    messages, refs = refs[:count_y], refs[count_y:]
    source_ref, zsource_ref, message_ref, ends_ref, *state = refs
    nz, ny, nx = ypart_ref.shape
    if count_y > 2:
        first, last = chain_ends("gy", messages, yends_ref, ysource_ref[0], *state)
    else:
        odd = lax.axis_index("gy") % 2 == 1
        mine, other = messages
        outer = jnp.where(odd, yends_ref[5], yends_ref[6])
        between = yends_ref[4]
        factor = outer / (other[0] + outer)
        near = (mine[1] + factor * other[1]) / (mine[0] + factor * other[0])
        far_own = jnp.where(odd, yends_ref[3], yends_ref[2])
        far_source = jnp.where(odd, ysource_ref[1], ysource_ref[0])
        far = (far_source + between * near) / (far_own + between)
        first, last = jnp.where(odd, near, far), jnp.where(odd, far, near)
    ends_ref[0], ends_ref[1] = first, last
    source_first, source_last = jnp.zeros((ny, nx), F32), jnp.zeros((ny, nx), F32)
    for k in range(nz):
        source = (
            ypart_ref[k]
            + ylow_ref[k] * ends_ref[0, pl.ds(k, 1), :]
            + yhigh_ref[k] * ends_ref[1, pl.ds(k, 1), :]
        )
        source_ref[k] = source
        source_first = source_first + zlow_ref[k] * source
        source_last = source_last + zhigh_ref[k] * source
    zsource_ref[...] = source_first
    outer, between, inverse = (zends_ref[i] for i in range(3))
    message_ref[0], message_ref[1], message_ref[3] = (zends_ref[i] for i in range(3, 6))
    message_ref[2] = outer * inverse * source_first
    message_ref[4] = source_last + between * inverse * source_first


def z_source_kernel(source_ref, zl_ref, zr_ref, zinv_ref, zpart_ref):
    zpart_ref[...] = reduce_source(source_ref[...], 0, zl_ref, zr_ref, zinv_ref[...])


def finish_kernel(
    count_z, heat_ref, zpart_ref, zlow_ref, zhigh_ref, zends_ref, zsource_ref, *refs
):
    messages, (theirs_ref, mine_ref, blocks_ref, state_ref) = refs[:count_z], refs[count_z:]
    index = lax.axis_index("gz")
    for shift, message in enumerate(messages):
        blocks_ref[lax.rem(index - shift + count_z, count_z)] = message[...]
    blocks = [tuple(blocks_ref[k, i] for i in range(5)) for k in range(count_z)]
    below, last = chain(blocks, count_z, index, state_ref)
    outer, between, inverse = (zends_ref[i] for i in range(3))
    first = (zsource_ref[...] + outer * below + between * last) * inverse
    nx = theirs_ref.shape[-1]
    heated = heat_ref[...] + zpart_ref[...] + zlow_ref[...] * first + zhigh_ref[...] * last
    theirs_ref[...], mine_ref[...] = heated[:, :, :nx], heated[:, :, nx:]


VMEM = pl.BlockSpec(memory_space=pltpu.VMEM)
HBM = pl.BlockSpec(memory_space=pltpu.HBM)


def call(kernel, outs, operands, scratch=(), specs=None, ops=200_000, vmem=32):
    return pl.pallas_call(
        kernel,
        out_shape=[jax.ShapeDtypeStruct(out, F32) if isinstance(out, tuple) else out for out in outs],
        in_specs=specs or [VMEM] * len(operands),
        out_specs=[VMEM] * len(outs),
        scratch_shapes=[pltpu.VMEM(item, F32) if isinstance(item, tuple) else item for item in scratch],
        compiler_params=pltpu.CompilerParams(vmem_limit_bytes=vmem * 1024 * 1024),
        cost_estimate=pl.CostEstimate(flops=ops, bytes_accessed=ops, transcendentals=0),
    )(*operands)


def neighbour_swaps(name, other, faces):
    count, width = lax.axis_size(name), lax.axis_size(other)
    received = [lax.ppermute(faces[0], name, [(i, i ^ 1) for i in range(count)])]
    if count > 2:
        pairs = []
        for j in range(width):
            for i in range(count):
                at = (j ^ 1, i) if i in (0, count - 1) else (j, ((i + 1) ^ 1) - 1)
                pairs.append(((j, i), at))
        if (other, name) == ("gy", "gz"):
            axes, place = (other, name), lambda at: at[0] * count + at[1]
        else:
            axes, place = (name, other), lambda at: at[1] * width + at[0]
        pairs = [(place(source), place(target)) for source, target in pairs]
        received.append(lax.ppermute(faces[1], axes, pairs))
    return received


def swap_all(name, message, stride=1):
    count = lax.axis_size(name)
    return [message] + [
        lax.ppermute(message, name, [(i, (i + shift) % count) for i in range(count)])
        for shift in range(stride, count, stride)
    ]


def other_core(values):
    count = lax.axis_size("gx")
    return lax.ppermute(values, "gx", [(i, i ^ 1) for i in range(count)])


def chip_step(heat_a, label_a, edge_a, heat_b, conduct_b, edge_b, table):
    nz, ny, half = heat_a.shape
    nx = 2 * half
    block, lines, layer, rows = (nz, ny, nx), (nx, nz * ny), (ny, nx), (nz, nx)
    count_x, count_y, count_z = (lax.axis_size(name) for name in ("gx", "gy", "gz"))
    count_x = count_x // 2
    tiles = (nx // 8, 8, lines[1])
    y_steps, z_steps = (len(steps_of(length)) for length in (ny, nz))

    halo_counts = swaps_along("gz"), swaps_along("gy")
    heat, conduct, edge, *faces = call(
        start_kernel,
        [block, block, layer] + [(2, *layer)] * halo_counts[0] + [(2, *rows)] * halo_counts[1],
        [heat_a, label_a, edge_a, heat_b, conduct_b, edge_b, table],
    )
    z_halo = neighbour_swaps("gz", "gy", faces[: halo_counts[0]])
    y_halo = neighbour_swaps("gy", "gz", faces[halo_counts[0] :])

    (
        x_left, x_right, x_low, x_high, x_kept, x_gone, x_ends, x_local, x_low_block, x_high_block,
        z_left, z_right, z_low, z_high, z_inverse, z_inner,
    ) = call(
        x_bands_kernel,
        [(3, *lines)] * 2 + [lines] * 2 + [(2, *tiles), (3, *tiles), (8, lines[1])] + [block] * 3
        + [(z_steps, *block)] * 2 + [block] * 3 + [(3, *layer)],
        [heat, conduct],
    )
    x_message, z_flow, y_flow, z_ends = call(
        functools.partial(x_message_kernel, halo_counts),
        [(8, lines[1]), (2, *layer), (2, *rows), (6, *layer)],
        [heat, conduct, edge, x_low_block, x_high_block, x_ends, z_inner,
         *join_halos(z_halo, y_halo)],
    )
    x_messages = swap_all("gx", x_message, 2)
    two = count_y == 2
    y_left, y_right, y_low, y_high, y_inverse, y_ends, *y_two = call(
        functools.partial(y_bands_kernel, len(y_halo)),
        [(y_steps, *block)] * 2 + [block] * 3 + [(7, *rows)] + [(2, *rows), block] * two,
        [conduct, *y_halo],
    )
    y_sum, y_share = y_two[:1], y_two[1:]
    (x_part,) = call(
        x_source_kernel,
        [lines],
        [x_local, z_flow, y_flow, x_left, x_right, x_kept, x_gone],
        [block],
    )
    y_rows = 2 if two else 5
    y_source, y_message = call(
        functools.partial(y_message_kernel, count_x, count_y),
        [block, (y_rows, *rows)],
        [heat, x_part, x_low, x_high, y_ends, *x_messages, *(y_share or (y_low, y_high)), *y_sum],
        [(count_x, 8, lines[1]), (8, count_x, lines[1]), (5, count_x, 8, lines[1])],
    )
    y_messages = swap_all("gy", y_message)
    y_part, y_end_sources = call(
        y_source_kernel,
        [block, (2, *rows)],
        [y_source, y_left, y_right, y_inverse, y_ends],
    )
    z_source, z_first, z_message = call(
        functools.partial(z_message_kernel, count_y),
        [block, layer, (5, *layer)],
        [y_part, y_low, y_high, y_ends, y_end_sources, z_low, z_high, z_ends, *y_messages],
        [(2, *rows)] + ([] if two else [(count_y, y_rows, *rows), (5, count_y, *rows)]),
    )
    z_messages = swap_all("gz", z_message)
    (z_part,) = call(z_source_kernel, [block], [z_source, z_left, z_right, z_inverse])
    return call(
        functools.partial(finish_kernel, count_z),
        [heat_a.shape] * 2,
        [heat, z_part, z_low, z_high, z_ends, z_first, *z_messages],
        [(count_z, 5, *layer), (5, count_z, *layer)],
    )


def local(heat, label, table, edge):
    label_a, heat_a, edge_a = (other_core(values) for values in (label, heat, edge))
    entries = table.shape[0]
    own_heat, own_conduct, rows, own_edge = call(
        stage_kernel,
        [heat.shape, heat.shape, (entries, 8, heat.shape[-1]),
         jax.ShapeDtypeStruct(edge.shape, edge.dtype)],
        [heat, label, table, edge],
        [pltpu.VMEM(label.shape, label.dtype), pltpu.SMEM(table.shape, F32),
         pltpu.SemaphoreType.DMA((4,))],
        [HBM] * 4,
        vmem=60,
    )
    second = lax.axis_index("gx") % 2 == 1
    theirs, mine = lax.cond(
        second,
        chip_step,
        lambda heat_a, label_a, edge_a, heat_b, *rest: (heat_a, heat_b),
        heat_a, label_a, edge_a, own_heat, own_conduct, own_edge, rows,
    )
    return jnp.where(second, mine, other_core(theirs))


def solution(mesh):
    return jax.shard_map(
        local,
        mesh=mesh,
        in_specs=(P("gz", "gy", "gx"), P("gz", "gy", "gx"), P(), P("gy", "gx")),
        out_specs=P("gz", "gy", "gx"),
        check_vma=False,
    )
```

```python
import functools

import jax
import jax.numpy as jnp
from jax import lax
from jax.experimental import pallas as pl
from jax.experimental.pallas import tpu as pltpu
from jax.sharding import PartitionSpec as P

FLAT_SCALE = 1000.0
UPWARD_SCALE = 200.0
F32 = jnp.float32


def link_of(scale, one, other):
    return scale * one * other / (one + other)


def roll(values, offset, axis):
    if axis == 0 and values.ndim == 3:
        offset = offset % values.shape[0]
        return jnp.concatenate([values[-offset:], values[:-offset]], 0)
    return pltpu.roll(values, offset % values.shape[axis], axis)


def steps_of(length):
    steps, distance = [], 1
    while distance < length - 1:
        steps.append(distance)
        distance *= 2
    return steps


def reduce_interior(link, axis, left_ref, right_ref):
    length = link.shape[axis]
    row = lax.broadcasted_iota(jnp.int32, link.shape, axis)
    low, high, own = link, roll(link, -1, axis), jnp.ones_like(link)
    high = jnp.where(row == length - 1, 0.0, high)
    for step, distance in enumerate(steps_of(length)):
        inverse = 1.0 / (own + low + high)
        open_low, open_high = row > distance, row < length - 1 - distance
        left = jnp.where(open_low, low * roll(inverse, distance, axis), 0.0)
        right = jnp.where(open_high, high * roll(inverse, -distance, axis), 0.0)
        left_ref[step], right_ref[step] = left, right
        own = own + left * roll(own, distance, axis) + right * roll(own, -distance, axis)
        low = jnp.where(open_low, left * roll(low, distance, axis), low)
        high = jnp.where(open_high, right * roll(high, -distance, axis), high)
    inverse = 1.0 / (own + low + high)
    inner = (row > 0) & (row < length - 1)
    share_low = jnp.where(inner, low * inverse, jnp.where(row == 0, 1.0, 0.0))
    share_high = jnp.where(inner, high * inverse, jnp.where(row == 0, 0.0, 1.0))
    return share_low, share_high, jnp.where(inner, inverse, 0.0), own * inverse


def reduce_source(source, axis, left_ref, right_ref, inverse):
    length = source.shape[axis]
    for step, distance in enumerate(steps_of(length)):
        source = (
            source
            + left_ref[step] * roll(source, distance, axis)
            + right_ref[step] * roll(source, -distance, axis)
        )
    return source * inverse


def halvings(count):
    rows, stages = list(range(count)), []
    while len(rows) > 1:
        near = [
            (row, rows[i - 1] if i else None, rows[i + 1] if i + 1 < len(rows) else None)
            for i, row in enumerate(rows)
        ]
        stages.append((near[0::2], near[1::2]))
        rows = rows[0::2]
    return stages


def reduce_lines(link, left_ref, right_ref, kept_ref, gone_ref):
    length = link.shape[0]
    count = length // 8
    row = lax.broadcasted_iota(jnp.int32, link.shape, 0)
    low, high, own = link, roll(link, -1, 0), jnp.ones_like(link)
    for step, distance in enumerate((1, 2, 4)):
        inverse = 1.0 / (own + low + high)
        open_low, open_high = row > distance, row < length - 1 - distance
        left = jnp.where(open_low, low * roll(inverse, distance, 0), 0.0)
        right = jnp.where(open_high, high * roll(inverse, -distance, 0), 0.0)
        left_ref[step], right_ref[step] = left, right
        own = own + left * roll(own, distance, 0) + right * roll(own, -distance, 0)
        low = jnp.where(open_low, left * roll(low, distance, 0), low)
        high = jnp.where(open_high, right * roll(high, -distance, 0), high)
    first, last = row == 0, row == length - 1
    own = jnp.where(first | last, 0.0, own)
    low = jnp.where(first, 1.0, jnp.where(last, 0.0, low))
    high = jnp.where(last, 1.0, jnp.where(first, 0.0, high))
    tiles = lambda values: [values[8 * k : 8 * k + 8] for k in range(count)]
    own, low, high = tiles(own), tiles(low), tiles(high)
    inverse, share_low, share_high, share_own = {}, {}, {}, {}

    def finish(k):
        inverse[k] = 1.0 / (own[k] + low[k] + high[k])
        gone_ref[0, k], gone_ref[1, k] = low[k] * inverse[k], high[k] * inverse[k]
        gone_ref[2, k] = inverse[k]

    slot = 0
    for kept, gone in halvings(count):
        for k, _, _ in gone:
            finish(k)
        for k, below, above in kept:
            new_low, new_high = low[k], high[k]
            if below is not None:
                factor = low[k] * inverse[below]
                kept_ref[0, slot] = factor
                own[k] = own[k] + factor * own[below]
                new_low = factor * low[below]
            if above is not None:
                factor = high[k] * inverse[above]
                kept_ref[1, slot] = factor
                own[k] = own[k] + factor * own[above]
                new_high = factor * high[above]
            low[k], high[k] = new_low, new_high
            slot += 1
    finish(0)
    share_low[0], share_high[0] = low[0] * inverse[0], high[0] * inverse[0]
    share_own[0] = own[0] * inverse[0]
    for _, gone in halvings(count)[::-1]:
        for k, below, above in gone:
            to_low, to_high = low[k] * inverse[k], high[k] * inverse[k]
            share_low[k] = to_low * share_low[below]
            share_high[k] = to_low * share_high[below]
            if above is None:
                share_high[k] = share_high[k] + to_high
                share_own[k] = own[k] * inverse[k] + to_low * share_own[below]
            else:
                share_low[k] = share_low[k] + to_high * share_low[above]
                share_high[k] = share_high[k] + to_high * share_high[above]
    whole = lambda shares: jnp.concatenate([shares[k] for k in range(count)], 0)
    return whole(share_low), whole(share_high), share_own[0][1:2], share_own[count - 1][6:7]


def solve_lines(source, left_ref, right_ref, kept_ref, gone_ref):
    length = source.shape[0]
    count = length // 8
    for step, distance in enumerate((1, 2, 4)):
        source = (
            source
            + left_ref[step] * roll(source, distance, 0)
            + right_ref[step] * roll(source, -distance, 0)
        )
    row = lax.broadcasted_iota(jnp.int32, source.shape, 0)
    source = jnp.where((row == 0) | (row == length - 1), 0.0, source)
    source = [source[8 * k : 8 * k + 8] for k in range(count)]
    slot, stages = 0, halvings(count)
    for kept, _ in stages:
        for k, below, above in kept:
            if below is not None:
                source[k] = source[k] + kept_ref[0, slot] * source[below]
            if above is not None:
                source[k] = source[k] + kept_ref[1, slot] * source[above]
            slot += 1
    solved = {0: source[0] * gone_ref[2, 0]}
    for _, gone in stages[::-1]:
        for k, below, above in gone:
            solved[k] = source[k] * gone_ref[2, k] + gone_ref[0, k] * solved[below]
            if above is not None:
                solved[k] = solved[k] + gone_ref[1, k] * solved[above]
    return jnp.concatenate([solved[k] for k in range(count)], 0)


def chain(blocks, count, index, state):
    own = [blocks[k][3] + (blocks[k + 1][1] if k + 1 < count else 0.0) for k in range(count)]
    source = [blocks[k][4] + (blocks[k + 1][2] if k + 1 < count else 0.0) for k in range(count)]
    shape = own[0].shape
    state[0, 0], state[1, 0] = jnp.ones(shape, F32), jnp.zeros(shape, F32)
    up_own, up_source = own[0], source[0]
    for k in range(1, count):
        state[0, k], state[1, k] = up_own, up_source
        factor = blocks[k][0] / (up_own + blocks[k][0])
        up_own, up_source = own[k] + factor * up_own, source[k] + factor * up_source
    down_own, down_source = own[count - 1], source[count - 1]
    state[2, count - 1], state[3, count - 1] = down_own, down_source
    for k in range(count - 2, -1, -1):
        factor = blocks[k + 1][0] / (down_own + blocks[k + 1][0])
        down_own, down_source = own[k] + factor * down_own, source[k] + factor * down_source
        state[2, k], state[3, k] = down_own, down_source
    for k in range(count):
        state[4, k] = blocks[k][0]
    up_own, up_source, down_own, down_source, link = (state[i, index] for i in range(5))
    inverse = 1.0 / (up_own * down_own + link * (up_own + down_own))
    below = ((down_own + link) * up_source + link * down_source) * inverse
    here = ((up_own + link) * down_source + link * up_source) * inverse
    return below, here


def pick_halo(name, received, odd):
    first = received[0][...]
    second = received[1][...] if len(received) > 1 else jnp.zeros_like(first)
    index, count = lax.axis_index(name), lax.axis_size(name)
    below = jnp.where(odd, first, second)
    above = jnp.where(odd, second, first)
    return jnp.where(index > 0, below, 0.0), jnp.where(index < count - 1, above, 0.0)


def swaps_along(name):
    return min(lax.axis_size(name) - 1, 2)


def look_up(label, table_ref):
    conduct = jnp.broadcast_to(table_ref[0], label.shape)
    for entry in range(1, table_ref.shape[0]):
        conduct = jnp.where(label == entry, table_ref[entry], conduct)
    return conduct


def stage_kernel(
    heat_in, label_in, table_in, edge_in, heat_ref, conduct_ref, table_ref, edge_ref, label_ref,
    entries_ref, sems
):
    copies = [
        pltpu.make_async_copy(source, target, sems.at[i])
        for i, (source, target) in enumerate(
            (
                (table_in, entries_ref), (label_in, label_ref), (heat_in, heat_ref),
                (edge_in, edge_ref),
            )
        )
    ]
    for copy in copies:
        copy.start()
    copies[0].wait()
    for entry in range(table_ref.shape[0]):
        table_ref[entry] = jnp.full(table_ref.shape[1:], entries_ref[entry], F32)
    copies[1].wait()
    conduct_ref[...] = look_up(label_ref[...], table_ref)
    copies[2].wait()
    copies[3].wait()


def join_halos(z_halo, y_halo):
    return [*z_halo[1:], z_halo[0], *y_halo]


def split_halos(counts, refs):
    halos = refs[: sum(counts)]
    return [halos[counts[0] - 1], *halos[: counts[0] - 1]], halos[counts[0] :]


def start_kernel(
    heat_a_ref, label_a_ref, edge_a_ref, heat_b_ref, conduct_b_ref, edge_b_ref, table_ref,
    heat_ref, conduct_ref, edge_ref, *faces
):
    nx = heat_a_ref.shape[-1]
    heat_ref[:, :, :nx], heat_ref[:, :, nx:] = heat_a_ref[...], heat_b_ref[...]
    conduct_ref[:, :, :nx] = look_up(label_a_ref[...], table_ref)
    conduct_ref[:, :, nx:] = conduct_b_ref[...]
    edge_ref[:, :nx] = edge_a_ref[...].astype(F32)
    edge_ref[:, nx:] = edge_b_ref[...].astype(F32)
    z_faces, y_faces = faces[: swaps_along("gz")], faces[swaps_along("gz") :]
    odd_z = lax.axis_index("gz") % 2 == 1
    odd_y = lax.axis_index("gy") % 2 == 1
    for i, ref in enumerate((heat_ref, conduct_ref)):
        low, high = ref[0], ref[ref.shape[0] - 1]
        for face_ref, pick in zip(z_faces, (odd_z, ~odd_z)):
            face_ref[i] = jnp.where(pick, low, high)
        low, high = ref[:, 0, :], ref[:, ref.shape[1] - 1, :]
        for face_ref, pick in zip(y_faces, (odd_y, ~odd_y)):
            face_ref[i] = jnp.where(pick, low, high)


def end_bands(link, first, last, axis, high, own):
    length = high.shape[axis]
    at = lambda values, i: lax.index_in_dim(values, i, axis, keepdims=False)
    return (
        1.0 + first * at(own, 1),
        1.0 + last * at(own, length - 2),
        first * at(high, 1),
    )


def x_bands_kernel(
    heat_ref, conduct_ref, left_ref, right_ref, low_ref, high_ref, kept_ref, gone_ref, ends_ref,
    local_ref, low_block_ref, high_block_ref, zl_ref, zr_ref, zlow_ref, zhigh_ref, zinv_ref, zinner_ref
):
    nz, ny, nx = conduct_ref.shape
    conduct = conduct_ref[...]
    link = link_of(UPWARD_SCALE, conduct[1:], conduct[:-1])
    link = jnp.concatenate([jnp.zeros_like(conduct[:1]), link], 0)
    low, high, inverse, own = reduce_interior(link, 0, zl_ref, zr_ref)
    zlow_ref[...], zhigh_ref[...], zinv_ref[...] = low, high, inverse
    inner = end_bands(link, link[1], link[nz - 1], 0, high, own)
    for i, value in enumerate((*inner, link[1], link[nz - 1])):
        zinner_ref[i] = value
    heat = heat_ref[...]
    local = 2.0 * heat
    across = 2.0 * link_of(UPWARD_SCALE, conduct[1:], conduct[:-1]) * (heat[1:] - heat[:-1])
    nothing = jnp.zeros_like(heat[:1])
    local = local + jnp.concatenate([across, nothing], 0) - jnp.concatenate([nothing, across], 0)
    row = lax.broadcasted_iota(jnp.int32, conduct.shape, 1)
    across = 2.0 * link_of(FLAT_SCALE, conduct, roll(conduct, 1, 1)) * (heat - roll(heat, 1, 1))
    across = jnp.where(row > 0, across, 0.0)
    local = local - across + roll(across, -1, 1)
    local_ref[...] = local
    lines = conduct.reshape(nz * ny, nx).T
    row = lax.broadcasted_iota(jnp.int32, lines.shape, 0)
    link = jnp.where(row > 0, link_of(FLAT_SCALE, lines, roll(lines, 1, 0)), 0.0)
    low, high, own_low, own_high = reduce_lines(link, left_ref, right_ref, kept_ref, gone_ref)
    low_ref[...], high_ref[...] = low, high
    low_block_ref[...] = low.T.reshape(nz, ny, nx)
    high_block_ref[...] = high.T.reshape(nz, ny, nx)
    local = local.reshape(nz * ny, nx).T
    first, last = link[1:2], link[nx - 1 :]
    ends_ref[...] = jnp.concatenate(
        [
            jnp.sum(low * local, 0, keepdims=True),
            jnp.sum(high * local, 0, keepdims=True),
            1.0 + first * own_low,
            1.0 + last * own_high,
            first * high[1:2],
            lines[:1],
            lines[nx - 1 :],
            jnp.zeros_like(first),
        ],
        0,
    )


def x_message_kernel(
    halo_counts, heat_ref, conduct_ref, edge_ref, low_ref, high_ref, ends_ref, zinner_ref, *refs
):
    z_halo, y_halo = split_halos(halo_counts, refs)
    message_ref, z_flow_ref, y_flow_ref, zends_ref = refs[sum(halo_counts) :]
    nz, ny, nx = conduct_ref.shape
    lanes = nz * ny
    index_z, index_y = lax.axis_index("gz"), lax.axis_index("gy")
    below, above = pick_halo("gz", z_halo, index_z % 2 == 1)
    ground = jnp.where(index_z == 0, UPWARD_SCALE * conduct_ref[0] * edge_ref[...], 0.0)
    outer = link_of(UPWARD_SCALE, conduct_ref[0], below[1])
    z_flow_ref[0] = 2.0 * (outer * (below[0] - heat_ref[0]) - ground * heat_ref[0])
    own_first, own_last, between = zinner_ref[0] + ground, zinner_ref[1], zinner_ref[2]
    inverse = 1.0 / (own_first + between + outer)
    for i, value in enumerate((outer, between, inverse, zinner_ref[3], zinner_ref[4])):
        zends_ref[i] = value
    flow = link_of(UPWARD_SCALE, conduct_ref[nz - 1], above[1]) * (above[0] - heat_ref[nz - 1])
    z_flow_ref[1] = 2.0 * flow
    below, above = pick_halo("gy", y_halo, index_y % 2 == 1)
    flow = link_of(FLAT_SCALE, conduct_ref[:, 0, :], below[1]) * (below[0] - heat_ref[:, 0, :])
    y_flow_ref[0] = 2.0 * flow
    flow = link_of(FLAT_SCALE, conduct_ref[:, ny - 1, :], above[1])
    y_flow_ref[1] = 2.0 * flow * (above[0] - heat_ref[:, ny - 1, :])

    def spread(values, first, step):
        shape = (values.shape[0], lanes)
        row = lax.broadcasted_iota(jnp.int32, shape, 0)
        lane = lax.broadcasted_iota(jnp.int32, shape, 1)
        return jnp.where(lane == first + step * row, jnp.sum(values, 1, keepdims=True), 0.0)

    sums = []
    for share in (low_ref, high_ref):
        layers = spread(share[0] * z_flow_ref[0], 0, 1)
        layers = layers + spread(share[nz - 1] * z_flow_ref[1], lanes - ny, 1)
        rows = spread(share[:, 0, :] * y_flow_ref[0], 0, ny)
        rows = rows + spread(share[:, ny - 1, :] * y_flow_ref[1], ny - 1, ny)
        sums.append(jnp.sum(layers, 0, keepdims=True) + jnp.sum(rows, 0, keepdims=True))
    ends = ends_ref[...]
    message_ref[...] = jnp.concatenate([ends[0:1] + sums[0], ends[1:2] + sums[1], ends[2:8]], 0)


def x_source_kernel(
    local_ref, z_flow_ref, y_flow_ref, left_ref, right_ref, kept_ref, gone_ref, part_ref, source_ref
):
    nz, ny, nx = local_ref.shape
    source_ref[...] = local_ref[...]
    source_ref[0] += z_flow_ref[0]
    source_ref[nz - 1] += z_flow_ref[1]
    source_ref[:, 0, :] += y_flow_ref[0]
    source_ref[:, ny - 1, :] += y_flow_ref[1]
    source = source_ref[...].reshape(nz * ny, nx).T
    part_ref[...] = solve_lines(source, left_ref, right_ref, kept_ref, gone_ref)


def y_bands_kernel(halo_count, conduct_ref, *refs):
    y_halo = refs[:halo_count]
    yl_ref, yr_ref, ylow_ref, yhigh_ref, yinv_ref, yends_ref, *y_two_refs = refs[halo_count:]
    nz, ny, nx = conduct_ref.shape
    index_y = lax.axis_index("gy")
    conduct = conduct_ref[...]
    row = lax.broadcasted_iota(jnp.int32, conduct.shape, 1)
    link = jnp.where(row > 0, link_of(FLAT_SCALE, conduct, roll(conduct, 1, 1)), 0.0)
    low, high, inverse, own = reduce_interior(link, 1, yl_ref, yr_ref)
    ylow_ref[...], yhigh_ref[...], yinv_ref[...] = low, high, inverse
    below, above = pick_halo("gy", y_halo, index_y % 2 == 1)
    first = link_of(FLAT_SCALE, conduct_ref[:, 0, :], conduct_ref[:, 1, :])
    last = link_of(FLAT_SCALE, conduct_ref[:, ny - 1, :], conduct_ref[:, ny - 2, :])
    own_first, own_last, between = end_bands(link, first, last, 1, high, own)
    outer_low = link_of(FLAT_SCALE, conduct_ref[:, 0, :], below[1])
    outer_high = link_of(FLAT_SCALE, conduct_ref[:, ny - 1, :], above[1])
    for i, value in enumerate((first, last, own_first, own_last, between, outer_low, outer_high)):
        yends_ref[i] = value
    if y_two_refs:
        ysum_ref, yshare_ref = y_two_refs
        odd = index_y % 2 == 1
        near_own, far_own = jnp.where(odd, own_first, own_last), jnp.where(odd, own_last, own_first)
        share = between / (far_own + between)
        ysum_ref[0] = near_own + share * far_own
        ysum_ref[1] = share
        for k in range(nz):
            near, far = jnp.where(odd, low[k], high[k]), jnp.where(odd, high[k], low[k])
            yshare_ref[k] = near + ysum_ref[1, pl.ds(k, 1), :] * far


def chain_message(ends_ref, source_first, source_last, message_ref):
    own_first, own_last, between, outer = (ends_ref[i] for i in range(2, 6))
    inverse = 1.0 / (own_first + between + outer)
    message_ref[0] = outer * between * inverse
    message_ref[1] = outer * own_first * inverse
    message_ref[2] = outer * inverse * source_first
    message_ref[3] = own_last + between * own_first * inverse
    message_ref[4] = source_last + between * inverse * source_first


def chain_ends(name, messages, ends_ref, source_first, blocks_ref, state_ref):
    count, index = lax.axis_size(name), lax.axis_index(name)
    for shift, message in enumerate(messages):
        blocks_ref[lax.rem(index - shift + count, count)] = message[...]
    blocks = [tuple(blocks_ref[k, i] for i in range(5)) for k in range(count)]
    below, last = chain(blocks, count, index, state_ref)
    own_first, between, outer = ends_ref[2], ends_ref[4], ends_ref[5]
    first = (source_first + outer * below + between * last) / (own_first + between + outer)
    return first, last


def y_message_kernel(
    count_x, count_y, heat_ref, part_ref, low_ref, high_ref, yends_ref, *refs
):
    messages, refs = refs[:count_x], refs[count_x:]
    shares, refs = (refs[:2], refs[2:]) if count_y > 2 else (refs[:1], refs[1:])
    sums_ref, refs = (None, refs) if count_y > 2 else (refs[0], refs[1:])
    source_ref, message_ref, blocks_ref, rows_ref, state_ref = refs
    nz, ny, nx = heat_ref.shape
    index = lax.axis_index("gx") // 2
    for shift, message in enumerate(messages):
        blocks_ref[lax.rem(index - shift + count_x, count_x)] = message[...]
    first, last, own_first, own_last, between, c_first, c_last = (
        blocks_ref[:, i, :] for i in range(7)
    )
    before = jnp.zeros_like(c_last[:1])
    if count_x > 1:
        before = jnp.concatenate([before, c_last[:-1]], 0)
    outer = link_of(FLAT_SCALE, c_first, before)
    inverse = 1.0 / (own_first + between + outer)
    rows = (
        outer * between * inverse,
        outer * own_first * inverse,
        outer * inverse * first,
        own_last + between * own_first * inverse,
        last + between * inverse * first,
        first * inverse,
        outer * inverse,
        between * inverse,
    )
    for i, value in enumerate(rows):
        rows_ref[i] = value
    whole = lambda i, k: jnp.broadcast_to(rows_ref[i, pl.ds(k, 1), :], (8, rows_ref.shape[2]))
    blocks = [tuple(whole(i, k) for i in range(5)) for k in range(count_x)]
    below, last = chain(blocks, count_x, index, state_ref)
    first = whole(5, index) + whole(6, index) * below + whole(7, index) * last
    lines = part_ref[...] + low_ref[...] * first[:1] + high_ref[...] * last[:1]
    source = lines.T.reshape(nz, ny, nx) - 2.0 * heat_ref[...]
    source_ref[...] = source
    sums = [jnp.sum(share[...] * source, 1) for share in shares]
    if count_y > 2:
        chain_message(yends_ref, *sums, message_ref)
    else:
        message_ref[0], message_ref[1] = sums_ref[0], sums[0]


def y_source_kernel(
    heat_ref, source_ref, yl_ref, yr_ref, yinv_ref, yends_ref, ypart_ref, ysource_ref, spare_ref,
    heat_out_ref
):
    spare_ref[...] = jnp.zeros_like(spare_ref)
    heat_out_ref[...] = heat_ref[...]
    ny = source_ref.shape[1]
    part = reduce_source(source_ref[...], 1, yl_ref, yr_ref, yinv_ref[...])
    ypart_ref[...] = part
    ysource_ref[0] = source_ref[:, 0, :] + yends_ref[0] * ypart_ref[:, 1, :]
    ysource_ref[1] = source_ref[:, ny - 1, :] + yends_ref[1] * ypart_ref[:, ny - 2, :]


def z_message_kernel(
    count_y, ypart_ref, ylow_ref, yhigh_ref, yends_ref, ysource_ref, zlow_ref, zhigh_ref,
    zends_ref, *refs
):
    messages, refs = refs[:count_y], refs[count_y:]
    source_ref, small_ref, message_ref, ends_ref, *state = refs
    nz, ny, nx = ypart_ref.shape
    if count_y > 2:
        first, last = chain_ends("gy", messages, yends_ref, ysource_ref[0], *state)
    else:
        odd = lax.axis_index("gy") % 2 == 1
        mine, other = messages
        outer = jnp.where(odd, yends_ref[5], yends_ref[6])
        between = yends_ref[4]
        factor = outer / (other[0] + outer)
        near = (mine[1] + factor * other[1]) / (mine[0] + factor * other[0])
        far_own = jnp.where(odd, yends_ref[3], yends_ref[2])
        far_source = jnp.where(odd, ysource_ref[1], ysource_ref[0])
        far = (far_source + between * near) / (far_own + between)
        first, last = jnp.where(odd, near, far), jnp.where(odd, far, near)
    ends_ref[0], ends_ref[1] = first, last
    source_first, source_last = jnp.zeros((ny, nx), F32), jnp.zeros((ny, nx), F32)
    for k in range(nz):
        source = (
            ypart_ref[k]
            + ylow_ref[k] * ends_ref[0, pl.ds(k, 1), :]
            + yhigh_ref[k] * ends_ref[1, pl.ds(k, 1), :]
        )
        source_ref[k] = source
        source_first = source_first + zlow_ref[k] * source
        source_last = source_last + zhigh_ref[k] * source
    outer, between, inverse = (zends_ref[i] for i in range(3))
    for i, value in enumerate(
        (outer, between, inverse, source_first, zends_ref[3], zends_ref[4])
    ):
        small_ref[i] = value
    message_ref[0] = outer * inverse * source_first
    message_ref[1] = source_last + between * inverse * source_first


def z_source_kernel(heat_ref, source_ref, zl_ref, zr_ref, zinv_ref, small_ref, ready_ref):
    nz = source_ref.shape[0]
    inverse = zinv_ref[...]
    ready_ref[0] = heat_ref[...] + reduce_source(source_ref[...], 0, zl_ref, zr_ref, inverse)
    nothing = jnp.zeros_like(small_ref[0])
    low = jnp.stack([nothing, small_ref[4]] + [nothing] * (nz - 2), 0)
    ready_ref[1] = reduce_source(low, 0, zl_ref, zr_ref, inverse)
    ready_ref[1, 0] = jnp.ones_like(nothing)
    high = jnp.stack([nothing] * (nz - 2) + [small_ref[5], nothing], 0)
    ready_ref[2] = reduce_source(high, 0, zl_ref, zr_ref, inverse)
    ready_ref[2, nz - 1] = jnp.ones_like(nothing)


def starting_order(messages, back=False):
    if back:
        return [messages[0], messages[-1], *messages[1:-1]]
    return [messages[0], *messages[2:], messages[1]]


def join_kernel(small_ref, *refs):
    tail_ref, count, index = refs[-1], len(refs) - 1, lax.axis_index("gz")
    messages = [refs[k] for k in starting_order(list(range(count)), True)]
    tail_ref[:4] = small_ref[:4]
    for shift, message in enumerate(messages):
        place = 4 + 2 * lax.rem(index - shift + count, count)
        tail_ref[pl.ds(place, 2)] = message[...]


def finish_kernel(ready_ref, tail_ref, bands_ref, theirs_ref, mine_ref, state_ref):
    count, index = (tail_ref.shape[0] - 4) // 2, lax.axis_index("gz")
    blocks = [
        (bands_ref[3 * k], bands_ref[3 * k + 1], tail_ref[4 + 2 * k], bands_ref[3 * k + 2],
         tail_ref[5 + 2 * k])
        for k in range(count)
    ]
    below, last = chain(blocks, count, index, state_ref)
    outer, between, inverse, source_first = (tail_ref[i] for i in range(4))
    first = (source_first + outer * below + between * last) * inverse
    nx = theirs_ref.shape[-1]
    heated = ready_ref[0] + ready_ref[1] * first + ready_ref[2] * last
    theirs_ref[...], mine_ref[...] = heated[:, :, :nx], heated[:, :, nx:]


def ends_kernel(
    conduct_a_ref, edge_a_ref, label_b_ref, edge_b_ref, table_ref, zl_ref, zr_ref, zinv_ref,
    message_ref, conduct_ref, edge_ref
):
    half = conduct_a_ref.shape[-1]
    conduct_ref[:, :, :half] = conduct_a_ref[...]
    conduct_ref[:, :, half:] = look_up(label_b_ref[...], table_ref)
    edge_ref[:, :half] = edge_a_ref[...].astype(F32)
    edge_ref[:, half:] = edge_b_ref[...].astype(F32)
    conduct = conduct_ref[...]
    nz = conduct.shape[0]
    link = link_of(UPWARD_SCALE, conduct[1:], conduct[:-1])
    link = jnp.concatenate([jnp.zeros_like(conduct[:1]), link], 0)
    _, high, inverse, own = reduce_interior(link, 0, zl_ref, zr_ref)
    zinv_ref[...] = inverse
    own_first, own_last, between = end_bands(link, link[1], link[nz - 1], 0, high, own)
    ground = UPWARD_SCALE * conduct[0] * edge_ref[...]
    own_first = own_first + jnp.where(lax.axis_index("gz") == 0, ground, 0.0)
    for i, value in enumerate((own_first, own_last, between, conduct[0], conduct[nz - 1])):
        message_ref[i] = value


def all_bands_kernel(*refs):
    messages, (bands_ref, blocks_ref) = refs[:-2], refs[-2:]
    count, index = len(messages), lax.axis_index("gz")
    for shift, message in enumerate(messages):
        blocks_ref[lax.rem(index - shift + count, count)] = message[...]
    for k in range(count):
        own_first, own_last, between, first, _ = (blocks_ref[k, i] for i in range(5))
        outer = jnp.zeros_like(first)
        if k > 0:
            outer = link_of(UPWARD_SCALE, first, blocks_ref[k - 1, 4])
        inverse = 1.0 / (own_first + between + outer)
        bands_ref[3 * k] = outer * between * inverse
        bands_ref[3 * k + 1] = outer * own_first * inverse
        bands_ref[3 * k + 2] = own_last + between * own_first * inverse


VMEM = pl.BlockSpec(memory_space=pltpu.VMEM)
HBM = pl.BlockSpec(memory_space=pltpu.HBM)


def call(kernel, outs, operands, scratch=(), specs=None, ops=200_000, vmem=32):
    return pl.pallas_call(
        kernel,
        out_shape=[jax.ShapeDtypeStruct(out, F32) if isinstance(out, tuple) else out for out in outs],
        in_specs=specs or [VMEM] * len(operands),
        out_specs=[VMEM] * len(outs),
        scratch_shapes=[pltpu.VMEM(item, F32) if isinstance(item, tuple) else item for item in scratch],
        compiler_params=pltpu.CompilerParams(vmem_limit_bytes=vmem * 1024 * 1024),
        cost_estimate=pl.CostEstimate(flops=ops, bytes_accessed=ops, transcendentals=0),
    )(*operands)


def neighbour_swaps(name, other, faces):
    count, width = lax.axis_size(name), lax.axis_size(other)
    received = [lax.ppermute(faces[0], name, [(i, i ^ 1) for i in range(count)])]
    if count > 2:
        pairs = []
        for j in range(width):
            for i in range(count):
                at = (j ^ 1, i) if i in (0, count - 1) else (j, ((i + 1) ^ 1) - 1)
                pairs.append(((j, i), at))
        if (other, name) == ("gy", "gz"):
            axes, place = (other, name), lambda at: at[0] * count + at[1]
        else:
            axes, place = (name, other), lambda at: at[1] * width + at[0]
        pairs = [(place(source), place(target)) for source, target in pairs]
        received.append(lax.ppermute(faces[1], axes, pairs))
    return received


def swap_all(name, message, stride=1):
    count = lax.axis_size(name)
    return [message] + [
        lax.ppermute(message, name, [(i, (i + shift) % count) for i in range(count)])
        for shift in range(stride, count, stride)
    ]


def other_core(values):
    count = lax.axis_size("gx")
    return lax.ppermute(values, "gx", [(i, i ^ 1) for i in range(count)])


def chip_step(heat_a, label_a, edge_a, heat_b, conduct_b, edge_b, table):
    nz, ny, half = heat_a.shape
    nx = 2 * half
    block, lines, layer, rows = (nz, ny, nx), (nx, nz * ny), (ny, nx), (nz, nx)
    count_x, count_y, count_z = (lax.axis_size(name) for name in ("gx", "gy", "gz"))
    count_x = count_x // 2
    tiles = (nx // 8, 8, lines[1])
    y_steps, z_steps = (len(steps_of(length)) for length in (ny, nz))

    halo_counts = swaps_along("gz"), swaps_along("gy")
    heat, conduct, edge, *faces = call(
        start_kernel,
        [block, block, layer] + [(2, *layer)] * halo_counts[0] + [(2, *rows)] * halo_counts[1],
        [heat_a, label_a, edge_a, heat_b, conduct_b, edge_b, table],
    )
    z_halo = neighbour_swaps("gz", "gy", faces[: halo_counts[0]])
    y_halo = neighbour_swaps("gy", "gz", faces[halo_counts[0] :])

    (
        x_left, x_right, x_low, x_high, x_kept, x_gone, x_ends, x_local, x_low_block, x_high_block,
        z_left, z_right, z_low, z_high, z_inverse, z_inner,
    ) = call(
        x_bands_kernel,
        [(3, *lines)] * 2 + [lines] * 2 + [(2, *tiles), (3, *tiles), (8, lines[1])] + [block] * 3
        + [(z_steps, *block)] * 2 + [block] * 3 + [(5, *layer)],
        [heat, conduct],
    )
    x_message, z_flow, y_flow, z_ends = call(
        functools.partial(x_message_kernel, halo_counts),
        [(8, lines[1]), (2, *layer), (2, *rows), (5, *layer)],
        [heat, conduct, edge, x_low_block, x_high_block, x_ends, z_inner,
         *join_halos(z_halo, y_halo)],
    )
    x_messages = swap_all("gx", x_message, 2)
    two = count_y == 2
    y_left, y_right, y_low, y_high, y_inverse, y_ends, *y_two = call(
        functools.partial(y_bands_kernel, len(y_halo)),
        [(y_steps, *block)] * 2 + [block] * 3 + [(7, *rows)] + [(2, *rows), block] * two,
        [conduct, *y_halo],
    )
    y_sum, y_share = y_two[:1], y_two[1:]
    (x_part,) = call(
        x_source_kernel,
        [lines],
        [x_local, z_flow, y_flow, x_left, x_right, x_kept, x_gone],
        [block],
    )
    y_rows = 2 if two else 5
    y_source, y_message = call(
        functools.partial(y_message_kernel, count_x, count_y),
        [block, (y_rows, *rows)],
        [heat, x_part, x_low, x_high, y_ends, *x_messages, *(y_share or (y_low, y_high)), *y_sum],
        [(count_x, 8, lines[1]), (8, count_x, lines[1]), (5, count_x, 8, lines[1])],
    )
    y_messages = swap_all("gy", y_message)
    y_part, y_end_sources, spare, heat_out = call(
        y_source_kernel,
        [block, (2, *rows), (bands_rows(count_z, nz), *layer), block],
        [heat, y_source, y_left, y_right, y_inverse, y_ends],
    )
    z_source, z_small, z_message = call(
        functools.partial(z_message_kernel, count_y),
        [block, (6, *layer), (2, *layer)],
        [y_part, y_low, y_high, y_ends, y_end_sources, z_low, z_high, z_ends, *y_messages],
        [(2, *rows)] + ([] if two else [(count_y, y_rows, *rows), (5, count_y, *rows)]),
    )
    return heat_out, spare, z_source, z_left, z_right, z_inverse, z_small, z_message


def bands_rows(count_z, nz):
    return -(-3 * count_z // nz) * nz


def chip_bands(heat_b, label_b, edge_b, heat_a, conduct_a, edge_a, table):
    nz, ny, half = conduct_a.shape
    nx = 2 * half
    block, layer, count_z = (nz, ny, nx), (ny, nx), lax.axis_size("gz")
    z_steps = len(steps_of(nz))
    z_left, z_right, z_inverse, message = call(
        ends_kernel,
        [(z_steps, *block)] * 2 + [block] + [(5, *layer)],
        [conduct_a, edge_a, label_b, edge_b, table],
        [block, layer],
    )
    (bands,) = call(
        all_bands_kernel,
        [(bands_rows(count_z, nz), *layer)],
        swap_all("gz", message),
        [(count_z, 5, *layer)],
    )
    zeros = lambda *shape: jnp.zeros(shape, F32)
    return (
        zeros(*block), bands, zeros(*block), z_left, z_right, z_inverse, zeros(6, *layer),
        zeros(2, *layer),
    )


def z_round(heat, _, z_source, z_left, z_right, z_inverse, z_small, z_message):
    count_z, block, layer = lax.axis_size("gz"), heat.shape, heat.shape[1:]
    messages = swap_all("gz", z_message)
    (ready,) = call(
        z_source_kernel, [(3, *block)], [heat, z_source, z_left, z_right, z_inverse, z_small]
    )
    (tail,) = call(join_kernel, [(4 + 2 * count_z, *layer)], [z_small, *starting_order(messages)])
    return ready, tail


def z_idle(heat, *_):
    count_z, block, layer = lax.axis_size("gz"), heat.shape, heat.shape[1:]
    return jnp.zeros((3, *block), F32), jnp.zeros((4 + 2 * count_z, *layer), F32)


def local(heat, label, table, edge):
    label_a, heat_a, edge_a = (other_core(values) for values in (label, heat, edge))
    entries = table.shape[0]
    own_heat, own_conduct, rows, own_edge = call(
        stage_kernel,
        [heat.shape, heat.shape, (entries, 8, heat.shape[-1]),
         jax.ShapeDtypeStruct(edge.shape, edge.dtype)],
        [heat, label, table, edge],
        [pltpu.VMEM(label.shape, label.dtype), pltpu.SMEM(table.shape, F32),
         pltpu.SemaphoreType.DMA((4,))],
        [HBM] * 4,
        vmem=60,
    )
    second = lax.axis_index("gx") % 2 == 1
    state = lax.cond(
        second, chip_step, chip_bands,
        heat_a, label_a, edge_a, own_heat, own_conduct, own_edge, rows,
    )
    bands = other_core(state[1])
    ready, tail = lax.cond(second, z_round, z_idle, *state)
    theirs, mine = call(
        finish_kernel,
        [heat_a.shape] * 2,
        [ready, tail, bands],
        [(5, lax.axis_size("gz"), *tail.shape[1:])],
    )
    return jnp.where(second, mine, other_core(theirs))


def solution(mesh):
    return jax.shard_map(
        local,
        mesh=mesh,
        in_specs=(P("gz", "gy", "gx"), P("gz", "gy", "gx"), P(), P("gy", "gx")),
        out_specs=P("gz", "gy", "gx"),
        check_vma=False,
    )
```

```python
import functools

import jax
import jax.numpy as jnp
from jax import lax
from jax.experimental import pallas as pl
from jax.experimental.pallas import tpu as pltpu
from jax.sharding import PartitionSpec as P

FLAT_SCALE = 1000.0
UPWARD_SCALE = 200.0
F32 = jnp.float32


def link_of(scale, one, other):
    return scale * one * other / (one + other)


def roll(values, offset, axis):
    if axis == 0 and values.ndim == 3:
        offset = offset % values.shape[0]
        return jnp.concatenate([values[-offset:], values[:-offset]], 0)
    return pltpu.roll(values, offset % values.shape[axis], axis)


def steps_of(length):
    steps, distance = [], 1
    while distance < length - 1:
        steps.append(distance)
        distance *= 2
    return steps


def reduce_interior(link, axis, left_ref, right_ref):
    length = link.shape[axis]
    row = lax.broadcasted_iota(jnp.int32, link.shape, axis)
    low, high, own = link, roll(link, -1, axis), jnp.ones_like(link)
    high = jnp.where(row == length - 1, 0.0, high)
    for step, distance in enumerate(steps_of(length)):
        inverse = 1.0 / (own + low + high)
        open_low, open_high = row > distance, row < length - 1 - distance
        left = jnp.where(open_low, low * roll(inverse, distance, axis), 0.0)
        right = jnp.where(open_high, high * roll(inverse, -distance, axis), 0.0)
        left_ref[step], right_ref[step] = left, right
        own = own + left * roll(own, distance, axis) + right * roll(own, -distance, axis)
        low = jnp.where(open_low, left * roll(low, distance, axis), low)
        high = jnp.where(open_high, right * roll(high, -distance, axis), high)
    inverse = 1.0 / (own + low + high)
    inner = (row > 0) & (row < length - 1)
    share_low = jnp.where(inner, low * inverse, jnp.where(row == 0, 1.0, 0.0))
    share_high = jnp.where(inner, high * inverse, jnp.where(row == 0, 0.0, 1.0))
    return share_low, share_high, jnp.where(inner, inverse, 0.0), own * inverse


def reduce_source(source, axis, left_ref, right_ref, inverse):
    length = source.shape[axis]
    for step, distance in enumerate(steps_of(length)):
        source = (
            source
            + left_ref[step] * roll(source, distance, axis)
            + right_ref[step] * roll(source, -distance, axis)
        )
    return source * inverse


def halvings(count):
    rows, stages = list(range(count)), []
    while len(rows) > 1:
        near = [
            (row, rows[i - 1] if i else None, rows[i + 1] if i + 1 < len(rows) else None)
            for i, row in enumerate(rows)
        ]
        stages.append((near[0::2], near[1::2]))
        rows = rows[0::2]
    return stages


def reduce_lines(link, left_ref, right_ref, kept_ref, gone_ref):
    length = link.shape[0]
    count = length // 8
    row = lax.broadcasted_iota(jnp.int32, link.shape, 0)
    low, high, own = link, roll(link, -1, 0), jnp.ones_like(link)
    for step, distance in enumerate((1, 2, 4)):
        inverse = 1.0 / (own + low + high)
        open_low, open_high = row > distance, row < length - 1 - distance
        left = jnp.where(open_low, low * roll(inverse, distance, 0), 0.0)
        right = jnp.where(open_high, high * roll(inverse, -distance, 0), 0.0)
        left_ref[step], right_ref[step] = left, right
        own = own + left * roll(own, distance, 0) + right * roll(own, -distance, 0)
        low = jnp.where(open_low, left * roll(low, distance, 0), low)
        high = jnp.where(open_high, right * roll(high, -distance, 0), high)
    first, last = row == 0, row == length - 1
    own = jnp.where(first | last, 0.0, own)
    low = jnp.where(first, 1.0, jnp.where(last, 0.0, low))
    high = jnp.where(last, 1.0, jnp.where(first, 0.0, high))
    tiles = lambda values: [values[8 * k : 8 * k + 8] for k in range(count)]
    own, low, high = tiles(own), tiles(low), tiles(high)
    inverse, share_low, share_high, share_own = {}, {}, {}, {}

    def finish(k):
        inverse[k] = 1.0 / (own[k] + low[k] + high[k])
        gone_ref[0, k], gone_ref[1, k] = low[k] * inverse[k], high[k] * inverse[k]
        gone_ref[2, k] = inverse[k]

    slot = 0
    for kept, gone in halvings(count):
        for k, _, _ in gone:
            finish(k)
        for k, below, above in kept:
            new_low, new_high = low[k], high[k]
            if below is not None:
                factor = low[k] * inverse[below]
                kept_ref[0, slot] = factor
                own[k] = own[k] + factor * own[below]
                new_low = factor * low[below]
            if above is not None:
                factor = high[k] * inverse[above]
                kept_ref[1, slot] = factor
                own[k] = own[k] + factor * own[above]
                new_high = factor * high[above]
            low[k], high[k] = new_low, new_high
            slot += 1
    finish(0)
    share_low[0], share_high[0] = low[0] * inverse[0], high[0] * inverse[0]
    share_own[0] = own[0] * inverse[0]
    for _, gone in halvings(count)[::-1]:
        for k, below, above in gone:
            to_low, to_high = low[k] * inverse[k], high[k] * inverse[k]
            share_low[k] = to_low * share_low[below]
            share_high[k] = to_low * share_high[below]
            if above is None:
                share_high[k] = share_high[k] + to_high
                share_own[k] = own[k] * inverse[k] + to_low * share_own[below]
            else:
                share_low[k] = share_low[k] + to_high * share_low[above]
                share_high[k] = share_high[k] + to_high * share_high[above]
    whole = lambda shares: jnp.concatenate([shares[k] for k in range(count)], 0)
    return whole(share_low), whole(share_high), share_own[0][1:2], share_own[count - 1][6:7]


def solve_lines(source, left_ref, right_ref, kept_ref, gone_ref):
    length = source.shape[0]
    count = length // 8
    for step, distance in enumerate((1, 2, 4)):
        source = (
            source
            + left_ref[step] * roll(source, distance, 0)
            + right_ref[step] * roll(source, -distance, 0)
        )
    row = lax.broadcasted_iota(jnp.int32, source.shape, 0)
    source = jnp.where((row == 0) | (row == length - 1), 0.0, source)
    source = [source[8 * k : 8 * k + 8] for k in range(count)]
    slot, stages = 0, halvings(count)
    for kept, _ in stages:
        for k, below, above in kept:
            if below is not None:
                source[k] = source[k] + kept_ref[0, slot] * source[below]
            if above is not None:
                source[k] = source[k] + kept_ref[1, slot] * source[above]
            slot += 1
    solved = {0: source[0] * gone_ref[2, 0]}
    for _, gone in stages[::-1]:
        for k, below, above in gone:
            solved[k] = source[k] * gone_ref[2, k] + gone_ref[0, k] * solved[below]
            if above is not None:
                solved[k] = solved[k] + gone_ref[1, k] * solved[above]
    return jnp.concatenate([solved[k] for k in range(count)], 0)


def chain(blocks, count, index, state):
    own = [blocks[k][3] + (blocks[k + 1][1] if k + 1 < count else 0.0) for k in range(count)]
    source = [blocks[k][4] + (blocks[k + 1][2] if k + 1 < count else 0.0) for k in range(count)]
    shape = own[0].shape
    state[0, 0], state[1, 0] = jnp.ones(shape, F32), jnp.zeros(shape, F32)
    up_own, up_source = own[0], source[0]
    for k in range(1, count):
        state[0, k], state[1, k] = up_own, up_source
        factor = blocks[k][0] / (up_own + blocks[k][0])
        up_own, up_source = own[k] + factor * up_own, source[k] + factor * up_source
    down_own, down_source = own[count - 1], source[count - 1]
    state[2, count - 1], state[3, count - 1] = down_own, down_source
    for k in range(count - 2, -1, -1):
        factor = blocks[k + 1][0] / (down_own + blocks[k + 1][0])
        down_own, down_source = own[k] + factor * down_own, source[k] + factor * down_source
        state[2, k], state[3, k] = down_own, down_source
    for k in range(count):
        state[4, k] = blocks[k][0]
    up_own, up_source, down_own, down_source, link = (state[i, index] for i in range(5))
    inverse = 1.0 / (up_own * down_own + link * (up_own + down_own))
    below = ((down_own + link) * up_source + link * down_source) * inverse
    here = ((up_own + link) * down_source + link * up_source) * inverse
    return below, here


def pick_halo(name, received, odd):
    first = received[0][...]
    second = received[1][...] if len(received) > 1 else jnp.zeros_like(first)
    index, count = lax.axis_index(name), lax.axis_size(name)
    below = jnp.where(odd, first, second)
    above = jnp.where(odd, second, first)
    return jnp.where(index > 0, below, 0.0), jnp.where(index < count - 1, above, 0.0)


def swaps_along(name):
    return min(lax.axis_size(name) - 1, 2)


def look_up(label, table_ref):
    conduct = jnp.broadcast_to(table_ref[0], label.shape)
    for entry in range(1, table_ref.shape[0]):
        conduct = jnp.where(label == entry, table_ref[entry], conduct)
    return conduct


def stage_kernel(
    heat_in, label_in, table_in, edge_in, heat_ref, conduct_ref, table_ref, edge_ref, label_ref,
    entries_ref, sems
):
    copies = [
        pltpu.make_async_copy(source, target, sems.at[i])
        for i, (source, target) in enumerate(
            (
                (table_in, entries_ref), (label_in, label_ref), (heat_in, heat_ref),
                (edge_in, edge_ref),
            )
        )
    ]
    for copy in copies:
        copy.start()
    copies[0].wait()
    for entry in range(table_ref.shape[0]):
        table_ref[entry] = jnp.full(table_ref.shape[1:], entries_ref[entry], F32)
    copies[1].wait()
    conduct_ref[...] = look_up(label_ref[...], table_ref)
    copies[2].wait()
    copies[3].wait()


def join_halos(z_halo, y_halo):
    return [*z_halo[1:], z_halo[0], *y_halo]


def split_halos(counts, refs):
    halos = refs[: sum(counts)]
    return [halos[counts[0] - 1], *halos[: counts[0] - 1]], halos[counts[0] :]


def start_kernel(
    heat_a_ref, label_a_ref, edge_a_ref, heat_b_ref, conduct_b_ref, edge_b_ref, table_ref,
    heat_ref, conduct_ref, edge_ref, *faces
):
    nx = heat_a_ref.shape[-1]
    heat_ref[:, :, :nx], heat_ref[:, :, nx:] = heat_a_ref[...], heat_b_ref[...]
    conduct_ref[:, :, :nx] = look_up(label_a_ref[...], table_ref)
    conduct_ref[:, :, nx:] = conduct_b_ref[...]
    edge_ref[:, :nx] = edge_a_ref[...].astype(F32)
    edge_ref[:, nx:] = edge_b_ref[...].astype(F32)
    z_faces, y_faces = faces[: swaps_along("gz")], faces[swaps_along("gz") :]
    odd_z = lax.axis_index("gz") % 2 == 1
    odd_y = lax.axis_index("gy") % 2 == 1
    for i, ref in enumerate((heat_ref, conduct_ref)):
        low, high = ref[0], ref[ref.shape[0] - 1]
        for face_ref, pick in zip(z_faces, (odd_z, ~odd_z)):
            face_ref[i] = jnp.where(pick, low, high)
        low, high = ref[:, 0, :], ref[:, ref.shape[1] - 1, :]
        for face_ref, pick in zip(y_faces, (odd_y, ~odd_y)):
            face_ref[i] = jnp.where(pick, low, high)


def end_bands(link, first, last, axis, high, own):
    length = high.shape[axis]
    at = lambda values, i: lax.index_in_dim(values, i, axis, keepdims=False)
    return (
        1.0 + first * at(own, 1),
        1.0 + last * at(own, length - 2),
        first * at(high, 1),
    )


def x_bands_kernel(
    heat_ref, conduct_ref, left_ref, right_ref, low_ref, high_ref, kept_ref, gone_ref, ends_ref,
    local_ref, low_block_ref, high_block_ref, zl_ref, zr_ref, zlow_ref, zhigh_ref, zinv_ref, zinner_ref
):
    nz, ny, nx = conduct_ref.shape
    conduct = conduct_ref[...]
    link = link_of(UPWARD_SCALE, conduct[1:], conduct[:-1])
    link = jnp.concatenate([jnp.zeros_like(conduct[:1]), link], 0)
    low, high, inverse, own = reduce_interior(link, 0, zl_ref, zr_ref)
    zlow_ref[...], zhigh_ref[...], zinv_ref[...] = low, high, inverse
    inner = end_bands(link, link[1], link[nz - 1], 0, high, own)
    for i, value in enumerate((*inner, link[1], link[nz - 1])):
        zinner_ref[i] = value
    heat = heat_ref[...]
    local = 2.0 * heat
    across = 2.0 * link_of(UPWARD_SCALE, conduct[1:], conduct[:-1]) * (heat[1:] - heat[:-1])
    nothing = jnp.zeros_like(heat[:1])
    local = local + jnp.concatenate([across, nothing], 0) - jnp.concatenate([nothing, across], 0)
    row = lax.broadcasted_iota(jnp.int32, conduct.shape, 1)
    across = 2.0 * link_of(FLAT_SCALE, conduct, roll(conduct, 1, 1)) * (heat - roll(heat, 1, 1))
    across = jnp.where(row > 0, across, 0.0)
    local = local - across + roll(across, -1, 1)
    local_ref[...] = local
    lines = conduct.reshape(nz * ny, nx).T
    row = lax.broadcasted_iota(jnp.int32, lines.shape, 0)
    link = jnp.where(row > 0, link_of(FLAT_SCALE, lines, roll(lines, 1, 0)), 0.0)
    low, high, own_low, own_high = reduce_lines(link, left_ref, right_ref, kept_ref, gone_ref)
    low_ref[...], high_ref[...] = low, high
    low_block_ref[...] = low.T.reshape(nz, ny, nx)
    high_block_ref[...] = high.T.reshape(nz, ny, nx)
    local = local.reshape(nz * ny, nx).T
    first, last = link[1:2], link[nx - 1 :]
    ends_ref[...] = jnp.concatenate(
        [
            jnp.sum(low * local, 0, keepdims=True),
            jnp.sum(high * local, 0, keepdims=True),
            1.0 + first * own_low,
            1.0 + last * own_high,
            first * high[1:2],
            lines[:1],
            lines[nx - 1 :],
            jnp.zeros_like(first),
        ],
        0,
    )


def x_message_kernel(
    halo_counts, heat_ref, conduct_ref, edge_ref, low_ref, high_ref, ends_ref, zinner_ref, *refs
):
    z_halo, y_halo = split_halos(halo_counts, refs)
    message_ref, z_flow_ref, y_flow_ref, zends_ref = refs[sum(halo_counts) :]
    nz, ny, nx = conduct_ref.shape
    lanes = nz * ny
    index_z, index_y = lax.axis_index("gz"), lax.axis_index("gy")
    below, above = pick_halo("gz", z_halo, index_z % 2 == 1)
    ground = jnp.where(index_z == 0, UPWARD_SCALE * conduct_ref[0] * edge_ref[...], 0.0)
    outer = link_of(UPWARD_SCALE, conduct_ref[0], below[1])
    z_flow_ref[0] = 2.0 * (outer * (below[0] - heat_ref[0]) - ground * heat_ref[0])
    own_first, own_last, between = zinner_ref[0] + ground, zinner_ref[1], zinner_ref[2]
    inverse = 1.0 / (own_first + between + outer)
    for i, value in enumerate((outer, between, inverse, zinner_ref[3], zinner_ref[4])):
        zends_ref[i] = value
    flow = link_of(UPWARD_SCALE, conduct_ref[nz - 1], above[1]) * (above[0] - heat_ref[nz - 1])
    z_flow_ref[1] = 2.0 * flow
    below, above = pick_halo("gy", y_halo, index_y % 2 == 1)
    flow = link_of(FLAT_SCALE, conduct_ref[:, 0, :], below[1]) * (below[0] - heat_ref[:, 0, :])
    y_flow_ref[0] = 2.0 * flow
    flow = link_of(FLAT_SCALE, conduct_ref[:, ny - 1, :], above[1])
    y_flow_ref[1] = 2.0 * flow * (above[0] - heat_ref[:, ny - 1, :])

    def spread(values, first, step):
        shape = (values.shape[0], lanes)
        row = lax.broadcasted_iota(jnp.int32, shape, 0)
        lane = lax.broadcasted_iota(jnp.int32, shape, 1)
        return jnp.where(lane == first + step * row, jnp.sum(values, 1, keepdims=True), 0.0)

    sums = []
    for share in (low_ref, high_ref):
        layers = spread(share[0] * z_flow_ref[0], 0, 1)
        layers = layers + spread(share[nz - 1] * z_flow_ref[1], lanes - ny, 1)
        rows = spread(share[:, 0, :] * y_flow_ref[0], 0, ny)
        rows = rows + spread(share[:, ny - 1, :] * y_flow_ref[1], ny - 1, ny)
        sums.append(jnp.sum(layers, 0, keepdims=True) + jnp.sum(rows, 0, keepdims=True))
    ends = ends_ref[...]
    message_ref[...] = jnp.concatenate([ends[0:1] + sums[0], ends[1:2] + sums[1], ends[2:8]], 0)


def x_source_kernel(
    local_ref, z_flow_ref, y_flow_ref, left_ref, right_ref, kept_ref, gone_ref, part_ref, source_ref
):
    nz, ny, nx = local_ref.shape
    source_ref[...] = local_ref[...]
    source_ref[0] += z_flow_ref[0]
    source_ref[nz - 1] += z_flow_ref[1]
    source_ref[:, 0, :] += y_flow_ref[0]
    source_ref[:, ny - 1, :] += y_flow_ref[1]
    source = source_ref[...].reshape(nz * ny, nx).T
    part_ref[...] = solve_lines(source, left_ref, right_ref, kept_ref, gone_ref)


def y_bands_kernel(halo_count, conduct_ref, *refs):
    y_halo = refs[:halo_count]
    yl_ref, yr_ref, ylow_ref, yhigh_ref, yinv_ref, yends_ref, *y_two_refs = refs[halo_count:]
    nz, ny, nx = conduct_ref.shape
    index_y = lax.axis_index("gy")
    conduct = conduct_ref[...]
    row = lax.broadcasted_iota(jnp.int32, conduct.shape, 1)
    link = jnp.where(row > 0, link_of(FLAT_SCALE, conduct, roll(conduct, 1, 1)), 0.0)
    low, high, inverse, own = reduce_interior(link, 1, yl_ref, yr_ref)
    ylow_ref[...], yhigh_ref[...], yinv_ref[...] = low, high, inverse
    below, above = pick_halo("gy", y_halo, index_y % 2 == 1)
    first = link_of(FLAT_SCALE, conduct_ref[:, 0, :], conduct_ref[:, 1, :])
    last = link_of(FLAT_SCALE, conduct_ref[:, ny - 1, :], conduct_ref[:, ny - 2, :])
    own_first, own_last, between = end_bands(link, first, last, 1, high, own)
    outer_low = link_of(FLAT_SCALE, conduct_ref[:, 0, :], below[1])
    outer_high = link_of(FLAT_SCALE, conduct_ref[:, ny - 1, :], above[1])
    for i, value in enumerate((first, last, own_first, own_last, between, outer_low, outer_high)):
        yends_ref[i] = value
    if y_two_refs:
        ysum_ref, yshare_ref = y_two_refs
        odd = index_y % 2 == 1
        near_own, far_own = jnp.where(odd, own_first, own_last), jnp.where(odd, own_last, own_first)
        share = between / (far_own + between)
        ysum_ref[0] = near_own + share * far_own
        ysum_ref[1] = share
        for k in range(nz):
            near, far = jnp.where(odd, low[k], high[k]), jnp.where(odd, high[k], low[k])
            yshare_ref[k] = near + ysum_ref[1, pl.ds(k, 1), :] * far


def chain_message(ends_ref, source_first, source_last, message_ref):
    own_first, own_last, between, outer = (ends_ref[i] for i in range(2, 6))
    inverse = 1.0 / (own_first + between + outer)
    message_ref[0] = outer * between * inverse
    message_ref[1] = outer * own_first * inverse
    message_ref[2] = outer * inverse * source_first
    message_ref[3] = own_last + between * own_first * inverse
    message_ref[4] = source_last + between * inverse * source_first


def chain_ends(name, messages, ends_ref, source_first, blocks_ref, state_ref):
    count, index = lax.axis_size(name), lax.axis_index(name)
    for shift, message in enumerate(messages):
        blocks_ref[lax.rem(index - shift + count, count)] = message[...]
    blocks = [tuple(blocks_ref[k, i] for i in range(5)) for k in range(count)]
    below, last = chain(blocks, count, index, state_ref)
    own_first, between, outer = ends_ref[2], ends_ref[4], ends_ref[5]
    first = (source_first + outer * below + between * last) / (own_first + between + outer)
    return first, last


def y_message_kernel(
    count_x, count_y, heat_ref, part_ref, low_ref, high_ref, yends_ref, *refs
):
    messages, refs = refs[:count_x], refs[count_x:]
    shares, refs = (refs[:2], refs[2:]) if count_y > 2 else (refs[:1], refs[1:])
    sums_ref, refs = (None, refs) if count_y > 2 else (refs[0], refs[1:])
    source_ref, message_ref, blocks_ref, rows_ref, state_ref = refs
    nz, ny, nx = heat_ref.shape
    index = lax.axis_index("gx") // 2
    for shift, message in enumerate(messages):
        blocks_ref[lax.rem(index - shift + count_x, count_x)] = message[...]
    first, last, own_first, own_last, between, c_first, c_last = (
        blocks_ref[:, i, :] for i in range(7)
    )
    before = jnp.zeros_like(c_last[:1])
    if count_x > 1:
        before = jnp.concatenate([before, c_last[:-1]], 0)
    outer = link_of(FLAT_SCALE, c_first, before)
    inverse = 1.0 / (own_first + between + outer)
    rows = (
        outer * between * inverse,
        outer * own_first * inverse,
        outer * inverse * first,
        own_last + between * own_first * inverse,
        last + between * inverse * first,
        first * inverse,
        outer * inverse,
        between * inverse,
    )
    for i, value in enumerate(rows):
        rows_ref[i] = value
    whole = lambda i, k: jnp.broadcast_to(rows_ref[i, pl.ds(k, 1), :], (8, rows_ref.shape[2]))
    blocks = [tuple(whole(i, k) for i in range(5)) for k in range(count_x)]
    below, last = chain(blocks, count_x, index, state_ref)
    first = whole(5, index) + whole(6, index) * below + whole(7, index) * last
    lines = part_ref[...] + low_ref[...] * first[:1] + high_ref[...] * last[:1]
    source = lines.T.reshape(nz, ny, nx) - 2.0 * heat_ref[...]
    source_ref[...] = source
    sums = [jnp.sum(share[...] * source, 1) for share in shares]
    if count_y > 2:
        chain_message(yends_ref, *sums, message_ref)
    else:
        message_ref[0], message_ref[1] = sums_ref[0], sums[0]


def y_source_kernel(
    heat_ref, source_ref, yl_ref, yr_ref, yinv_ref, yends_ref, ypart_ref, ysource_ref, spare_ref,
    heat_out_ref
):
    spare_ref[...] = jnp.zeros_like(spare_ref)
    heat_out_ref[...] = heat_ref[...]
    ny = source_ref.shape[1]
    part = reduce_source(source_ref[...], 1, yl_ref, yr_ref, yinv_ref[...])
    ypart_ref[...] = part
    ysource_ref[0] = source_ref[:, 0, :] + yends_ref[0] * ypart_ref[:, 1, :]
    ysource_ref[1] = source_ref[:, ny - 1, :] + yends_ref[1] * ypart_ref[:, ny - 2, :]


def z_message_kernel(
    count_y, ypart_ref, ylow_ref, yhigh_ref, yends_ref, ysource_ref, zlow_ref, zhigh_ref,
    zends_ref, *refs
):
    messages, refs = refs[:count_y], refs[count_y:]
    source_ref, small_ref, message_ref, ends_ref, *state = refs
    nz, ny, nx = ypart_ref.shape
    if count_y > 2:
        first, last = chain_ends("gy", messages, yends_ref, ysource_ref[0], *state)
    else:
        odd = lax.axis_index("gy") % 2 == 1
        mine, other = messages
        outer = jnp.where(odd, yends_ref[5], yends_ref[6])
        between = yends_ref[4]
        factor = outer / (other[0] + outer)
        near = (mine[1] + factor * other[1]) / (mine[0] + factor * other[0])
        far_own = jnp.where(odd, yends_ref[3], yends_ref[2])
        far_source = jnp.where(odd, ysource_ref[1], ysource_ref[0])
        far = (far_source + between * near) / (far_own + between)
        first, last = jnp.where(odd, near, far), jnp.where(odd, far, near)
    ends_ref[0], ends_ref[1] = first, last
    source_first, source_last = jnp.zeros((ny, nx), F32), jnp.zeros((ny, nx), F32)
    for k in range(nz):
        source = (
            ypart_ref[k]
            + ylow_ref[k] * ends_ref[0, pl.ds(k, 1), :]
            + yhigh_ref[k] * ends_ref[1, pl.ds(k, 1), :]
        )
        source_ref[k] = source
        source_first = source_first + zlow_ref[k] * source
        source_last = source_last + zhigh_ref[k] * source
    outer, between, inverse = (zends_ref[i] for i in range(3))
    for i, value in enumerate(
        (outer, between, inverse, source_first, zends_ref[3], zends_ref[4])
    ):
        small_ref[i] = value
    message_ref[0] = outer * inverse * source_first
    message_ref[1] = source_last + between * inverse * source_first


def z_source_kernel(heat_ref, source_ref, zl_ref, zr_ref, zinv_ref, small_ref, ready_ref):
    nz = source_ref.shape[0]
    inverse = zinv_ref[...]
    ready_ref[0] = heat_ref[...] + reduce_source(source_ref[...], 0, zl_ref, zr_ref, inverse)
    nothing = jnp.zeros_like(small_ref[0])
    low = jnp.stack([nothing, small_ref[4]] + [nothing] * (nz - 2), 0)
    ready_ref[1] = reduce_source(low, 0, zl_ref, zr_ref, inverse)
    ready_ref[1, 0] = jnp.ones_like(nothing)
    high = jnp.stack([nothing] * (nz - 2) + [small_ref[5], nothing], 0)
    ready_ref[2] = reduce_source(high, 0, zl_ref, zr_ref, inverse)
    ready_ref[2, nz - 1] = jnp.ones_like(nothing)


def starting_order(messages, back=False):
    if back:
        return [messages[0], messages[-1], *messages[1:-1]]
    return [messages[0], *messages[2:], messages[1]]


def join_kernel(small_ref, *refs):
    tail_ref, count, index = refs[-1], len(refs) - 1, lax.axis_index("gz")
    messages = [refs[k] for k in starting_order(list(range(count)), True)]
    tail_ref[:4] = small_ref[:4]
    for shift, message in enumerate(messages):
        place = 4 + 2 * lax.rem(index - shift + count, count)
        tail_ref[pl.ds(place, 2)] = message[...]


def finish_kernel(ready_ref, tail_ref, bands_ref, theirs_ref, mine_ref, state_ref):
    count, index = (tail_ref.shape[0] - 4) // 2, lax.axis_index("gz")
    blocks = [
        (bands_ref[3 * k], bands_ref[3 * k + 1], tail_ref[4 + 2 * k], bands_ref[3 * k + 2],
         tail_ref[5 + 2 * k])
        for k in range(count)
    ]
    below, last = chain(blocks, count, index, state_ref)
    outer, between, inverse, source_first = (tail_ref[i] for i in range(4))
    first = (source_first + outer * below + between * last) * inverse
    nx = theirs_ref.shape[-1]
    heated = ready_ref[0] + ready_ref[1] * first + ready_ref[2] * last
    theirs_ref[...], mine_ref[...] = heated[:, :, :nx], heated[:, :, nx:]


def ends_kernel(
    conduct_a_ref, edge_a_ref, label_b_ref, edge_b_ref, table_ref, zl_ref, zr_ref, zinv_ref,
    message_ref, conduct_ref, edge_ref
):
    half = conduct_a_ref.shape[-1]
    conduct_ref[:, :, :half] = conduct_a_ref[...]
    conduct_ref[:, :, half:] = look_up(label_b_ref[...], table_ref)
    edge_ref[:, :half] = edge_a_ref[...].astype(F32)
    edge_ref[:, half:] = edge_b_ref[...].astype(F32)
    conduct = conduct_ref[...]
    nz = conduct.shape[0]
    link = link_of(UPWARD_SCALE, conduct[1:], conduct[:-1])
    link = jnp.concatenate([jnp.zeros_like(conduct[:1]), link], 0)
    _, high, inverse, own = reduce_interior(link, 0, zl_ref, zr_ref)
    zinv_ref[...] = inverse
    own_first, own_last, between = end_bands(link, link[1], link[nz - 1], 0, high, own)
    ground = UPWARD_SCALE * conduct[0] * edge_ref[...]
    own_first = own_first + jnp.where(lax.axis_index("gz") == 0, ground, 0.0)
    for i, value in enumerate((own_first, own_last, between, conduct[0], conduct[nz - 1])):
        message_ref[i] = value


def all_bands_kernel(*refs):
    messages, (bands_ref, blocks_ref) = refs[:-2][::-1], refs[-2:]
    count, index = len(messages), lax.axis_index("gz")
    for shift, message in enumerate(messages):
        blocks_ref[lax.rem(index - shift + count, count)] = message[...]
    for k in range(count):
        own_first, own_last, between, first, _ = (blocks_ref[k, i] for i in range(5))
        outer = jnp.zeros_like(first)
        if k > 0:
            outer = link_of(UPWARD_SCALE, first, blocks_ref[k - 1, 4])
        inverse = 1.0 / (own_first + between + outer)
        bands_ref[3 * k] = outer * between * inverse
        bands_ref[3 * k + 1] = outer * own_first * inverse
        bands_ref[3 * k + 2] = own_last + between * own_first * inverse


VMEM = pl.BlockSpec(memory_space=pltpu.VMEM)
HBM = pl.BlockSpec(memory_space=pltpu.HBM)


def call(kernel, outs, operands, scratch=(), specs=None, ops=200_000, vmem=32):
    return pl.pallas_call(
        kernel,
        out_shape=[jax.ShapeDtypeStruct(out, F32) if isinstance(out, tuple) else out for out in outs],
        in_specs=specs or [VMEM] * len(operands),
        out_specs=[VMEM] * len(outs),
        scratch_shapes=[pltpu.VMEM(item, F32) if isinstance(item, tuple) else item for item in scratch],
        compiler_params=pltpu.CompilerParams(vmem_limit_bytes=vmem * 1024 * 1024),
        cost_estimate=pl.CostEstimate(flops=ops, bytes_accessed=ops, transcendentals=0),
    )(*operands)


def neighbour_swaps(name, other, faces):
    count, width = lax.axis_size(name), lax.axis_size(other)
    received = [lax.ppermute(faces[0], name, [(i, i ^ 1) for i in range(count)])]
    if count > 2:
        pairs = []
        for j in range(width):
            for i in range(count):
                at = (j ^ 1, i) if i in (0, count - 1) else (j, ((i + 1) ^ 1) - 1)
                pairs.append(((j, i), at))
        if (other, name) == ("gy", "gz"):
            axes, place = (other, name), lambda at: at[0] * count + at[1]
        else:
            axes, place = (name, other), lambda at: at[1] * width + at[0]
        pairs = [(place(source), place(target)) for source, target in pairs]
        received.append(lax.ppermute(faces[1], axes, pairs))
    return received


def swap_all(name, message, stride=1):
    count = lax.axis_size(name)
    return [message] + [
        lax.ppermute(message, name, [(i, (i + shift) % count) for i in range(count)])
        for shift in range(stride, count, stride)
    ]


def other_core(values):
    count = lax.axis_size("gx")
    return lax.ppermute(values, "gx", [(i, i ^ 1) for i in range(count)])


def chip_step(heat_a, label_a, edge_a, heat_b, conduct_b, edge_b, table):
    nz, ny, half = heat_a.shape
    nx = 2 * half
    block, lines, layer, rows = (nz, ny, nx), (nx, nz * ny), (ny, nx), (nz, nx)
    count_x, count_y, count_z = (lax.axis_size(name) for name in ("gx", "gy", "gz"))
    count_x = count_x // 2
    tiles = (nx // 8, 8, lines[1])
    y_steps, z_steps = (len(steps_of(length)) for length in (ny, nz))

    halo_counts = swaps_along("gz"), swaps_along("gy")
    heat, conduct, edge, *faces = call(
        start_kernel,
        [block, block, layer] + [(2, *layer)] * halo_counts[0] + [(2, *rows)] * halo_counts[1],
        [heat_a, label_a, edge_a, heat_b, conduct_b, edge_b, table],
    )
    z_halo = neighbour_swaps("gz", "gy", faces[: halo_counts[0]])
    y_halo = neighbour_swaps("gy", "gz", faces[halo_counts[0] :])

    (
        x_left, x_right, x_low, x_high, x_kept, x_gone, x_ends, x_local, x_low_block, x_high_block,
        z_left, z_right, z_low, z_high, z_inverse, z_inner,
    ) = call(
        x_bands_kernel,
        [(3, *lines)] * 2 + [lines] * 2 + [(2, *tiles), (3, *tiles), (8, lines[1])] + [block] * 3
        + [(z_steps, *block)] * 2 + [block] * 3 + [(5, *layer)],
        [heat, conduct],
    )
    x_message, z_flow, y_flow, z_ends = call(
        functools.partial(x_message_kernel, halo_counts),
        [(8, lines[1]), (2, *layer), (2, *rows), (5, *layer)],
        [heat, conduct, edge, x_low_block, x_high_block, x_ends, z_inner,
         *join_halos(z_halo, y_halo)],
    )
    x_messages = swap_all("gx", x_message, 2)
    two = count_y == 2
    y_left, y_right, y_low, y_high, y_inverse, y_ends, *y_two = call(
        functools.partial(y_bands_kernel, len(y_halo)),
        [(y_steps, *block)] * 2 + [block] * 3 + [(7, *rows)] + [(2, *rows), block] * two,
        [conduct, *y_halo],
    )
    y_sum, y_share = y_two[:1], y_two[1:]
    (x_part,) = call(
        x_source_kernel,
        [lines],
        [x_local, z_flow, y_flow, x_left, x_right, x_kept, x_gone],
        [block],
    )
    y_rows = 2 if two else 5
    y_source, y_message = call(
        functools.partial(y_message_kernel, count_x, count_y),
        [block, (y_rows, *rows)],
        [heat, x_part, x_low, x_high, y_ends, *x_messages, *(y_share or (y_low, y_high)), *y_sum],
        [(count_x, 8, lines[1]), (8, count_x, lines[1]), (5, count_x, 8, lines[1])],
    )
    y_messages = swap_all("gy", y_message)
    y_part, y_end_sources, spare, heat_out = call(
        y_source_kernel,
        [block, (2, *rows), (bands_rows(count_z, nz), *layer), block],
        [heat, y_source, y_left, y_right, y_inverse, y_ends],
    )
    z_source, z_small, z_message = call(
        functools.partial(z_message_kernel, count_y),
        [block, (6, *layer), (2, *layer)],
        [y_part, y_low, y_high, y_ends, y_end_sources, z_low, z_high, z_ends, *y_messages],
        [(2, *rows)] + ([] if two else [(count_y, y_rows, *rows), (5, count_y, *rows)]),
    )
    return heat_out, spare, z_source, z_left, z_right, z_inverse, z_small, z_message


def bands_rows(count_z, nz):
    return -(-3 * count_z // nz) * nz


def chip_bands(heat_b, label_b, edge_b, heat_a, conduct_a, edge_a, table):
    nz, ny, half = conduct_a.shape
    nx = 2 * half
    block, layer, count_z = (nz, ny, nx), (ny, nx), lax.axis_size("gz")
    z_steps = len(steps_of(nz))
    z_left, z_right, z_inverse, message = call(
        ends_kernel,
        [(z_steps, *block)] * 2 + [block] + [(5, *layer)],
        [conduct_a, edge_a, label_b, edge_b, table],
        [block, layer],
    )
    (bands,) = call(
        all_bands_kernel,
        [(bands_rows(count_z, nz), *layer)],
        swap_all("gz", message)[::-1],
        [(count_z, 5, *layer)],
    )
    zeros = lambda *shape: jnp.zeros(shape, F32)
    return (
        zeros(*block), bands, zeros(*block), z_left, z_right, z_inverse, zeros(6, *layer),
        zeros(2, *layer),
    )


def z_round(heat, _, z_source, z_left, z_right, z_inverse, z_small, z_message):
    count_z, block, layer = lax.axis_size("gz"), heat.shape, heat.shape[1:]
    messages = swap_all("gz", z_message)
    (ready,) = call(
        z_source_kernel, [(3, *block)], [heat, z_source, z_left, z_right, z_inverse, z_small]
    )
    (tail,) = call(join_kernel, [(4 + 2 * count_z, *layer)], [z_small, *starting_order(messages)])
    return ready, tail


def z_idle(heat, *_):
    count_z, block, layer = lax.axis_size("gz"), heat.shape, heat.shape[1:]
    return jnp.zeros((3, *block), F32), jnp.zeros((4 + 2 * count_z, *layer), F32)


def local(heat, label, table, edge):
    label_a, heat_a, edge_a = (other_core(values) for values in (label, heat, edge))
    entries = table.shape[0]
    own_heat, own_conduct, rows, own_edge = call(
        stage_kernel,
        [heat.shape, heat.shape, (entries, 8, heat.shape[-1]),
         jax.ShapeDtypeStruct(edge.shape, edge.dtype)],
        [heat, label, table, edge],
        [pltpu.VMEM(label.shape, label.dtype), pltpu.SMEM(table.shape, F32),
         pltpu.SemaphoreType.DMA((4,))],
        [HBM] * 4,
        vmem=60,
    )
    second = lax.axis_index("gx") % 2 == 1
    state = lax.cond(
        second, chip_step, chip_bands,
        heat_a, label_a, edge_a, own_heat, own_conduct, own_edge, rows,
    )
    bands = other_core(state[1])
    ready, tail = lax.cond(second, z_round, z_idle, *state)
    theirs, mine = call(
        finish_kernel,
        [heat_a.shape] * 2,
        [ready, tail, bands],
        [(5, lax.axis_size("gz"), *tail.shape[1:])],
    )
    return jnp.where(second, mine, other_core(theirs))


def solution(mesh):
    return jax.shard_map(
        local,
        mesh=mesh,
        in_specs=(P("gz", "gy", "gx"), P("gz", "gy", "gx"), P(), P("gy", "gx")),
        out_specs=P("gz", "gy", "gx"),
        check_vma=False,
    )
```

```python
import functools

import jax
import jax.numpy as jnp
from jax import lax
from jax.experimental import pallas as pl
from jax.experimental.pallas import tpu as pltpu
from jax.sharding import PartitionSpec as P

FLAT_SCALE = 1000.0
UPWARD_SCALE = 200.0
F32 = jnp.float32


def link_of(scale, one, other):
    return scale * one * other / (one + other)


def roll(values, offset, axis):
    if axis == 0 and values.ndim == 3:
        offset = offset % values.shape[0]
        return jnp.concatenate([values[-offset:], values[:-offset]], 0)
    return pltpu.roll(values, offset % values.shape[axis], axis)


def steps_of(length):
    steps, distance = [], 1
    while distance < length - 1:
        steps.append(distance)
        distance *= 2
    return steps


def reduce_interior(link, axis, left_ref, right_ref):
    length = link.shape[axis]
    row = lax.broadcasted_iota(jnp.int32, link.shape, axis)
    low, high, own = link, roll(link, -1, axis), jnp.ones_like(link)
    high = jnp.where(row == length - 1, 0.0, high)
    for step, distance in enumerate(steps_of(length)):
        inverse = 1.0 / (own + low + high)
        open_low, open_high = row > distance, row < length - 1 - distance
        left = jnp.where(open_low, low * roll(inverse, distance, axis), 0.0)
        right = jnp.where(open_high, high * roll(inverse, -distance, axis), 0.0)
        left_ref[step], right_ref[step] = left, right
        own = own + left * roll(own, distance, axis) + right * roll(own, -distance, axis)
        low = jnp.where(open_low, left * roll(low, distance, axis), low)
        high = jnp.where(open_high, right * roll(high, -distance, axis), high)
    inverse = 1.0 / (own + low + high)
    inner = (row > 0) & (row < length - 1)
    share_low = jnp.where(inner, low * inverse, jnp.where(row == 0, 1.0, 0.0))
    share_high = jnp.where(inner, high * inverse, jnp.where(row == 0, 0.0, 1.0))
    return share_low, share_high, jnp.where(inner, inverse, 0.0), own * inverse


def reduce_source(source, axis, left_ref, right_ref, inverse):
    length = source.shape[axis]
    for step, distance in enumerate(steps_of(length)):
        source = (
            source
            + left_ref[step] * roll(source, distance, axis)
            + right_ref[step] * roll(source, -distance, axis)
        )
    return source * inverse


def halvings(count):
    rows, stages = list(range(count)), []
    while len(rows) > 1:
        near = [
            (row, rows[i - 1] if i else None, rows[i + 1] if i + 1 < len(rows) else None)
            for i, row in enumerate(rows)
        ]
        stages.append((near[0::2], near[1::2]))
        rows = rows[0::2]
    return stages


def reduce_lines(link, left_ref, right_ref, kept_ref, gone_ref):
    length = link.shape[0]
    count = length // 8
    row = lax.broadcasted_iota(jnp.int32, link.shape, 0)
    low, high, own = link, roll(link, -1, 0), jnp.ones_like(link)
    for step, distance in enumerate((1, 2, 4)):
        inverse = 1.0 / (own + low + high)
        open_low, open_high = row > distance, row < length - 1 - distance
        left = jnp.where(open_low, low * roll(inverse, distance, 0), 0.0)
        right = jnp.where(open_high, high * roll(inverse, -distance, 0), 0.0)
        left_ref[step], right_ref[step] = left, right
        own = own + left * roll(own, distance, 0) + right * roll(own, -distance, 0)
        low = jnp.where(open_low, left * roll(low, distance, 0), low)
        high = jnp.where(open_high, right * roll(high, -distance, 0), high)
    first, last = row == 0, row == length - 1
    own = jnp.where(first | last, 0.0, own)
    low = jnp.where(first, 1.0, jnp.where(last, 0.0, low))
    high = jnp.where(last, 1.0, jnp.where(first, 0.0, high))
    tiles = lambda values: [values[8 * k : 8 * k + 8] for k in range(count)]
    own, low, high = tiles(own), tiles(low), tiles(high)
    inverse, share_low, share_high, share_own = {}, {}, {}, {}

    def finish(k):
        inverse[k] = 1.0 / (own[k] + low[k] + high[k])
        gone_ref[0, k], gone_ref[1, k] = low[k] * inverse[k], high[k] * inverse[k]
        gone_ref[2, k] = inverse[k]

    slot = 0
    for kept, gone in halvings(count):
        for k, _, _ in gone:
            finish(k)
        for k, below, above in kept:
            new_low, new_high = low[k], high[k]
            if below is not None:
                factor = low[k] * inverse[below]
                kept_ref[0, slot] = factor
                own[k] = own[k] + factor * own[below]
                new_low = factor * low[below]
            if above is not None:
                factor = high[k] * inverse[above]
                kept_ref[1, slot] = factor
                own[k] = own[k] + factor * own[above]
                new_high = factor * high[above]
            low[k], high[k] = new_low, new_high
            slot += 1
    finish(0)
    share_low[0], share_high[0] = low[0] * inverse[0], high[0] * inverse[0]
    share_own[0] = own[0] * inverse[0]
    for _, gone in halvings(count)[::-1]:
        for k, below, above in gone:
            to_low, to_high = low[k] * inverse[k], high[k] * inverse[k]
            share_low[k] = to_low * share_low[below]
            share_high[k] = to_low * share_high[below]
            if above is None:
                share_high[k] = share_high[k] + to_high
                share_own[k] = own[k] * inverse[k] + to_low * share_own[below]
            else:
                share_low[k] = share_low[k] + to_high * share_low[above]
                share_high[k] = share_high[k] + to_high * share_high[above]
    whole = lambda shares: jnp.concatenate([shares[k] for k in range(count)], 0)
    return whole(share_low), whole(share_high), share_own[0][1:2], share_own[count - 1][6:7]


def solve_lines(source, left_ref, right_ref, kept_ref, gone_ref):
    length = source.shape[0]
    count = length // 8
    for step, distance in enumerate((1, 2, 4)):
        source = (
            source
            + left_ref[step] * roll(source, distance, 0)
            + right_ref[step] * roll(source, -distance, 0)
        )
    row = lax.broadcasted_iota(jnp.int32, source.shape, 0)
    source = jnp.where((row == 0) | (row == length - 1), 0.0, source)
    source = [source[8 * k : 8 * k + 8] for k in range(count)]
    slot, stages = 0, halvings(count)
    for kept, _ in stages:
        for k, below, above in kept:
            if below is not None:
                source[k] = source[k] + kept_ref[0, slot] * source[below]
            if above is not None:
                source[k] = source[k] + kept_ref[1, slot] * source[above]
            slot += 1
    solved = {0: source[0] * gone_ref[2, 0]}
    for _, gone in stages[::-1]:
        for k, below, above in gone:
            solved[k] = source[k] * gone_ref[2, k] + gone_ref[0, k] * solved[below]
            if above is not None:
                solved[k] = solved[k] + gone_ref[1, k] * solved[above]
    return jnp.concatenate([solved[k] for k in range(count)], 0)


def chain(blocks, count, index, state):
    own = [blocks[k][3] + (blocks[k + 1][1] if k + 1 < count else 0.0) for k in range(count)]
    source = [blocks[k][4] + (blocks[k + 1][2] if k + 1 < count else 0.0) for k in range(count)]
    shape = own[0].shape
    state[0, 0], state[1, 0] = jnp.ones(shape, F32), jnp.zeros(shape, F32)
    up_own, up_source = own[0], source[0]
    for k in range(1, count):
        state[0, k], state[1, k] = up_own, up_source
        factor = blocks[k][0] / (up_own + blocks[k][0])
        up_own, up_source = own[k] + factor * up_own, source[k] + factor * up_source
    down_own, down_source = own[count - 1], source[count - 1]
    state[2, count - 1], state[3, count - 1] = down_own, down_source
    for k in range(count - 2, -1, -1):
        factor = blocks[k + 1][0] / (down_own + blocks[k + 1][0])
        down_own, down_source = own[k] + factor * down_own, source[k] + factor * down_source
        state[2, k], state[3, k] = down_own, down_source
    for k in range(count):
        state[4, k] = blocks[k][0]
    up_own, up_source, down_own, down_source, link = (state[i, index] for i in range(5))
    inverse = 1.0 / (up_own * down_own + link * (up_own + down_own))
    below = ((down_own + link) * up_source + link * down_source) * inverse
    here = ((up_own + link) * down_source + link * up_source) * inverse
    return below, here


def pick_halo(name, received, odd):
    first = received[0][...]
    second = received[1][...] if len(received) > 1 else jnp.zeros_like(first)
    index, count = lax.axis_index(name), lax.axis_size(name)
    below = jnp.where(odd, first, second)
    above = jnp.where(odd, second, first)
    return jnp.where(index > 0, below, 0.0), jnp.where(index < count - 1, above, 0.0)


def swaps_along(name):
    return min(lax.axis_size(name) - 1, 2)


def look_up(label, table_ref):
    conduct = jnp.broadcast_to(table_ref[0], label.shape)
    for entry in range(1, table_ref.shape[0]):
        conduct = jnp.where(label == entry, table_ref[entry], conduct)
    return conduct


def stage_kernel(
    heat_in, label_in, table_in, edge_in, heat_ref, conduct_ref, table_ref, edge_ref, label_ref,
    entries_ref, sems
):
    copies = [
        pltpu.make_async_copy(source, target, sems.at[i])
        for i, (source, target) in enumerate(
            (
                (table_in, entries_ref), (label_in, label_ref), (heat_in, heat_ref),
                (edge_in, edge_ref),
            )
        )
    ]
    for copy in copies:
        copy.start()
    copies[0].wait()
    for entry in range(table_ref.shape[0]):
        table_ref[entry] = jnp.full(table_ref.shape[1:], entries_ref[entry], F32)
    copies[1].wait()
    conduct_ref[...] = look_up(label_ref[...], table_ref)
    copies[2].wait()
    copies[3].wait()


def join_halos(z_halo, y_halo):
    return [*z_halo[1:], z_halo[0], *y_halo]


def split_halos(counts, refs):
    halos = refs[: sum(counts)]
    return [halos[counts[0] - 1], *halos[: counts[0] - 1]], halos[counts[0] :]


def start_kernel(
    heat_a_ref, label_a_ref, edge_a_ref, heat_b_ref, conduct_b_ref, edge_b_ref, table_ref,
    heat_ref, conduct_ref, edge_ref, *faces
):
    nx = heat_a_ref.shape[-1]
    heat_ref[:, :, :nx], heat_ref[:, :, nx:] = heat_a_ref[...], heat_b_ref[...]
    conduct_ref[:, :, :nx] = look_up(label_a_ref[...], table_ref)
    conduct_ref[:, :, nx:] = conduct_b_ref[...]
    edge_ref[:, :nx] = edge_a_ref[...].astype(F32)
    edge_ref[:, nx:] = edge_b_ref[...].astype(F32)
    z_faces, y_faces = faces[: swaps_along("gz")], faces[swaps_along("gz") :]
    odd_z = lax.axis_index("gz") % 2 == 1
    odd_y = lax.axis_index("gy") % 2 == 1
    for i, ref in enumerate((heat_ref, conduct_ref)):
        low, high = ref[0], ref[ref.shape[0] - 1]
        for face_ref, pick in zip(z_faces, (odd_z, ~odd_z)):
            face_ref[i] = jnp.where(pick, low, high)
        low, high = ref[:, 0, :], ref[:, ref.shape[1] - 1, :]
        for face_ref, pick in zip(y_faces, (odd_y, ~odd_y)):
            face_ref[i] = jnp.where(pick, low, high)


def end_bands(link, first, last, axis, high, own):
    length = high.shape[axis]
    at = lambda values, i: lax.index_in_dim(values, i, axis, keepdims=False)
    return (
        1.0 + first * at(own, 1),
        1.0 + last * at(own, length - 2),
        first * at(high, 1),
    )


def x_bands_kernel(
    heat_ref, conduct_ref, left_ref, right_ref, low_ref, high_ref, kept_ref, gone_ref, ends_ref,
    local_ref, low_block_ref, high_block_ref, zl_ref, zr_ref, zlow_ref, zhigh_ref, zinv_ref, zinner_ref
):
    nz, ny, nx = conduct_ref.shape
    conduct = conduct_ref[...]
    link = link_of(UPWARD_SCALE, conduct[1:], conduct[:-1])
    link = jnp.concatenate([jnp.zeros_like(conduct[:1]), link], 0)
    low, high, inverse, own = reduce_interior(link, 0, zl_ref, zr_ref)
    zlow_ref[...], zhigh_ref[...], zinv_ref[...] = low, high, inverse
    inner = end_bands(link, link[1], link[nz - 1], 0, high, own)
    for i, value in enumerate((*inner, link[1], link[nz - 1])):
        zinner_ref[i] = value
    heat = heat_ref[...]
    local = 2.0 * heat
    across = 2.0 * link_of(UPWARD_SCALE, conduct[1:], conduct[:-1]) * (heat[1:] - heat[:-1])
    nothing = jnp.zeros_like(heat[:1])
    local = local + jnp.concatenate([across, nothing], 0) - jnp.concatenate([nothing, across], 0)
    row = lax.broadcasted_iota(jnp.int32, conduct.shape, 1)
    across = 2.0 * link_of(FLAT_SCALE, conduct, roll(conduct, 1, 1)) * (heat - roll(heat, 1, 1))
    across = jnp.where(row > 0, across, 0.0)
    local = local - across + roll(across, -1, 1)
    local_ref[...] = local
    lines = conduct.reshape(nz * ny, nx).T
    row = lax.broadcasted_iota(jnp.int32, lines.shape, 0)
    link = jnp.where(row > 0, link_of(FLAT_SCALE, lines, roll(lines, 1, 0)), 0.0)
    low, high, own_low, own_high = reduce_lines(link, left_ref, right_ref, kept_ref, gone_ref)
    low_ref[...], high_ref[...] = low, high
    low_block_ref[...] = low.T.reshape(nz, ny, nx)
    high_block_ref[...] = high.T.reshape(nz, ny, nx)
    local = local.reshape(nz * ny, nx).T
    first, last = link[1:2], link[nx - 1 :]
    ends_ref[...] = jnp.concatenate(
        [
            jnp.sum(low * local, 0, keepdims=True),
            jnp.sum(high * local, 0, keepdims=True),
            1.0 + first * own_low,
            1.0 + last * own_high,
            first * high[1:2],
            lines[:1],
            lines[nx - 1 :],
            jnp.zeros_like(first),
        ],
        0,
    )


def x_message_kernel(
    halo_counts, heat_ref, conduct_ref, edge_ref, low_ref, high_ref, ends_ref, zinner_ref, *refs
):
    z_halo, y_halo = split_halos(halo_counts, refs)
    message_ref, z_flow_ref, y_flow_ref, zends_ref = refs[sum(halo_counts) :]
    nz, ny, nx = conduct_ref.shape
    lanes = nz * ny
    index_z, index_y = lax.axis_index("gz"), lax.axis_index("gy")
    below, above = pick_halo("gz", z_halo, index_z % 2 == 1)
    ground = jnp.where(index_z == 0, UPWARD_SCALE * conduct_ref[0] * edge_ref[...], 0.0)
    outer = link_of(UPWARD_SCALE, conduct_ref[0], below[1])
    z_flow_ref[0] = 2.0 * (outer * (below[0] - heat_ref[0]) - ground * heat_ref[0])
    own_first, own_last, between = zinner_ref[0] + ground, zinner_ref[1], zinner_ref[2]
    inverse = 1.0 / (own_first + between + outer)
    for i, value in enumerate((outer, between, inverse, zinner_ref[3], zinner_ref[4])):
        zends_ref[i] = value
    flow = link_of(UPWARD_SCALE, conduct_ref[nz - 1], above[1]) * (above[0] - heat_ref[nz - 1])
    z_flow_ref[1] = 2.0 * flow
    odd = index_y % 2 == 1
    near = lambda ref: jnp.where(odd, ref[:, 0, :], ref[:, ny - 1, :])
    if len(y_halo) == 1:
        flow = link_of(FLAT_SCALE, near(conduct_ref), y_halo[0][1])
        flow = 2.0 * flow * (y_halo[0][0] - near(heat_ref))
        y_flow_ref[0] = jnp.where(odd, flow, 0.0)
        y_flow_ref[1] = jnp.where(odd, 0.0, flow)
    else:
        below, above = pick_halo("gy", y_halo, index_y % 2 == 1)
        flow = link_of(FLAT_SCALE, conduct_ref[:, 0, :], below[1]) * (below[0] - heat_ref[:, 0, :])
        y_flow_ref[0] = 2.0 * flow
        flow = link_of(FLAT_SCALE, conduct_ref[:, ny - 1, :], above[1])
        y_flow_ref[1] = 2.0 * flow * (above[0] - heat_ref[:, ny - 1, :])

    def spread(values, first, step):
        shape = (values.shape[0], lanes)
        row = lax.broadcasted_iota(jnp.int32, shape, 0)
        lane = lax.broadcasted_iota(jnp.int32, shape, 1)
        return jnp.where(lane == first + step * row, jnp.sum(values, 1, keepdims=True), 0.0)

    sums = []
    for share in (low_ref, high_ref):
        layers = spread(share[0] * z_flow_ref[0], 0, 1)
        layers = layers + spread(share[nz - 1] * z_flow_ref[1], lanes - ny, 1)
        if len(y_halo) == 1:
            rows = spread(near(share) * flow, jnp.where(odd, 0, ny - 1), ny)
        else:
            rows = spread(share[:, 0, :] * y_flow_ref[0], 0, ny)
            rows = rows + spread(share[:, ny - 1, :] * y_flow_ref[1], ny - 1, ny)
        sums.append(jnp.sum(layers, 0, keepdims=True) + jnp.sum(rows, 0, keepdims=True))
    ends = ends_ref[...]
    message_ref[...] = jnp.concatenate([ends[0:1] + sums[0], ends[1:2] + sums[1], ends[2:8]], 0)


def x_source_kernel(
    local_ref, z_flow_ref, y_flow_ref, left_ref, right_ref, kept_ref, gone_ref, part_ref, source_ref
):
    nz, ny, nx = local_ref.shape
    source_ref[...] = local_ref[...]
    source_ref[0] += z_flow_ref[0]
    source_ref[nz - 1] += z_flow_ref[1]
    source_ref[:, 0, :] += y_flow_ref[0]
    source_ref[:, ny - 1, :] += y_flow_ref[1]
    source = source_ref[...].reshape(nz * ny, nx).T
    part_ref[...] = solve_lines(source, left_ref, right_ref, kept_ref, gone_ref)


def y_bands_kernel(halo_count, conduct_ref, *refs):
    y_halo = refs[:halo_count]
    yl_ref, yr_ref, ylow_ref, yhigh_ref, yinv_ref, yends_ref, *y_two_refs = refs[halo_count:]
    nz, ny, nx = conduct_ref.shape
    index_y = lax.axis_index("gy")
    conduct = conduct_ref[...]
    row = lax.broadcasted_iota(jnp.int32, conduct.shape, 1)
    link = jnp.where(row > 0, link_of(FLAT_SCALE, conduct, roll(conduct, 1, 1)), 0.0)
    low, high, inverse, own = reduce_interior(link, 1, yl_ref, yr_ref)
    ylow_ref[...], yhigh_ref[...], yinv_ref[...] = low, high, inverse
    below, above = pick_halo("gy", y_halo, index_y % 2 == 1)
    first = link_of(FLAT_SCALE, conduct_ref[:, 0, :], conduct_ref[:, 1, :])
    last = link_of(FLAT_SCALE, conduct_ref[:, ny - 1, :], conduct_ref[:, ny - 2, :])
    own_first, own_last, between = end_bands(link, first, last, 1, high, own)
    outer_low = link_of(FLAT_SCALE, conduct_ref[:, 0, :], below[1])
    outer_high = link_of(FLAT_SCALE, conduct_ref[:, ny - 1, :], above[1])
    for i, value in enumerate((first, last, own_first, own_last, between, outer_low, outer_high)):
        yends_ref[i] = value
    if y_two_refs:
        ysum_ref, yshare_ref = y_two_refs
        odd = index_y % 2 == 1
        near_own, far_own = jnp.where(odd, own_first, own_last), jnp.where(odd, own_last, own_first)
        share = between / (far_own + between)
        ysum_ref[0] = near_own + share * far_own
        ysum_ref[1] = share
        for k in range(nz):
            near, far = jnp.where(odd, low[k], high[k]), jnp.where(odd, high[k], low[k])
            yshare_ref[k] = near + ysum_ref[1, pl.ds(k, 1), :] * far


def chain_message(ends_ref, source_first, source_last, message_ref):
    own_first, own_last, between, outer = (ends_ref[i] for i in range(2, 6))
    inverse = 1.0 / (own_first + between + outer)
    message_ref[0] = outer * between * inverse
    message_ref[1] = outer * own_first * inverse
    message_ref[2] = outer * inverse * source_first
    message_ref[3] = own_last + between * own_first * inverse
    message_ref[4] = source_last + between * inverse * source_first


def chain_ends(name, messages, ends_ref, source_first, blocks_ref, state_ref):
    count, index = lax.axis_size(name), lax.axis_index(name)
    for shift, message in enumerate(messages):
        blocks_ref[lax.rem(index - shift + count, count)] = message[...]
    blocks = [tuple(blocks_ref[k, i] for i in range(5)) for k in range(count)]
    below, last = chain(blocks, count, index, state_ref)
    own_first, between, outer = ends_ref[2], ends_ref[4], ends_ref[5]
    first = (source_first + outer * below + between * last) / (own_first + between + outer)
    return first, last


def y_message_kernel(
    count_x, count_y, heat_ref, part_ref, low_ref, high_ref, yends_ref, *refs
):
    messages, refs = refs[:count_x], refs[count_x:]
    shares, refs = (refs[:2], refs[2:]) if count_y > 2 else (refs[:1], refs[1:])
    sums_ref, refs = (None, refs) if count_y > 2 else (refs[0], refs[1:])
    source_ref, message_ref, blocks_ref, rows_ref, state_ref = refs
    nz, ny, nx = heat_ref.shape
    index = lax.axis_index("gx") // 2
    for shift, message in enumerate(messages):
        blocks_ref[lax.rem(index - shift + count_x, count_x)] = message[...]
    first, last, own_first, own_last, between, c_first, c_last = (
        blocks_ref[:, i, :] for i in range(7)
    )
    before = jnp.zeros_like(c_last[:1])
    if count_x > 1:
        before = jnp.concatenate([before, c_last[:-1]], 0)
    outer = link_of(FLAT_SCALE, c_first, before)
    inverse = 1.0 / (own_first + between + outer)
    rows = (
        outer * between * inverse,
        outer * own_first * inverse,
        outer * inverse * first,
        own_last + between * own_first * inverse,
        last + between * inverse * first,
        first * inverse,
        outer * inverse,
        between * inverse,
    )
    for i, value in enumerate(rows):
        rows_ref[i] = value
    whole = lambda i, k: jnp.broadcast_to(rows_ref[i, pl.ds(k, 1), :], (8, rows_ref.shape[2]))
    blocks = [tuple(whole(i, k) for i in range(5)) for k in range(count_x)]
    below, last = chain(blocks, count_x, index, state_ref)
    first = whole(5, index) + whole(6, index) * below + whole(7, index) * last
    lines = part_ref[...] + low_ref[...] * first[:1] + high_ref[...] * last[:1]
    source = lines.T.reshape(nz, ny, nx) - 2.0 * heat_ref[...]
    source_ref[...] = source
    sums = [jnp.sum(share[...] * source, 1) for share in shares]
    if count_y > 2:
        chain_message(yends_ref, *sums, message_ref)
    else:
        message_ref[0], message_ref[1] = sums_ref[0], sums[0]


def y_source_kernel(
    heat_ref, source_ref, yl_ref, yr_ref, yinv_ref, yends_ref, ypart_ref, ysource_ref, spare_ref,
    heat_out_ref
):
    spare_ref[...] = jnp.zeros_like(spare_ref)
    heat_out_ref[...] = heat_ref[...]
    ny = source_ref.shape[1]
    part = reduce_source(source_ref[...], 1, yl_ref, yr_ref, yinv_ref[...])
    ypart_ref[...] = part
    ysource_ref[0] = source_ref[:, 0, :] + yends_ref[0] * ypart_ref[:, 1, :]
    ysource_ref[1] = source_ref[:, ny - 1, :] + yends_ref[1] * ypart_ref[:, ny - 2, :]


def z_message_kernel(
    count_y, ypart_ref, ylow_ref, yhigh_ref, yends_ref, ysource_ref, zlow_ref, zhigh_ref,
    zends_ref, *refs
):
    messages, refs = refs[:count_y], refs[count_y:]
    source_ref, small_ref, message_ref, ends_ref, *state = refs
    nz, ny, nx = ypart_ref.shape
    if count_y > 2:
        first, last = chain_ends("gy", messages, yends_ref, ysource_ref[0], *state)
    else:
        odd = lax.axis_index("gy") % 2 == 1
        mine, other = messages
        outer = jnp.where(odd, yends_ref[5], yends_ref[6])
        between = yends_ref[4]
        factor = outer / (other[0] + outer)
        near = (mine[1] + factor * other[1]) / (mine[0] + factor * other[0])
        far_own = jnp.where(odd, yends_ref[3], yends_ref[2])
        far_source = jnp.where(odd, ysource_ref[1], ysource_ref[0])
        far = (far_source + between * near) / (far_own + between)
        first, last = jnp.where(odd, near, far), jnp.where(odd, far, near)
    ends_ref[0], ends_ref[1] = first, last
    source_first, source_last = jnp.zeros((ny, nx), F32), jnp.zeros((ny, nx), F32)
    for k in range(nz):
        source = (
            ypart_ref[k]
            + ylow_ref[k] * ends_ref[0, pl.ds(k, 1), :]
            + yhigh_ref[k] * ends_ref[1, pl.ds(k, 1), :]
        )
        source_ref[k] = source
        source_first = source_first + zlow_ref[k] * source
        source_last = source_last + zhigh_ref[k] * source
    outer, between, inverse = (zends_ref[i] for i in range(3))
    for i, value in enumerate(
        (outer, between, inverse, source_first, zends_ref[3], zends_ref[4])
    ):
        small_ref[i] = value
    message_ref[0] = outer * inverse * source_first
    message_ref[1] = source_last + between * inverse * source_first


def z_source_kernel(heat_ref, source_ref, zl_ref, zr_ref, zinv_ref, small_ref, ready_ref):
    nz = source_ref.shape[0]
    inverse = zinv_ref[...]
    ready_ref[0] = heat_ref[...] + reduce_source(source_ref[...], 0, zl_ref, zr_ref, inverse)
    nothing = jnp.zeros_like(small_ref[0])
    low = jnp.stack([nothing, small_ref[4]] + [nothing] * (nz - 2), 0)
    ready_ref[1] = reduce_source(low, 0, zl_ref, zr_ref, inverse)
    ready_ref[1, 0] = jnp.ones_like(nothing)
    high = jnp.stack([nothing] * (nz - 2) + [small_ref[5], nothing], 0)
    ready_ref[2] = reduce_source(high, 0, zl_ref, zr_ref, inverse)
    ready_ref[2, nz - 1] = jnp.ones_like(nothing)


def starting_order(messages, back=False):
    if back:
        return [messages[0], messages[-1], *messages[1:-1]]
    return [messages[0], *messages[2:], messages[1]]


def join_kernel(small_ref, *refs):
    tail_ref, count, index = refs[-1], len(refs) - 1, lax.axis_index("gz")
    messages = [refs[k] for k in starting_order(list(range(count)), True)]
    tail_ref[:4] = small_ref[:4]
    for shift, message in enumerate(messages):
        place = 4 + 2 * lax.rem(index - shift + count, count)
        tail_ref[pl.ds(place, 2)] = message[...]


def finish_kernel(ready_ref, tail_ref, bands_ref, theirs_ref, mine_ref, state_ref):
    count, index = (tail_ref.shape[0] - 4) // 2, lax.axis_index("gz")
    blocks = [
        (bands_ref[3 * k], bands_ref[3 * k + 1], tail_ref[4 + 2 * k], bands_ref[3 * k + 2],
         tail_ref[5 + 2 * k])
        for k in range(count)
    ]
    below, last = chain(blocks, count, index, state_ref)
    outer, between, inverse, source_first = (tail_ref[i] for i in range(4))
    first = (source_first + outer * below + between * last) * inverse
    nx = theirs_ref.shape[-1]
    heated = ready_ref[0] + ready_ref[1] * first + ready_ref[2] * last
    theirs_ref[...], mine_ref[...] = heated[:, :, :nx], heated[:, :, nx:]


def ends_kernel(
    conduct_a_ref, edge_a_ref, label_b_ref, edge_b_ref, table_ref, zl_ref, zr_ref, zinv_ref,
    message_ref, conduct_ref, edge_ref
):
    half = conduct_a_ref.shape[-1]
    conduct_ref[:, :, :half] = conduct_a_ref[...]
    conduct_ref[:, :, half:] = look_up(label_b_ref[...], table_ref)
    edge_ref[:, :half] = edge_a_ref[...].astype(F32)
    edge_ref[:, half:] = edge_b_ref[...].astype(F32)
    conduct = conduct_ref[...]
    nz = conduct.shape[0]
    link = link_of(UPWARD_SCALE, conduct[1:], conduct[:-1])
    link = jnp.concatenate([jnp.zeros_like(conduct[:1]), link], 0)
    _, high, inverse, own = reduce_interior(link, 0, zl_ref, zr_ref)
    zinv_ref[...] = inverse
    own_first, own_last, between = end_bands(link, link[1], link[nz - 1], 0, high, own)
    ground = UPWARD_SCALE * conduct[0] * edge_ref[...]
    own_first = own_first + jnp.where(lax.axis_index("gz") == 0, ground, 0.0)
    for i, value in enumerate((own_first, own_last, between, conduct[0], conduct[nz - 1])):
        message_ref[i] = value


def all_bands_kernel(*refs):
    messages, (bands_ref, blocks_ref) = refs[:-2][::-1], refs[-2:]
    count, index = len(messages), lax.axis_index("gz")
    for shift, message in enumerate(messages):
        blocks_ref[lax.rem(index - shift + count, count)] = message[...]
    for k in range(count):
        own_first, own_last, between, first, _ = (blocks_ref[k, i] for i in range(5))
        outer = jnp.zeros_like(first)
        if k > 0:
            outer = link_of(UPWARD_SCALE, first, blocks_ref[k - 1, 4])
        inverse = 1.0 / (own_first + between + outer)
        bands_ref[3 * k] = outer * between * inverse
        bands_ref[3 * k + 1] = outer * own_first * inverse
        bands_ref[3 * k + 2] = own_last + between * own_first * inverse


VMEM = pl.BlockSpec(memory_space=pltpu.VMEM)
HBM = pl.BlockSpec(memory_space=pltpu.HBM)


def call(kernel, outs, operands, scratch=(), specs=None, ops=200_000, vmem=32):
    return pl.pallas_call(
        kernel,
        out_shape=[jax.ShapeDtypeStruct(out, F32) if isinstance(out, tuple) else out for out in outs],
        in_specs=specs or [VMEM] * len(operands),
        out_specs=[VMEM] * len(outs),
        scratch_shapes=[pltpu.VMEM(item, F32) if isinstance(item, tuple) else item for item in scratch],
        compiler_params=pltpu.CompilerParams(vmem_limit_bytes=vmem * 1024 * 1024),
        cost_estimate=pl.CostEstimate(flops=ops, bytes_accessed=ops, transcendentals=0),
    )(*operands)


def neighbour_swaps(name, other, faces):
    count, width = lax.axis_size(name), lax.axis_size(other)
    received = [lax.ppermute(faces[0], name, [(i, i ^ 1) for i in range(count)])]
    if count > 2:
        pairs = []
        for j in range(width):
            for i in range(count):
                at = (j ^ 1, i) if i in (0, count - 1) else (j, ((i + 1) ^ 1) - 1)
                pairs.append(((j, i), at))
        if (other, name) == ("gy", "gz"):
            axes, place = (other, name), lambda at: at[0] * count + at[1]
        else:
            axes, place = (name, other), lambda at: at[1] * width + at[0]
        pairs = [(place(source), place(target)) for source, target in pairs]
        received.append(lax.ppermute(faces[1], axes, pairs))
    return received


def swap_all(name, message, stride=1):
    count = lax.axis_size(name)
    return [message] + [
        lax.ppermute(message, name, [(i, (i + shift) % count) for i in range(count)])
        for shift in range(stride, count, stride)
    ]


def other_core(values):
    count = lax.axis_size("gx")
    return lax.ppermute(values, "gx", [(i, i ^ 1) for i in range(count)])


def chip_step(heat_a, label_a, edge_a, heat_b, conduct_b, edge_b, table):
    nz, ny, half = heat_a.shape
    nx = 2 * half
    block, lines, layer, rows = (nz, ny, nx), (nx, nz * ny), (ny, nx), (nz, nx)
    count_x, count_y, count_z = (lax.axis_size(name) for name in ("gx", "gy", "gz"))
    count_x = count_x // 2
    tiles = (nx // 8, 8, lines[1])
    y_steps, z_steps = (len(steps_of(length)) for length in (ny, nz))

    halo_counts = swaps_along("gz"), swaps_along("gy")
    heat, conduct, edge, *faces = call(
        start_kernel,
        [block, block, layer] + [(2, *layer)] * halo_counts[0] + [(2, *rows)] * halo_counts[1],
        [heat_a, label_a, edge_a, heat_b, conduct_b, edge_b, table],
    )
    z_halo = neighbour_swaps("gz", "gy", faces[: halo_counts[0]])
    y_halo = neighbour_swaps("gy", "gz", faces[halo_counts[0] :])

    (
        x_left, x_right, x_low, x_high, x_kept, x_gone, x_ends, x_local, x_low_block, x_high_block,
        z_left, z_right, z_low, z_high, z_inverse, z_inner,
    ) = call(
        x_bands_kernel,
        [(3, *lines)] * 2 + [lines] * 2 + [(2, *tiles), (3, *tiles), (8, lines[1])] + [block] * 3
        + [(z_steps, *block)] * 2 + [block] * 3 + [(5, *layer)],
        [heat, conduct],
    )
    x_message, z_flow, y_flow, z_ends = call(
        functools.partial(x_message_kernel, halo_counts),
        [(8, lines[1]), (2, *layer), (2, *rows), (5, *layer)],
        [heat, conduct, edge, x_low_block, x_high_block, x_ends, z_inner,
         *join_halos(z_halo, y_halo)],
    )
    x_messages = swap_all("gx", x_message, 2)
    two = count_y == 2
    y_left, y_right, y_low, y_high, y_inverse, y_ends, *y_two = call(
        functools.partial(y_bands_kernel, len(y_halo)),
        [(y_steps, *block)] * 2 + [block] * 3 + [(7, *rows)] + [(2, *rows), block] * two,
        [conduct, *y_halo],
    )
    y_sum, y_share = y_two[:1], y_two[1:]
    (x_part,) = call(
        x_source_kernel,
        [lines],
        [x_local, z_flow, y_flow, x_left, x_right, x_kept, x_gone],
        [block],
    )
    y_rows = 2 if two else 5
    y_source, y_message = call(
        functools.partial(y_message_kernel, count_x, count_y),
        [block, (y_rows, *rows)],
        [heat, x_part, x_low, x_high, y_ends, *x_messages, *(y_share or (y_low, y_high)), *y_sum],
        [(count_x, 8, lines[1]), (8, count_x, lines[1]), (5, count_x, 8, lines[1])],
    )
    y_messages = swap_all("gy", y_message)
    y_part, y_end_sources, spare, heat_out = call(
        y_source_kernel,
        [block, (2, *rows), (bands_rows(count_z, nz), *layer), block],
        [heat, y_source, y_left, y_right, y_inverse, y_ends],
    )
    z_source, z_small, z_message = call(
        functools.partial(z_message_kernel, count_y),
        [block, (6, *layer), (2, *layer)],
        [y_part, y_low, y_high, y_ends, y_end_sources, z_low, z_high, z_ends, *y_messages],
        [(2, *rows)] + ([] if two else [(count_y, y_rows, *rows), (5, count_y, *rows)]),
    )
    return heat_out, spare, z_source, z_left, z_right, z_inverse, z_small, z_message


def bands_rows(count_z, nz):
    return -(-3 * count_z // nz) * nz


def chip_bands(heat_b, label_b, edge_b, heat_a, conduct_a, edge_a, table):
    nz, ny, half = conduct_a.shape
    nx = 2 * half
    block, layer, count_z = (nz, ny, nx), (ny, nx), lax.axis_size("gz")
    z_steps = len(steps_of(nz))
    z_left, z_right, z_inverse, message = call(
        ends_kernel,
        [(z_steps, *block)] * 2 + [block] + [(5, *layer)],
        [conduct_a, edge_a, label_b, edge_b, table],
        [block, layer],
    )
    (bands,) = call(
        all_bands_kernel,
        [(bands_rows(count_z, nz), *layer)],
        swap_all("gz", message)[::-1],
        [(count_z, 5, *layer)],
    )
    zeros = lambda *shape: jnp.zeros(shape, F32)
    return (
        zeros(*block), bands, zeros(*block), z_left, z_right, z_inverse, zeros(6, *layer),
        zeros(2, *layer),
    )


def z_round(heat, _, z_source, z_left, z_right, z_inverse, z_small, z_message):
    count_z, block, layer = lax.axis_size("gz"), heat.shape, heat.shape[1:]
    messages = swap_all("gz", z_message)
    (ready,) = call(
        z_source_kernel, [(3, *block)], [heat, z_source, z_left, z_right, z_inverse, z_small]
    )
    (tail,) = call(join_kernel, [(4 + 2 * count_z, *layer)], [z_small, *starting_order(messages)])
    return ready, tail


def z_idle(heat, *_):
    count_z, block, layer = lax.axis_size("gz"), heat.shape, heat.shape[1:]
    return jnp.zeros((3, *block), F32), jnp.zeros((4 + 2 * count_z, *layer), F32)


def local(heat, label, table, edge):
    label_a, heat_a, edge_a = (other_core(values) for values in (label, heat, edge))
    entries = table.shape[0]
    own_heat, own_conduct, rows, own_edge = call(
        stage_kernel,
        [heat.shape, heat.shape, (entries, 8, heat.shape[-1]),
         jax.ShapeDtypeStruct(edge.shape, edge.dtype)],
        [heat, label, table, edge],
        [pltpu.VMEM(label.shape, label.dtype), pltpu.SMEM(table.shape, F32),
         pltpu.SemaphoreType.DMA((4,))],
        [HBM] * 4,
        vmem=60,
    )
    second = lax.axis_index("gx") % 2 == 1
    state = lax.cond(
        second, chip_step, chip_bands,
        heat_a, label_a, edge_a, own_heat, own_conduct, own_edge, rows,
    )
    bands = other_core(state[1])
    ready, tail = lax.cond(second, z_round, z_idle, *state)
    theirs, mine = call(
        finish_kernel,
        [heat_a.shape] * 2,
        [ready, tail, bands],
        [(5, lax.axis_size("gz"), *tail.shape[1:])],
    )
    return jnp.where(second, mine, other_core(theirs))


def solution(mesh):
    return jax.shard_map(
        local,
        mesh=mesh,
        in_specs=(P("gz", "gy", "gx"), P("gz", "gy", "gx"), P(), P("gy", "gx")),
        out_specs=P("gz", "gy", "gx"),
        check_vma=False,
    )
```

```python
import functools

import jax
import jax.numpy as jnp
from jax import lax
from jax.experimental import pallas as pl
from jax.experimental.pallas import tpu as pltpu
from jax.sharding import PartitionSpec as P

FLAT_SCALE = 1000.0
UPWARD_SCALE = 200.0
F32 = jnp.float32


def link_of(scale, one, other):
    return scale * one * other / (one + other)


def roll(values, offset, axis):
    if axis == 0 and values.ndim == 3:
        offset = offset % values.shape[0]
        return jnp.concatenate([values[-offset:], values[:-offset]], 0)
    return pltpu.roll(values, offset % values.shape[axis], axis)


def steps_of(length):
    steps, distance = [], 1
    while distance < length - 1:
        steps.append(distance)
        distance *= 2
    return steps


def reduce_interior(link, axis, left_ref, right_ref):
    length = link.shape[axis]
    row = lax.broadcasted_iota(jnp.int32, link.shape, axis)
    low, high, own = link, roll(link, -1, axis), jnp.ones_like(link)
    high = jnp.where(row == length - 1, 0.0, high)
    for step, distance in enumerate(steps_of(length)):
        inverse = 1.0 / (own + low + high)
        open_low, open_high = row > distance, row < length - 1 - distance
        left = jnp.where(open_low, low * roll(inverse, distance, axis), 0.0)
        right = jnp.where(open_high, high * roll(inverse, -distance, axis), 0.0)
        left_ref[step], right_ref[step] = left, right
        own = own + left * roll(own, distance, axis) + right * roll(own, -distance, axis)
        low = jnp.where(open_low, left * roll(low, distance, axis), low)
        high = jnp.where(open_high, right * roll(high, -distance, axis), high)
    inverse = 1.0 / (own + low + high)
    inner = (row > 0) & (row < length - 1)
    share_low = jnp.where(inner, low * inverse, jnp.where(row == 0, 1.0, 0.0))
    share_high = jnp.where(inner, high * inverse, jnp.where(row == 0, 0.0, 1.0))
    return share_low, share_high, jnp.where(inner, inverse, 0.0), own * inverse


def reduce_source(source, axis, left_ref, right_ref, inverse):
    length = source.shape[axis]
    for step, distance in enumerate(steps_of(length)):
        source = (
            source
            + left_ref[step] * roll(source, distance, axis)
            + right_ref[step] * roll(source, -distance, axis)
        )
    return source * inverse


def halvings(count):
    rows, stages = list(range(count)), []
    while len(rows) > 1:
        near = [
            (row, rows[i - 1] if i else None, rows[i + 1] if i + 1 < len(rows) else None)
            for i, row in enumerate(rows)
        ]
        stages.append((near[0::2], near[1::2]))
        rows = rows[0::2]
    return stages


def reduce_lines(link, left_ref, right_ref, kept_ref, gone_ref):
    length = link.shape[0]
    count = length // 8
    row = lax.broadcasted_iota(jnp.int32, link.shape, 0)
    low, high, own = link, roll(link, -1, 0), jnp.ones_like(link)
    for step, distance in enumerate((1, 2, 4)):
        inverse = 1.0 / (own + low + high)
        open_low, open_high = row > distance, row < length - 1 - distance
        left = jnp.where(open_low, low * roll(inverse, distance, 0), 0.0)
        right = jnp.where(open_high, high * roll(inverse, -distance, 0), 0.0)
        left_ref[step], right_ref[step] = left, right
        own = own + left * roll(own, distance, 0) + right * roll(own, -distance, 0)
        low = jnp.where(open_low, left * roll(low, distance, 0), low)
        high = jnp.where(open_high, right * roll(high, -distance, 0), high)
    first, last = row == 0, row == length - 1
    own = jnp.where(first | last, 0.0, own)
    low = jnp.where(first, 1.0, jnp.where(last, 0.0, low))
    high = jnp.where(last, 1.0, jnp.where(first, 0.0, high))
    tiles = lambda values: [values[8 * k : 8 * k + 8] for k in range(count)]
    own, low, high = tiles(own), tiles(low), tiles(high)
    inverse, share_low, share_high, share_own = {}, {}, {}, {}

    def finish(k):
        inverse[k] = 1.0 / (own[k] + low[k] + high[k])
        gone_ref[0, k], gone_ref[1, k] = low[k] * inverse[k], high[k] * inverse[k]
        gone_ref[2, k] = inverse[k]

    slot = 0
    for kept, gone in halvings(count):
        for k, _, _ in gone:
            finish(k)
        for k, below, above in kept:
            new_low, new_high = low[k], high[k]
            if below is not None:
                factor = low[k] * inverse[below]
                kept_ref[0, slot] = factor
                own[k] = own[k] + factor * own[below]
                new_low = factor * low[below]
            if above is not None:
                factor = high[k] * inverse[above]
                kept_ref[1, slot] = factor
                own[k] = own[k] + factor * own[above]
                new_high = factor * high[above]
            low[k], high[k] = new_low, new_high
            slot += 1
    finish(0)
    share_low[0], share_high[0] = low[0] * inverse[0], high[0] * inverse[0]
    share_own[0] = own[0] * inverse[0]
    for _, gone in halvings(count)[::-1]:
        for k, below, above in gone:
            to_low, to_high = low[k] * inverse[k], high[k] * inverse[k]
            share_low[k] = to_low * share_low[below]
            share_high[k] = to_low * share_high[below]
            if above is None:
                share_high[k] = share_high[k] + to_high
                share_own[k] = own[k] * inverse[k] + to_low * share_own[below]
            else:
                share_low[k] = share_low[k] + to_high * share_low[above]
                share_high[k] = share_high[k] + to_high * share_high[above]
    whole = lambda shares: jnp.concatenate([shares[k] for k in range(count)], 0)
    return whole(share_low), whole(share_high), share_own[0][1:2], share_own[count - 1][6:7]


def solve_lines(source, left_ref, right_ref, kept_ref, gone_ref):
    length = source.shape[0]
    count = length // 8
    for step, distance in enumerate((1, 2, 4)):
        source = (
            source
            + left_ref[step] * roll(source, distance, 0)
            + right_ref[step] * roll(source, -distance, 0)
        )
    row = lax.broadcasted_iota(jnp.int32, source.shape, 0)
    source = jnp.where((row == 0) | (row == length - 1), 0.0, source)
    source = [source[8 * k : 8 * k + 8] for k in range(count)]
    slot, stages = 0, halvings(count)
    for kept, _ in stages:
        for k, below, above in kept:
            if below is not None:
                source[k] = source[k] + kept_ref[0, slot] * source[below]
            if above is not None:
                source[k] = source[k] + kept_ref[1, slot] * source[above]
            slot += 1
    solved = {0: source[0] * gone_ref[2, 0]}
    for _, gone in stages[::-1]:
        for k, below, above in gone:
            solved[k] = source[k] * gone_ref[2, k] + gone_ref[0, k] * solved[below]
            if above is not None:
                solved[k] = solved[k] + gone_ref[1, k] * solved[above]
    return jnp.concatenate([solved[k] for k in range(count)], 0)


def chain(blocks, count, index, state):
    own = [blocks[k][3] + (blocks[k + 1][1] if k + 1 < count else 0.0) for k in range(count)]
    source = [blocks[k][4] + (blocks[k + 1][2] if k + 1 < count else 0.0) for k in range(count)]
    shape = own[0].shape
    state[0, 0], state[1, 0] = jnp.ones(shape, F32), jnp.zeros(shape, F32)
    up_own, up_source = own[0], source[0]
    for k in range(1, count):
        state[0, k], state[1, k] = up_own, up_source
        factor = blocks[k][0] / (up_own + blocks[k][0])
        up_own, up_source = own[k] + factor * up_own, source[k] + factor * up_source
    down_own, down_source = own[count - 1], source[count - 1]
    state[2, count - 1], state[3, count - 1] = down_own, down_source
    for k in range(count - 2, -1, -1):
        factor = blocks[k + 1][0] / (down_own + blocks[k + 1][0])
        down_own, down_source = own[k] + factor * down_own, source[k] + factor * down_source
        state[2, k], state[3, k] = down_own, down_source
    for k in range(count):
        state[4, k] = blocks[k][0]
    up_own, up_source, down_own, down_source, link = (state[i, index] for i in range(5))
    inverse = 1.0 / (up_own * down_own + link * (up_own + down_own))
    below = ((down_own + link) * up_source + link * down_source) * inverse
    here = ((up_own + link) * down_source + link * up_source) * inverse
    return below, here


def pick_halo(name, received, odd):
    first = received[0][...]
    second = received[1][...] if len(received) > 1 else jnp.zeros_like(first)
    index, count = lax.axis_index(name), lax.axis_size(name)
    below = jnp.where(odd, first, second)
    above = jnp.where(odd, second, first)
    return jnp.where(index > 0, below, 0.0), jnp.where(index < count - 1, above, 0.0)


def swaps_along(name):
    return min(lax.axis_size(name) - 1, 2)


def look_up(label, table_ref):
    conduct = jnp.broadcast_to(table_ref[0], label.shape)
    for entry in range(1, table_ref.shape[0]):
        conduct = jnp.where(label == entry, table_ref[entry], conduct)
    return conduct


def stage_kernel(
    heat_in, label_in, table_in, edge_in, heat_ref, conduct_ref, table_ref, edge_ref, label_ref,
    entries_ref, sems
):
    copies = [
        pltpu.make_async_copy(source, target, sems.at[i])
        for i, (source, target) in enumerate(
            (
                (table_in, entries_ref), (label_in, label_ref), (heat_in, heat_ref),
                (edge_in, edge_ref),
            )
        )
    ]
    for copy in copies:
        copy.start()
    copies[0].wait()
    for entry in range(table_ref.shape[0]):
        table_ref[entry] = jnp.full(table_ref.shape[1:], entries_ref[entry], F32)
    copies[1].wait()
    conduct_ref[...] = look_up(label_ref[...], table_ref)
    copies[2].wait()
    copies[3].wait()


def join_halos(z_halo, y_halo):
    return [*z_halo[1:], z_halo[0], *y_halo]


def split_halos(counts, refs):
    halos = refs[: sum(counts)]
    return [halos[counts[0] - 1], *halos[: counts[0] - 1]], halos[counts[0] :]


def start_kernel(
    heat_a_ref, label_a_ref, edge_a_ref, heat_b_ref, conduct_b_ref, edge_b_ref, table_ref,
    heat_ref, conduct_ref, edge_ref, *faces
):
    nx = heat_a_ref.shape[-1]
    heat_ref[:, :, :nx], heat_ref[:, :, nx:] = heat_a_ref[...], heat_b_ref[...]
    conduct_ref[:, :, :nx] = look_up(label_a_ref[...], table_ref)
    conduct_ref[:, :, nx:] = conduct_b_ref[...]
    edge_ref[:, :nx] = edge_a_ref[...].astype(F32)
    edge_ref[:, nx:] = edge_b_ref[...].astype(F32)
    z_faces, y_faces = faces[: swaps_along("gz")], faces[swaps_along("gz") :]
    odd_z = lax.axis_index("gz") % 2 == 1
    odd_y = lax.axis_index("gy") % 2 == 1
    for i, ref in enumerate((heat_ref, conduct_ref)):
        low, high = ref[0], ref[ref.shape[0] - 1]
        for face_ref, pick in zip(z_faces, (odd_z, ~odd_z)):
            face_ref[i] = jnp.where(pick, low, high)
        low, high = ref[:, 0, :], ref[:, ref.shape[1] - 1, :]
        for face_ref, pick in zip(y_faces, (odd_y, ~odd_y)):
            face_ref[i] = jnp.where(pick, low, high)


def end_bands(link, first, last, axis, high, own):
    length = high.shape[axis]
    at = lambda values, i: lax.index_in_dim(values, i, axis, keepdims=False)
    return (
        1.0 + first * at(own, 1),
        1.0 + last * at(own, length - 2),
        first * at(high, 1),
    )


def x_bands_kernel(
    heat_ref, conduct_ref, left_ref, right_ref, low_ref, high_ref, kept_ref, gone_ref, ends_ref,
    local_ref, low_block_ref, high_block_ref, zl_ref, zr_ref, zlow_ref, zhigh_ref, zinv_ref, zinner_ref
):
    nz, ny, nx = conduct_ref.shape
    conduct = conduct_ref[...]
    link = link_of(UPWARD_SCALE, conduct[1:], conduct[:-1])
    link = jnp.concatenate([jnp.zeros_like(conduct[:1]), link], 0)
    low, high, inverse, own = reduce_interior(link, 0, zl_ref, zr_ref)
    zlow_ref[...], zhigh_ref[...], zinv_ref[...] = low, high, inverse
    inner = end_bands(link, link[1], link[nz - 1], 0, high, own)
    for i, value in enumerate((*inner, link[1], link[nz - 1])):
        zinner_ref[i] = value
    heat = heat_ref[...]
    local = 2.0 * heat
    across = 2.0 * link_of(UPWARD_SCALE, conduct[1:], conduct[:-1]) * (heat[1:] - heat[:-1])
    nothing = jnp.zeros_like(heat[:1])
    local = local + jnp.concatenate([across, nothing], 0) - jnp.concatenate([nothing, across], 0)
    row = lax.broadcasted_iota(jnp.int32, conduct.shape, 1)
    across = 2.0 * link_of(FLAT_SCALE, conduct, roll(conduct, 1, 1)) * (heat - roll(heat, 1, 1))
    across = jnp.where(row > 0, across, 0.0)
    local = local - across + roll(across, -1, 1)
    local_ref[...] = local
    lines = conduct.reshape(nz * ny, nx).T
    row = lax.broadcasted_iota(jnp.int32, lines.shape, 0)
    link = jnp.where(row > 0, link_of(FLAT_SCALE, lines, roll(lines, 1, 0)), 0.0)
    low, high, own_low, own_high = reduce_lines(link, left_ref, right_ref, kept_ref, gone_ref)
    low_ref[...], high_ref[...] = low, high
    low_block_ref[...] = low.T.reshape(nz, ny, nx)
    high_block_ref[...] = high.T.reshape(nz, ny, nx)
    local = local.reshape(nz * ny, nx).T
    first, last = link[1:2], link[nx - 1 :]
    ends_ref[...] = jnp.concatenate(
        [
            jnp.sum(low * local, 0, keepdims=True),
            jnp.sum(high * local, 0, keepdims=True),
            1.0 + first * own_low,
            1.0 + last * own_high,
            first * high[1:2],
            lines[:1],
            lines[nx - 1 :],
            jnp.zeros_like(first),
        ],
        0,
    )


def x_message_kernel(
    halo_counts, heat_ref, conduct_ref, edge_ref, low_ref, high_ref, ends_ref, zinner_ref, *refs
):
    z_halo, y_halo = split_halos(halo_counts, refs)
    message_ref, z_flow_ref, y_flow_ref, zends_ref = refs[sum(halo_counts) :]
    nz, ny, nx = conduct_ref.shape
    lanes = nz * ny
    index_z, index_y = lax.axis_index("gz"), lax.axis_index("gy")
    below, above = pick_halo("gz", z_halo, index_z % 2 == 1)
    ground = jnp.where(index_z == 0, UPWARD_SCALE * conduct_ref[0] * edge_ref[...], 0.0)
    outer = link_of(UPWARD_SCALE, conduct_ref[0], below[1])
    z_flow_ref[0] = 2.0 * (outer * (below[0] - heat_ref[0]) - ground * heat_ref[0])
    own_first, own_last, between = zinner_ref[0] + ground, zinner_ref[1], zinner_ref[2]
    inverse = 1.0 / (own_first + between + outer)
    for i, value in enumerate((outer, between, inverse, zinner_ref[3], zinner_ref[4])):
        zends_ref[i] = value
    flow = link_of(UPWARD_SCALE, conduct_ref[nz - 1], above[1]) * (above[0] - heat_ref[nz - 1])
    z_flow_ref[1] = 2.0 * flow
    odd = index_y % 2 == 1
    near = lambda ref: jnp.where(odd, ref[:, 0, :], ref[:, ny - 1, :])
    if len(y_halo) == 1:
        flow = link_of(FLAT_SCALE, near(conduct_ref), y_halo[0][1])
        flow = 2.0 * flow * (y_halo[0][0] - near(heat_ref))
        y_flow_ref[0] = jnp.where(odd, flow, 0.0)
        y_flow_ref[1] = jnp.where(odd, 0.0, flow)
    else:
        below, above = pick_halo("gy", y_halo, index_y % 2 == 1)
        flow = link_of(FLAT_SCALE, conduct_ref[:, 0, :], below[1]) * (below[0] - heat_ref[:, 0, :])
        y_flow_ref[0] = 2.0 * flow
        flow = link_of(FLAT_SCALE, conduct_ref[:, ny - 1, :], above[1])
        y_flow_ref[1] = 2.0 * flow * (above[0] - heat_ref[:, ny - 1, :])

    def spread(values, first, step):
        shape = (values.shape[0], lanes)
        row = lax.broadcasted_iota(jnp.int32, shape, 0)
        lane = lax.broadcasted_iota(jnp.int32, shape, 1)
        return jnp.where(lane == first + step * row, jnp.sum(values, 1, keepdims=True), 0.0)

    sums = []
    for share in (low_ref, high_ref):
        layers = spread(share[0] * z_flow_ref[0], 0, 1)
        layers = layers + spread(share[nz - 1] * z_flow_ref[1], lanes - ny, 1)
        if len(y_halo) == 1:
            rows = spread(near(share) * flow, jnp.where(odd, 0, ny - 1), ny)
        else:
            rows = spread(share[:, 0, :] * y_flow_ref[0], 0, ny)
            rows = rows + spread(share[:, ny - 1, :] * y_flow_ref[1], ny - 1, ny)
        sums.append(jnp.sum(layers, 0, keepdims=True) + jnp.sum(rows, 0, keepdims=True))
    ends = ends_ref[...]
    message_ref[...] = jnp.concatenate([ends[0:1] + sums[0], ends[1:2] + sums[1], ends[2:8]], 0)


def x_source_kernel(
    local_ref, z_flow_ref, y_flow_ref, left_ref, right_ref, kept_ref, gone_ref, part_ref, source_ref
):
    nz, ny, nx = local_ref.shape
    source_ref[...] = local_ref[...]
    source_ref[0] += z_flow_ref[0]
    source_ref[nz - 1] += z_flow_ref[1]
    source_ref[:, 0, :] += y_flow_ref[0]
    source_ref[:, ny - 1, :] += y_flow_ref[1]
    source = source_ref[...].reshape(nz * ny, nx).T
    part_ref[...] = solve_lines(source, left_ref, right_ref, kept_ref, gone_ref)


def y_bands_kernel(halo_count, conduct_ref, *refs):
    y_halo = refs[:halo_count]
    yl_ref, yr_ref, ylow_ref, yhigh_ref, yinv_ref, yends_ref, *y_two_refs = refs[halo_count:]
    nz, ny, nx = conduct_ref.shape
    index_y = lax.axis_index("gy")
    conduct = conduct_ref[...]
    row = lax.broadcasted_iota(jnp.int32, conduct.shape, 1)
    link = jnp.where(row > 0, link_of(FLAT_SCALE, conduct, roll(conduct, 1, 1)), 0.0)
    low, high, inverse, own = reduce_interior(link, 1, yl_ref, yr_ref)
    ylow_ref[...], yhigh_ref[...], yinv_ref[...] = low, high, inverse
    below, above = pick_halo("gy", y_halo, index_y % 2 == 1)
    first = link_of(FLAT_SCALE, conduct_ref[:, 0, :], conduct_ref[:, 1, :])
    last = link_of(FLAT_SCALE, conduct_ref[:, ny - 1, :], conduct_ref[:, ny - 2, :])
    own_first, own_last, between = end_bands(link, first, last, 1, high, own)
    outer_low = link_of(FLAT_SCALE, conduct_ref[:, 0, :], below[1])
    outer_high = link_of(FLAT_SCALE, conduct_ref[:, ny - 1, :], above[1])
    for i, value in enumerate((first, last, own_first, own_last, between, outer_low, outer_high)):
        yends_ref[i] = value
    if y_two_refs:
        ysum_ref, yshare_ref = y_two_refs
        odd = index_y % 2 == 1
        near_own, far_own = jnp.where(odd, own_first, own_last), jnp.where(odd, own_last, own_first)
        share = between / (far_own + between)
        ysum_ref[0] = near_own + share * far_own
        ysum_ref[1] = share
        for k in range(nz):
            near, far = jnp.where(odd, low[k], high[k]), jnp.where(odd, high[k], low[k])
            yshare_ref[k] = near + ysum_ref[1, pl.ds(k, 1), :] * far


def chain_message(ends_ref, source_first, source_last, message_ref):
    own_first, own_last, between, outer = (ends_ref[i] for i in range(2, 6))
    inverse = 1.0 / (own_first + between + outer)
    message_ref[0] = outer * between * inverse
    message_ref[1] = outer * own_first * inverse
    message_ref[2] = outer * inverse * source_first
    message_ref[3] = own_last + between * own_first * inverse
    message_ref[4] = source_last + between * inverse * source_first


def chain_ends(name, messages, ends_ref, source_first, blocks_ref, state_ref):
    count, index = lax.axis_size(name), lax.axis_index(name)
    for shift, message in enumerate(messages):
        blocks_ref[lax.rem(index - shift + count, count)] = message[...]
    blocks = [tuple(blocks_ref[k, i] for i in range(5)) for k in range(count)]
    below, last = chain(blocks, count, index, state_ref)
    own_first, between, outer = ends_ref[2], ends_ref[4], ends_ref[5]
    first = (source_first + outer * below + between * last) / (own_first + between + outer)
    return first, last


def y_message_kernel(
    count_x, count_y, heat_ref, part_ref, low_ref, high_ref, yends_ref, *refs
):
    messages, refs = refs[:count_x], refs[count_x:]
    shares, refs = (refs[:2], refs[2:]) if count_y > 2 else (refs[:1], refs[1:])
    sums_ref, refs = (None, refs) if count_y > 2 else (refs[0], refs[1:])
    source_ref, message_ref, blocks_ref, rows_ref, state_ref = refs
    nz, ny, nx = heat_ref.shape
    index = lax.axis_index("gx") // 2
    for shift, message in enumerate(messages):
        blocks_ref[lax.rem(index - shift + count_x, count_x)] = message[...]
    first, last, own_first, own_last, between, c_first, c_last = (
        blocks_ref[:, i, :] for i in range(7)
    )
    before = jnp.zeros_like(c_last[:1])
    if count_x > 1:
        before = jnp.concatenate([before, c_last[:-1]], 0)
    outer = link_of(FLAT_SCALE, c_first, before)
    inverse = 1.0 / (own_first + between + outer)
    rows = (
        outer * between * inverse,
        outer * own_first * inverse,
        outer * inverse * first,
        own_last + between * own_first * inverse,
        last + between * inverse * first,
        first * inverse,
        outer * inverse,
        between * inverse,
    )
    for i, value in enumerate(rows):
        rows_ref[i] = value
    whole = lambda i, k: jnp.broadcast_to(rows_ref[i, pl.ds(k, 1), :], (8, rows_ref.shape[2]))
    blocks = [tuple(whole(i, k) for i in range(5)) for k in range(count_x)]
    below, last = chain(blocks, count_x, index, state_ref)
    first = whole(5, index) + whole(6, index) * below + whole(7, index) * last
    lines = part_ref[...] + low_ref[...] * first[:1] + high_ref[...] * last[:1]
    source = lines.T.reshape(nz, ny, nx) - 2.0 * heat_ref[...]
    source_ref[...] = source
    sums = [jnp.sum(share[...] * source, 1) for share in shares]
    if count_y > 2:
        chain_message(yends_ref, *sums, message_ref)
    else:
        message_ref[0], message_ref[1] = sums_ref[0], sums[0]


def y_source_kernel(
    heat_ref, source_ref, yl_ref, yr_ref, yinv_ref, yends_ref, ypart_ref, ysource_ref, spare_ref,
    heat_out_ref
):
    spare_ref[...] = jnp.zeros_like(spare_ref)
    heat_out_ref[...] = heat_ref[...]
    ny = source_ref.shape[1]
    part = reduce_source(source_ref[...], 1, yl_ref, yr_ref, yinv_ref[...])
    ypart_ref[...] = part
    ysource_ref[0] = source_ref[:, 0, :] + yends_ref[0] * ypart_ref[:, 1, :]
    ysource_ref[1] = source_ref[:, ny - 1, :] + yends_ref[1] * ypart_ref[:, ny - 2, :]


def z_message_kernel(
    count_y, ypart_ref, ylow_ref, yhigh_ref, yends_ref, ysource_ref, zlow_ref, zhigh_ref,
    zends_ref, *refs
):
    messages, refs = refs[:count_y], refs[count_y:]
    source_ref, small_ref, message_ref, ends_ref, *state = refs
    nz, ny, nx = ypart_ref.shape
    if count_y > 2:
        first, last = chain_ends("gy", messages, yends_ref, ysource_ref[0], *state)
    else:
        odd = lax.axis_index("gy") % 2 == 1
        mine, other = messages
        outer = jnp.where(odd, yends_ref[5], yends_ref[6])
        between = yends_ref[4]
        factor = outer / (other[0] + outer)
        near = (mine[1] + factor * other[1]) / (mine[0] + factor * other[0])
        far_own = jnp.where(odd, yends_ref[3], yends_ref[2])
        far_source = jnp.where(odd, ysource_ref[1], ysource_ref[0])
        far = (far_source + between * near) / (far_own + between)
        first, last = jnp.where(odd, near, far), jnp.where(odd, far, near)
    ends_ref[0], ends_ref[1] = first, last
    source_first, source_last = jnp.zeros((ny, nx), F32), jnp.zeros((ny, nx), F32)
    for k in range(nz):
        source = (
            ypart_ref[k]
            + ylow_ref[k] * ends_ref[0, pl.ds(k, 1), :]
            + yhigh_ref[k] * ends_ref[1, pl.ds(k, 1), :]
        )
        source_ref[k] = source
        source_first = source_first + zlow_ref[k] * source
        source_last = source_last + zhigh_ref[k] * source
    outer, between, inverse = (zends_ref[i] for i in range(3))
    for i, value in enumerate(
        (outer, between, inverse, source_first, zends_ref[3], zends_ref[4])
    ):
        small_ref[i] = value
    message_ref[0] = outer * inverse * source_first
    message_ref[1] = source_last + between * inverse * source_first


def z_source_kernel(heat_ref, source_ref, zl_ref, zr_ref, zinv_ref, small_ref, ready_ref):
    nz = source_ref.shape[0]
    inverse = zinv_ref[...]
    ready_ref[0] = heat_ref[...] + reduce_source(source_ref[...], 0, zl_ref, zr_ref, inverse)
    nothing = jnp.zeros_like(small_ref[0])
    low = jnp.stack([nothing, small_ref[4]] + [nothing] * (nz - 2), 0)
    ready_ref[1] = reduce_source(low, 0, zl_ref, zr_ref, inverse)
    ready_ref[1, 0] = jnp.ones_like(nothing)
    high = jnp.stack([nothing] * (nz - 2) + [small_ref[5], nothing], 0)
    ready_ref[2] = reduce_source(high, 0, zl_ref, zr_ref, inverse)
    ready_ref[2, nz - 1] = jnp.ones_like(nothing)


def starting_order(messages, back=False):
    if back:
        return [messages[0], messages[-1], *messages[1:-1]]
    return [messages[0], *messages[2:], messages[1]]


def join_kernel(small_ref, *refs):
    tail_ref, count, index = refs[-1], len(refs) - 1, lax.axis_index("gz")
    messages = [refs[k] for k in starting_order(list(range(count)), True)]
    tail_ref[:4] = small_ref[:4]
    for shift, message in enumerate(messages):
        place = 4 + 2 * lax.rem(index - shift + count, count)
        tail_ref[pl.ds(place, 2)] = message[...]


def finish_kernel(ready_ref, tail_ref, bands_ref, theirs_ref, mine_ref, state_ref):
    count, index = (tail_ref.shape[0] - 4) // 2, lax.axis_index("gz")
    blocks = [
        (bands_ref[3 * k], bands_ref[3 * k + 1], tail_ref[4 + 2 * k], bands_ref[3 * k + 2],
         tail_ref[5 + 2 * k])
        for k in range(count)
    ]
    below, last = chain(blocks, count, index, state_ref)
    outer, between, inverse, source_first = (tail_ref[i] for i in range(4))
    first = (source_first + outer * below + between * last) * inverse
    nx = theirs_ref.shape[-1]
    heated = ready_ref[0] + ready_ref[1] * first + ready_ref[2] * last
    theirs_ref[...], mine_ref[...] = heated[:, :, :nx], heated[:, :, nx:]


def ends_kernel(
    conduct_a_ref, edge_a_ref, label_b_ref, edge_b_ref, table_ref, zl_ref, zr_ref, zinv_ref,
    message_ref, conduct_ref, edge_ref
):
    half = conduct_a_ref.shape[-1]
    conduct_ref[:, :, :half] = conduct_a_ref[...]
    conduct_ref[:, :, half:] = look_up(label_b_ref[...], table_ref)
    edge_ref[:, :half] = edge_a_ref[...].astype(F32)
    edge_ref[:, half:] = edge_b_ref[...].astype(F32)
    conduct = conduct_ref[...]
    nz = conduct.shape[0]
    link = link_of(UPWARD_SCALE, conduct[1:], conduct[:-1])
    link = jnp.concatenate([jnp.zeros_like(conduct[:1]), link], 0)
    _, high, inverse, own = reduce_interior(link, 0, zl_ref, zr_ref)
    zinv_ref[...] = inverse
    own_first, own_last, between = end_bands(link, link[1], link[nz - 1], 0, high, own)
    ground = UPWARD_SCALE * conduct[0] * edge_ref[...]
    own_first = own_first + jnp.where(lax.axis_index("gz") == 0, ground, 0.0)
    for i, value in enumerate((own_first, own_last, between, conduct[0], conduct[nz - 1])):
        message_ref[i] = value


def all_bands_kernel(*refs):
    messages, (bands_ref, blocks_ref) = starting_order(refs[:-2], True), refs[-2:]
    count, index = len(messages), lax.axis_index("gz")
    for shift, message in enumerate(messages):
        blocks_ref[lax.rem(index - shift + count, count)] = message[...]
    for k in range(count):
        own_first, own_last, between, first, _ = (blocks_ref[k, i] for i in range(5))
        outer = jnp.zeros_like(first)
        if k > 0:
            outer = link_of(UPWARD_SCALE, first, blocks_ref[k - 1, 4])
        inverse = 1.0 / (own_first + between + outer)
        bands_ref[3 * k] = outer * between * inverse
        bands_ref[3 * k + 1] = outer * own_first * inverse
        bands_ref[3 * k + 2] = own_last + between * own_first * inverse


VMEM = pl.BlockSpec(memory_space=pltpu.VMEM)
HBM = pl.BlockSpec(memory_space=pltpu.HBM)


def call(kernel, outs, operands, scratch=(), specs=None, ops=200_000, vmem=32):
    return pl.pallas_call(
        kernel,
        out_shape=[jax.ShapeDtypeStruct(out, F32) if isinstance(out, tuple) else out for out in outs],
        in_specs=specs or [VMEM] * len(operands),
        out_specs=[VMEM] * len(outs),
        scratch_shapes=[pltpu.VMEM(item, F32) if isinstance(item, tuple) else item for item in scratch],
        compiler_params=pltpu.CompilerParams(vmem_limit_bytes=vmem * 1024 * 1024),
        cost_estimate=pl.CostEstimate(flops=ops, bytes_accessed=ops, transcendentals=0),
    )(*operands)


def neighbour_swaps(name, other, faces):
    count, width = lax.axis_size(name), lax.axis_size(other)
    received = [lax.ppermute(faces[0], name, [(i, i ^ 1) for i in range(count)])]
    if count > 2:
        pairs = []
        for j in range(width):
            for i in range(count):
                at = (j ^ 1, i) if i in (0, count - 1) else (j, ((i + 1) ^ 1) - 1)
                pairs.append(((j, i), at))
        if (other, name) == ("gy", "gz"):
            axes, place = (other, name), lambda at: at[0] * count + at[1]
        else:
            axes, place = (name, other), lambda at: at[1] * width + at[0]
        pairs = [(place(source), place(target)) for source, target in pairs]
        received.append(lax.ppermute(faces[1], axes, pairs))
    return received


def swap_all(name, message, stride=1):
    count = lax.axis_size(name)
    return [message] + [
        lax.ppermute(message, name, [(i, (i + shift) % count) for i in range(count)])
        for shift in range(stride, count, stride)
    ]


def other_core(values):
    count = lax.axis_size("gx")
    return lax.ppermute(values, "gx", [(i, i ^ 1) for i in range(count)])


def chip_step(heat_a, label_a, edge_a, heat_b, conduct_b, edge_b, table):
    nz, ny, half = heat_a.shape
    nx = 2 * half
    block, lines, layer, rows = (nz, ny, nx), (nx, nz * ny), (ny, nx), (nz, nx)
    count_x, count_y, count_z = (lax.axis_size(name) for name in ("gx", "gy", "gz"))
    count_x = count_x // 2
    tiles = (nx // 8, 8, lines[1])
    y_steps, z_steps = (len(steps_of(length)) for length in (ny, nz))

    halo_counts = swaps_along("gz"), swaps_along("gy")
    heat, conduct, edge, *faces = call(
        start_kernel,
        [block, block, layer] + [(2, *layer)] * halo_counts[0] + [(2, *rows)] * halo_counts[1],
        [heat_a, label_a, edge_a, heat_b, conduct_b, edge_b, table],
    )
    z_halo = neighbour_swaps("gz", "gy", faces[: halo_counts[0]])
    y_halo = neighbour_swaps("gy", "gz", faces[halo_counts[0] :])

    (
        x_left, x_right, x_low, x_high, x_kept, x_gone, x_ends, x_local, x_low_block, x_high_block,
        z_left, z_right, z_low, z_high, z_inverse, z_inner,
    ) = call(
        x_bands_kernel,
        [(3, *lines)] * 2 + [lines] * 2 + [(2, *tiles), (3, *tiles), (8, lines[1])] + [block] * 3
        + [(z_steps, *block)] * 2 + [block] * 3 + [(5, *layer)],
        [heat, conduct],
    )
    x_message, z_flow, y_flow, z_ends = call(
        functools.partial(x_message_kernel, halo_counts),
        [(8, lines[1]), (2, *layer), (2, *rows), (5, *layer)],
        [heat, conduct, edge, x_low_block, x_high_block, x_ends, z_inner,
         *join_halos(z_halo, y_halo)],
    )
    x_messages = swap_all("gx", x_message, 2)
    two = count_y == 2
    y_left, y_right, y_low, y_high, y_inverse, y_ends, *y_two = call(
        functools.partial(y_bands_kernel, len(y_halo)),
        [(y_steps, *block)] * 2 + [block] * 3 + [(7, *rows)] + [(2, *rows), block] * two,
        [conduct, *y_halo],
    )
    y_sum, y_share = y_two[:1], y_two[1:]
    (x_part,) = call(
        x_source_kernel,
        [lines],
        [x_local, z_flow, y_flow, x_left, x_right, x_kept, x_gone],
        [block],
    )
    y_rows = 2 if two else 5
    y_source, y_message = call(
        functools.partial(y_message_kernel, count_x, count_y),
        [block, (y_rows, *rows)],
        [heat, x_part, x_low, x_high, y_ends, *x_messages, *(y_share or (y_low, y_high)), *y_sum],
        [(count_x, 8, lines[1]), (8, count_x, lines[1]), (5, count_x, 8, lines[1])],
    )
    y_messages = swap_all("gy", y_message)
    y_part, y_end_sources, spare, heat_out = call(
        y_source_kernel,
        [block, (2, *rows), (bands_rows(count_z, nz), *layer), block],
        [heat, y_source, y_left, y_right, y_inverse, y_ends],
    )
    z_source, z_small, z_message = call(
        functools.partial(z_message_kernel, count_y),
        [block, (6, *layer), (2, *layer)],
        [y_part, y_low, y_high, y_ends, y_end_sources, z_low, z_high, z_ends, *y_messages],
        [(2, *rows)] + ([] if two else [(count_y, y_rows, *rows), (5, count_y, *rows)]),
    )
    return heat_out, spare, z_source, z_left, z_right, z_inverse, z_small, z_message


def bands_rows(count_z, nz):
    return -(-3 * count_z // nz) * nz


def chip_bands(heat_b, label_b, edge_b, heat_a, conduct_a, edge_a, table):
    nz, ny, half = conduct_a.shape
    nx = 2 * half
    block, layer, count_z = (nz, ny, nx), (ny, nx), lax.axis_size("gz")
    z_steps = len(steps_of(nz))
    z_left, z_right, z_inverse, message = call(
        ends_kernel,
        [(z_steps, *block)] * 2 + [block] + [(5, *layer)],
        [conduct_a, edge_a, label_b, edge_b, table],
        [block, layer],
    )
    (bands,) = call(
        all_bands_kernel,
        [(bands_rows(count_z, nz), *layer)],
        starting_order(swap_all("gz", message)),
        [(count_z, 5, *layer)],
    )
    zeros = lambda *shape: jnp.zeros(shape, F32)
    return (
        zeros(*block), bands, zeros(*block), z_left, z_right, z_inverse, zeros(6, *layer),
        zeros(2, *layer),
    )


def z_round(heat, _, z_source, z_left, z_right, z_inverse, z_small, z_message):
    count_z, block, layer = lax.axis_size("gz"), heat.shape, heat.shape[1:]
    messages = swap_all("gz", z_message)
    (ready,) = call(
        z_source_kernel, [(3, *block)], [heat, z_source, z_left, z_right, z_inverse, z_small]
    )
    (tail,) = call(join_kernel, [(4 + 2 * count_z, *layer)], [z_small, *starting_order(messages)])
    return ready, tail


def z_idle(heat, *_):
    count_z, block, layer = lax.axis_size("gz"), heat.shape, heat.shape[1:]
    return jnp.zeros((3, *block), F32), jnp.zeros((4 + 2 * count_z, *layer), F32)


def local(heat, label, table, edge):
    label_a, heat_a, edge_a = (other_core(values) for values in (label, heat, edge))
    entries = table.shape[0]
    own_heat, own_conduct, rows, own_edge = call(
        stage_kernel,
        [heat.shape, heat.shape, (entries, 8, heat.shape[-1]),
         jax.ShapeDtypeStruct(edge.shape, edge.dtype)],
        [heat, label, table, edge],
        [pltpu.VMEM(label.shape, label.dtype), pltpu.SMEM(table.shape, F32),
         pltpu.SemaphoreType.DMA((4,))],
        [HBM] * 4,
        vmem=60,
    )
    second = lax.axis_index("gx") % 2 == 1
    state = lax.cond(
        second, chip_step, chip_bands,
        heat_a, label_a, edge_a, own_heat, own_conduct, own_edge, rows,
    )
    bands = other_core(state[1])
    ready, tail = lax.cond(second, z_round, z_idle, *state)
    theirs, mine = call(
        finish_kernel,
        [heat_a.shape] * 2,
        [ready, tail, bands],
        [(5, lax.axis_size("gz"), *tail.shape[1:])],
    )
    return jnp.where(second, mine, other_core(theirs))


def solution(mesh):
    return jax.shard_map(
        local,
        mesh=mesh,
        in_specs=(P("gz", "gy", "gx"), P("gz", "gy", "gx"), P(), P("gy", "gx")),
        out_specs=P("gz", "gy", "gx"),
        check_vma=False,
    )
```

```python
import functools

import jax
import jax.numpy as jnp
from jax import lax
from jax.experimental import pallas as pl
from jax.experimental.pallas import tpu as pltpu
from jax.sharding import PartitionSpec as P

FLAT_SCALE = 1000.0
UPWARD_SCALE = 200.0
F32 = jnp.float32


def link_of(scale, one, other):
    return scale * one * other / (one + other)


def roll(values, offset, axis):
    if axis == 0 and values.ndim == 3:
        offset = offset % values.shape[0]
        return jnp.concatenate([values[-offset:], values[:-offset]], 0)
    return pltpu.roll(values, offset % values.shape[axis], axis)


def steps_of(length):
    steps, distance = [], 1
    while distance < length - 1:
        steps.append(distance)
        distance *= 2
    return steps


def reduce_interior(link, axis, left_ref, right_ref):
    length = link.shape[axis]
    row = lax.broadcasted_iota(jnp.int32, link.shape, axis)
    low, high, own = link, roll(link, -1, axis), jnp.ones_like(link)
    high = jnp.where(row == length - 1, 0.0, high)
    for step, distance in enumerate(steps_of(length)):
        inverse = 1.0 / (own + low + high)
        open_low, open_high = row > distance, row < length - 1 - distance
        left = jnp.where(open_low, low * roll(inverse, distance, axis), 0.0)
        right = jnp.where(open_high, high * roll(inverse, -distance, axis), 0.0)
        left_ref[step], right_ref[step] = left, right
        own = own + left * roll(own, distance, axis) + right * roll(own, -distance, axis)
        low = jnp.where(open_low, left * roll(low, distance, axis), low)
        high = jnp.where(open_high, right * roll(high, -distance, axis), high)
    inverse = 1.0 / (own + low + high)
    inner = (row > 0) & (row < length - 1)
    share_low = jnp.where(inner, low * inverse, jnp.where(row == 0, 1.0, 0.0))
    share_high = jnp.where(inner, high * inverse, jnp.where(row == 0, 0.0, 1.0))
    return share_low, share_high, jnp.where(inner, inverse, 0.0), own * inverse


def reduce_source(source, axis, left_ref, right_ref, inverse):
    length = source.shape[axis]
    for step, distance in enumerate(steps_of(length)):
        source = (
            source
            + left_ref[step] * roll(source, distance, axis)
            + right_ref[step] * roll(source, -distance, axis)
        )
    return source * inverse


def halvings(count):
    rows, stages = list(range(count)), []
    while len(rows) > 1:
        near = [
            (row, rows[i - 1] if i else None, rows[i + 1] if i + 1 < len(rows) else None)
            for i, row in enumerate(rows)
        ]
        stages.append((near[0::2], near[1::2]))
        rows = rows[0::2]
    return stages


def reduce_lines(link, left_ref, right_ref, kept_ref, gone_ref):
    length = link.shape[0]
    count = length // 8
    row = lax.broadcasted_iota(jnp.int32, link.shape, 0)
    low, high, own = link, roll(link, -1, 0), jnp.ones_like(link)
    for step, distance in enumerate((1, 2, 4)):
        inverse = 1.0 / (own + low + high)
        open_low, open_high = row > distance, row < length - 1 - distance
        left = jnp.where(open_low, low * roll(inverse, distance, 0), 0.0)
        right = jnp.where(open_high, high * roll(inverse, -distance, 0), 0.0)
        left_ref[step], right_ref[step] = left, right
        own = own + left * roll(own, distance, 0) + right * roll(own, -distance, 0)
        low = jnp.where(open_low, left * roll(low, distance, 0), low)
        high = jnp.where(open_high, right * roll(high, -distance, 0), high)
    first, last = row == 0, row == length - 1
    own = jnp.where(first | last, 0.0, own)
    low = jnp.where(first, 1.0, jnp.where(last, 0.0, low))
    high = jnp.where(last, 1.0, jnp.where(first, 0.0, high))
    tiles = lambda values: [values[8 * k : 8 * k + 8] for k in range(count)]
    own, low, high = tiles(own), tiles(low), tiles(high)
    inverse, share_low, share_high, share_own = {}, {}, {}, {}

    def finish(k):
        inverse[k] = 1.0 / (own[k] + low[k] + high[k])
        gone_ref[0, k], gone_ref[1, k] = low[k] * inverse[k], high[k] * inverse[k]
        gone_ref[2, k] = inverse[k]

    slot = 0
    for kept, gone in halvings(count):
        for k, _, _ in gone:
            finish(k)
        for k, below, above in kept:
            new_low, new_high = low[k], high[k]
            if below is not None:
                factor = low[k] * inverse[below]
                kept_ref[0, slot] = factor
                own[k] = own[k] + factor * own[below]
                new_low = factor * low[below]
            if above is not None:
                factor = high[k] * inverse[above]
                kept_ref[1, slot] = factor
                own[k] = own[k] + factor * own[above]
                new_high = factor * high[above]
            low[k], high[k] = new_low, new_high
            slot += 1
    finish(0)
    share_low[0], share_high[0] = low[0] * inverse[0], high[0] * inverse[0]
    share_own[0] = own[0] * inverse[0]
    for _, gone in halvings(count)[::-1]:
        for k, below, above in gone:
            to_low, to_high = low[k] * inverse[k], high[k] * inverse[k]
            share_low[k] = to_low * share_low[below]
            share_high[k] = to_low * share_high[below]
            if above is None:
                share_high[k] = share_high[k] + to_high
                share_own[k] = own[k] * inverse[k] + to_low * share_own[below]
            else:
                share_low[k] = share_low[k] + to_high * share_low[above]
                share_high[k] = share_high[k] + to_high * share_high[above]
    whole = lambda shares: jnp.concatenate([shares[k] for k in range(count)], 0)
    return whole(share_low), whole(share_high), share_own[0][1:2], share_own[count - 1][6:7]


def solve_lines(source, left_ref, right_ref, kept_ref, gone_ref):
    length = source.shape[0]
    count = length // 8
    for step, distance in enumerate((1, 2, 4)):
        source = (
            source
            + left_ref[step] * roll(source, distance, 0)
            + right_ref[step] * roll(source, -distance, 0)
        )
    row = lax.broadcasted_iota(jnp.int32, source.shape, 0)
    source = jnp.where((row == 0) | (row == length - 1), 0.0, source)
    source = [source[8 * k : 8 * k + 8] for k in range(count)]
    slot, stages = 0, halvings(count)
    for kept, _ in stages:
        for k, below, above in kept:
            if below is not None:
                source[k] = source[k] + kept_ref[0, slot] * source[below]
            if above is not None:
                source[k] = source[k] + kept_ref[1, slot] * source[above]
            slot += 1
    solved = {0: source[0] * gone_ref[2, 0]}
    for _, gone in stages[::-1]:
        for k, below, above in gone:
            solved[k] = source[k] * gone_ref[2, k] + gone_ref[0, k] * solved[below]
            if above is not None:
                solved[k] = solved[k] + gone_ref[1, k] * solved[above]
    return jnp.concatenate([solved[k] for k in range(count)], 0)


def chain(blocks, count, index, state):
    own = [blocks[k][3] + (blocks[k + 1][1] if k + 1 < count else 0.0) for k in range(count)]
    source = [blocks[k][4] + (blocks[k + 1][2] if k + 1 < count else 0.0) for k in range(count)]
    shape = own[0].shape
    state[0, 0], state[1, 0] = jnp.ones(shape, F32), jnp.zeros(shape, F32)
    up_own, up_source = own[0], source[0]
    for k in range(1, count):
        state[0, k], state[1, k] = up_own, up_source
        factor = blocks[k][0] / (up_own + blocks[k][0])
        up_own, up_source = own[k] + factor * up_own, source[k] + factor * up_source
    down_own, down_source = own[count - 1], source[count - 1]
    state[2, count - 1], state[3, count - 1] = down_own, down_source
    for k in range(count - 2, -1, -1):
        factor = blocks[k + 1][0] / (down_own + blocks[k + 1][0])
        down_own, down_source = own[k] + factor * down_own, source[k] + factor * down_source
        state[2, k], state[3, k] = down_own, down_source
    for k in range(count):
        state[4, k] = blocks[k][0]
    up_own, up_source, down_own, down_source, link = (state[i, index] for i in range(5))
    inverse = 1.0 / (up_own * down_own + link * (up_own + down_own))
    below = ((down_own + link) * up_source + link * down_source) * inverse
    here = ((up_own + link) * down_source + link * up_source) * inverse
    return below, here


def pick_halo(name, received, odd):
    first = received[0][...]
    second = received[1][...] if len(received) > 1 else jnp.zeros_like(first)
    index, count = lax.axis_index(name), lax.axis_size(name)
    below = jnp.where(odd, first, second)
    above = jnp.where(odd, second, first)
    return jnp.where(index > 0, below, 0.0), jnp.where(index < count - 1, above, 0.0)


def swaps_along(name):
    return min(lax.axis_size(name) - 1, 2)


def look_up(label, table_ref):
    conduct = jnp.broadcast_to(table_ref[0], label.shape)
    for entry in range(1, table_ref.shape[0]):
        conduct = jnp.where(label == entry, table_ref[entry], conduct)
    return conduct


def stage_kernel(
    heat_in, label_in, table_in, edge_in, heat_ref, conduct_ref, table_ref, edge_ref, label_ref,
    entries_ref, sems
):
    copies = [
        pltpu.make_async_copy(source, target, sems.at[i])
        for i, (source, target) in enumerate(
            (
                (table_in, entries_ref), (label_in, label_ref), (heat_in, heat_ref),
                (edge_in, edge_ref),
            )
        )
    ]
    for copy in copies:
        copy.start()
    copies[0].wait()
    for entry in range(table_ref.shape[0]):
        table_ref[entry] = jnp.full(table_ref.shape[1:], entries_ref[entry], F32)
    copies[1].wait()
    conduct_ref[...] = look_up(label_ref[...], table_ref)
    copies[2].wait()
    copies[3].wait()


def join_halos(z_halo, y_halo):
    return [*z_halo[1:], z_halo[0], *y_halo]


def split_halos(counts, refs):
    halos = refs[: sum(counts)]
    return [halos[counts[0] - 1], *halos[: counts[0] - 1]], halos[counts[0] :]


def start_kernel(
    heat_a_ref, label_a_ref, edge_a_ref, heat_b_ref, conduct_b_ref, edge_b_ref, table_ref,
    heat_ref, conduct_ref, edge_ref, *faces
):
    nx = heat_a_ref.shape[-1]
    heat_ref[:, :, :nx], heat_ref[:, :, nx:] = heat_a_ref[...], heat_b_ref[...]
    conduct_ref[:, :, :nx] = look_up(label_a_ref[...], table_ref)
    conduct_ref[:, :, nx:] = conduct_b_ref[...]
    edge_ref[:, :nx] = edge_a_ref[...].astype(F32)
    edge_ref[:, nx:] = edge_b_ref[...].astype(F32)
    z_faces, y_faces = faces[: swaps_along("gz")], faces[swaps_along("gz") :]
    odd_z = lax.axis_index("gz") % 2 == 1
    odd_y = lax.axis_index("gy") % 2 == 1
    for i, ref in enumerate((heat_ref, conduct_ref)):
        low, high = ref[0], ref[ref.shape[0] - 1]
        for face_ref, pick in zip(z_faces, (odd_z, ~odd_z)):
            face_ref[i] = jnp.where(pick, low, high)
        low, high = ref[:, 0, :], ref[:, ref.shape[1] - 1, :]
        for face_ref, pick in zip(y_faces, (odd_y, ~odd_y)):
            face_ref[i] = jnp.where(pick, low, high)


def end_bands(link, first, last, axis, high, own):
    length = high.shape[axis]
    at = lambda values, i: lax.index_in_dim(values, i, axis, keepdims=False)
    return (
        1.0 + first * at(own, 1),
        1.0 + last * at(own, length - 2),
        first * at(high, 1),
    )


def x_bands_kernel(
    heat_ref, conduct_ref, left_ref, right_ref, low_ref, high_ref, kept_ref, gone_ref, ends_ref,
    local_ref, low_block_ref, high_block_ref, zl_ref, zr_ref, zlow_ref, zhigh_ref, zinv_ref, zinner_ref
):
    nz, ny, nx = conduct_ref.shape
    conduct = conduct_ref[...]
    link = link_of(UPWARD_SCALE, conduct[1:], conduct[:-1])
    link = jnp.concatenate([jnp.zeros_like(conduct[:1]), link], 0)
    low, high, inverse, own = reduce_interior(link, 0, zl_ref, zr_ref)
    zlow_ref[...], zhigh_ref[...], zinv_ref[...] = low, high, inverse
    inner = end_bands(link, link[1], link[nz - 1], 0, high, own)
    for i, value in enumerate((*inner, link[1], link[nz - 1])):
        zinner_ref[i] = value
    heat = heat_ref[...]
    local = 2.0 * heat
    across = 2.0 * link_of(UPWARD_SCALE, conduct[1:], conduct[:-1]) * (heat[1:] - heat[:-1])
    nothing = jnp.zeros_like(heat[:1])
    local = local + jnp.concatenate([across, nothing], 0) - jnp.concatenate([nothing, across], 0)
    row = lax.broadcasted_iota(jnp.int32, conduct.shape, 1)
    across = 2.0 * link_of(FLAT_SCALE, conduct, roll(conduct, 1, 1)) * (heat - roll(heat, 1, 1))
    across = jnp.where(row > 0, across, 0.0)
    local = local - across + roll(across, -1, 1)
    local_ref[...] = local
    lines = conduct.reshape(nz * ny, nx).T
    row = lax.broadcasted_iota(jnp.int32, lines.shape, 0)
    link = jnp.where(row > 0, link_of(FLAT_SCALE, lines, roll(lines, 1, 0)), 0.0)
    low, high, own_low, own_high = reduce_lines(link, left_ref, right_ref, kept_ref, gone_ref)
    low_ref[...], high_ref[...] = low, high
    low_block_ref[...] = low.T.reshape(nz, ny, nx)
    high_block_ref[...] = high.T.reshape(nz, ny, nx)
    local = local.reshape(nz * ny, nx).T
    first, last = link[1:2], link[nx - 1 :]
    ends_ref[...] = jnp.concatenate(
        [
            jnp.sum(low * local, 0, keepdims=True),
            jnp.sum(high * local, 0, keepdims=True),
            1.0 + first * own_low,
            1.0 + last * own_high,
            first * high[1:2],
            lines[:1],
            lines[nx - 1 :],
            jnp.zeros_like(first),
        ],
        0,
    )


def x_message_kernel(
    halo_counts, heat_ref, conduct_ref, edge_ref, low_ref, high_ref, ends_ref, zinner_ref, *refs
):
    z_halo, y_halo = split_halos(halo_counts, refs)
    message_ref, z_flow_ref, y_flow_ref, zends_ref = refs[sum(halo_counts) :]
    nz, ny, nx = conduct_ref.shape
    lanes = nz * ny
    index_z, index_y = lax.axis_index("gz"), lax.axis_index("gy")
    below, above = pick_halo("gz", z_halo, index_z % 2 == 1)
    ground = jnp.where(index_z == 0, UPWARD_SCALE * conduct_ref[0] * edge_ref[...], 0.0)
    outer = link_of(UPWARD_SCALE, conduct_ref[0], below[1])
    z_flow_ref[0] = 2.0 * (outer * (below[0] - heat_ref[0]) - ground * heat_ref[0])
    own_first, own_last, between = zinner_ref[0] + ground, zinner_ref[1], zinner_ref[2]
    inverse = 1.0 / (own_first + between + outer)
    for i, value in enumerate((outer, between, inverse, zinner_ref[3], zinner_ref[4])):
        zends_ref[i] = value
    flow = link_of(UPWARD_SCALE, conduct_ref[nz - 1], above[1]) * (above[0] - heat_ref[nz - 1])
    z_flow_ref[1] = 2.0 * flow
    odd = index_y % 2 == 1
    near = lambda ref: jnp.where(odd, ref[:, 0, :], ref[:, ny - 1, :])
    if len(y_halo) == 1:
        flow = link_of(FLAT_SCALE, near(conduct_ref), y_halo[0][1])
        flow = 2.0 * flow * (y_halo[0][0] - near(heat_ref))
        y_flow_ref[0] = jnp.where(odd, flow, 0.0)
        y_flow_ref[1] = jnp.where(odd, 0.0, flow)
    else:
        below, above = pick_halo("gy", y_halo, index_y % 2 == 1)
        flow = link_of(FLAT_SCALE, conduct_ref[:, 0, :], below[1]) * (below[0] - heat_ref[:, 0, :])
        y_flow_ref[0] = 2.0 * flow
        flow = link_of(FLAT_SCALE, conduct_ref[:, ny - 1, :], above[1])
        y_flow_ref[1] = 2.0 * flow * (above[0] - heat_ref[:, ny - 1, :])

    def spread(values, first, step):
        shape = (values.shape[0], lanes)
        row = lax.broadcasted_iota(jnp.int32, shape, 0)
        lane = lax.broadcasted_iota(jnp.int32, shape, 1)
        return jnp.where(lane == first + step * row, jnp.sum(values, 1, keepdims=True), 0.0)

    sums = []
    for share in (low_ref, high_ref):
        layers = spread(share[0] * z_flow_ref[0], 0, 1)
        layers = layers + spread(share[nz - 1] * z_flow_ref[1], lanes - ny, 1)
        if len(y_halo) == 1:
            rows = spread(near(share) * flow, jnp.where(odd, 0, ny - 1), ny)
        else:
            rows = spread(share[:, 0, :] * y_flow_ref[0], 0, ny)
            rows = rows + spread(share[:, ny - 1, :] * y_flow_ref[1], ny - 1, ny)
        sums.append(jnp.sum(layers, 0, keepdims=True) + jnp.sum(rows, 0, keepdims=True))
    ends = ends_ref[...]
    message_ref[...] = jnp.concatenate([ends[0:1] + sums[0], ends[1:2] + sums[1], ends[2:8]], 0)


def x_source_kernel(
    local_ref, z_flow_ref, y_flow_ref, left_ref, right_ref, kept_ref, gone_ref, part_ref, source_ref
):
    nz, ny, nx = local_ref.shape
    source_ref[...] = local_ref[...]
    source_ref[0] += z_flow_ref[0]
    source_ref[nz - 1] += z_flow_ref[1]
    source_ref[:, 0, :] += y_flow_ref[0]
    source_ref[:, ny - 1, :] += y_flow_ref[1]
    source = source_ref[...].reshape(nz * ny, nx).T
    part_ref[...] = solve_lines(source, left_ref, right_ref, kept_ref, gone_ref)


def y_bands_kernel(halo_count, conduct_ref, *refs):
    y_halo = refs[:halo_count]
    yl_ref, yr_ref, ylow_ref, yhigh_ref, yinv_ref, yends_ref, *y_two_refs = refs[halo_count:]
    nz, ny, nx = conduct_ref.shape
    index_y = lax.axis_index("gy")
    conduct = conduct_ref[...]
    row = lax.broadcasted_iota(jnp.int32, conduct.shape, 1)
    link = jnp.where(row > 0, link_of(FLAT_SCALE, conduct, roll(conduct, 1, 1)), 0.0)
    low, high, inverse, own = reduce_interior(link, 1, yl_ref, yr_ref)
    ylow_ref[...], yhigh_ref[...], yinv_ref[...] = low, high, inverse
    below, above = pick_halo("gy", y_halo, index_y % 2 == 1)
    first = link_of(FLAT_SCALE, conduct_ref[:, 0, :], conduct_ref[:, 1, :])
    last = link_of(FLAT_SCALE, conduct_ref[:, ny - 1, :], conduct_ref[:, ny - 2, :])
    own_first, own_last, between = end_bands(link, first, last, 1, high, own)
    outer_low = link_of(FLAT_SCALE, conduct_ref[:, 0, :], below[1])
    outer_high = link_of(FLAT_SCALE, conduct_ref[:, ny - 1, :], above[1])
    for i, value in enumerate((first, last, own_first, own_last, between, outer_low, outer_high)):
        yends_ref[i] = value
    if y_two_refs:
        ysum_ref, yshare_ref = y_two_refs
        odd = index_y % 2 == 1
        near_own, far_own = jnp.where(odd, own_first, own_last), jnp.where(odd, own_last, own_first)
        share = between / (far_own + between)
        ysum_ref[0] = near_own + share * far_own
        ysum_ref[1] = share
        for k in range(nz):
            near, far = jnp.where(odd, low[k], high[k]), jnp.where(odd, high[k], low[k])
            yshare_ref[k] = near + ysum_ref[1, pl.ds(k, 1), :] * far


def chain_message(ends_ref, source_first, source_last, message_ref):
    own_first, own_last, between, outer = (ends_ref[i] for i in range(2, 6))
    inverse = 1.0 / (own_first + between + outer)
    message_ref[0] = outer * between * inverse
    message_ref[1] = outer * own_first * inverse
    message_ref[2] = outer * inverse * source_first
    message_ref[3] = own_last + between * own_first * inverse
    message_ref[4] = source_last + between * inverse * source_first


def chain_ends(name, messages, ends_ref, source_first, blocks_ref, state_ref):
    count, index = lax.axis_size(name), lax.axis_index(name)
    for shift, message in enumerate(messages):
        blocks_ref[lax.rem(index - shift + count, count)] = message[...]
    blocks = [tuple(blocks_ref[k, i] for i in range(5)) for k in range(count)]
    below, last = chain(blocks, count, index, state_ref)
    own_first, between, outer = ends_ref[2], ends_ref[4], ends_ref[5]
    first = (source_first + outer * below + between * last) / (own_first + between + outer)
    return first, last


def y_message_kernel(
    count_x, count_y, heat_ref, part_ref, low_ref, high_ref, yends_ref, *refs
):
    messages, refs = refs[:count_x], refs[count_x:]
    shares, refs = (refs[:2], refs[2:]) if count_y > 2 else (refs[:1], refs[1:])
    sums_ref, refs = (None, refs) if count_y > 2 else (refs[0], refs[1:])
    source_ref, message_ref, blocks_ref, rows_ref, state_ref = refs
    nz, ny, nx = heat_ref.shape
    index = lax.axis_index("gx") // 2
    for shift, message in enumerate(messages):
        blocks_ref[lax.rem(index - shift + count_x, count_x)] = message[...]
    first, last, own_first, own_last, between, c_first, c_last = (
        blocks_ref[:, i, :] for i in range(7)
    )
    before = jnp.zeros_like(c_last[:1])
    if count_x > 1:
        before = jnp.concatenate([before, c_last[:-1]], 0)
    outer = link_of(FLAT_SCALE, c_first, before)
    inverse = 1.0 / (own_first + between + outer)
    rows = (
        outer * between * inverse,
        outer * own_first * inverse,
        outer * inverse * first,
        own_last + between * own_first * inverse,
        last + between * inverse * first,
        first * inverse,
        outer * inverse,
        between * inverse,
    )
    for i, value in enumerate(rows):
        rows_ref[i] = value
    whole = lambda i, k: jnp.broadcast_to(rows_ref[i, pl.ds(k, 1), :], (8, rows_ref.shape[2]))
    blocks = [tuple(whole(i, k) for i in range(5)) for k in range(count_x)]
    below, last = chain(blocks, count_x, index, state_ref)
    first = whole(5, index) + whole(6, index) * below + whole(7, index) * last
    lines = part_ref[...] + low_ref[...] * first[:1] + high_ref[...] * last[:1]
    source = lines.T.reshape(nz, ny, nx) - 2.0 * heat_ref[...]
    source_ref[...] = source
    sums = [jnp.sum(share[...] * source, 1) for share in shares]
    if count_y > 2:
        chain_message(yends_ref, *sums, message_ref)
    else:
        message_ref[0], message_ref[1] = sums_ref[0], sums[0]


def y_source_kernel(
    heat_ref, source_ref, yl_ref, yr_ref, yinv_ref, yends_ref, ypart_ref, ysource_ref, spare_ref,
    heat_out_ref
):
    spare_ref[...] = jnp.zeros_like(spare_ref)
    heat_out_ref[...] = heat_ref[...]
    ny = source_ref.shape[1]
    part = reduce_source(source_ref[...], 1, yl_ref, yr_ref, yinv_ref[...])
    ypart_ref[...] = part
    ysource_ref[0] = source_ref[:, 0, :] + yends_ref[0] * ypart_ref[:, 1, :]
    ysource_ref[1] = source_ref[:, ny - 1, :] + yends_ref[1] * ypart_ref[:, ny - 2, :]


def z_message_kernel(
    count_y, ypart_ref, ylow_ref, yhigh_ref, yends_ref, ysource_ref, zlow_ref, zhigh_ref,
    zends_ref, *refs
):
    messages, refs = refs[:count_y], refs[count_y:]
    source_ref, small_ref, message_ref, ends_ref, *state = refs
    nz, ny, nx = ypart_ref.shape
    if count_y > 2:
        first, last = chain_ends("gy", messages, yends_ref, ysource_ref[0], *state)
    else:
        odd = lax.axis_index("gy") % 2 == 1
        mine, other = messages
        outer = jnp.where(odd, yends_ref[5], yends_ref[6])
        between = yends_ref[4]
        factor = outer / (other[0] + outer)
        near = (mine[1] + factor * other[1]) / (mine[0] + factor * other[0])
        far_own = jnp.where(odd, yends_ref[3], yends_ref[2])
        far_source = jnp.where(odd, ysource_ref[1], ysource_ref[0])
        far = (far_source + between * near) / (far_own + between)
        first, last = jnp.where(odd, near, far), jnp.where(odd, far, near)
    ends_ref[0], ends_ref[1] = first, last
    source_first, source_last = jnp.zeros((ny, nx), F32), jnp.zeros((ny, nx), F32)
    for k in range(nz):
        source = (
            ypart_ref[k]
            + ylow_ref[k] * ends_ref[0, pl.ds(k, 1), :]
            + yhigh_ref[k] * ends_ref[1, pl.ds(k, 1), :]
        )
        source_ref[k] = source
        source_first = source_first + zlow_ref[k] * source
        source_last = source_last + zhigh_ref[k] * source
    outer, between, inverse = (zends_ref[i] for i in range(3))
    for i, value in enumerate(
        (outer, between, inverse, source_first, zends_ref[3], zends_ref[4])
    ):
        small_ref[i] = value
    message_ref[0] = outer * inverse * source_first
    message_ref[1] = source_last + between * inverse * source_first


def z_source_kernel(heat_ref, source_ref, zl_ref, zr_ref, zinv_ref, small_ref, ready_ref):
    nz = source_ref.shape[0]
    inverse = zinv_ref[...]
    ready_ref[0] = heat_ref[...] + reduce_source(source_ref[...], 0, zl_ref, zr_ref, inverse)
    nothing = jnp.zeros_like(small_ref[0])
    low = jnp.stack([nothing, small_ref[4]] + [nothing] * (nz - 2), 0)
    ready_ref[1] = reduce_source(low, 0, zl_ref, zr_ref, inverse)
    ready_ref[1, 0] = jnp.ones_like(nothing)
    high = jnp.stack([nothing] * (nz - 2) + [small_ref[5], nothing], 0)
    ready_ref[2] = reduce_source(high, 0, zl_ref, zr_ref, inverse)
    ready_ref[2, nz - 1] = jnp.ones_like(nothing)


def starting_order(messages, back=False):
    if back:
        return [messages[0], messages[-1], *messages[1:-1]]
    return [messages[0], *messages[2:], messages[1]]


def join_kernel(small_ref, *refs):
    tail_ref, count, index = refs[-1], len(refs) - 1, lax.axis_index("gz")
    messages = [refs[k] for k in starting_order(list(range(count)), True)]
    tail_ref[:4] = small_ref[:4]
    for shift, message in enumerate(messages):
        place = 4 + 2 * lax.rem(index - shift + count, count)
        tail_ref[pl.ds(place, 2)] = message[...]


def mine_kernel(ready_ref, ends_ref, mine_ref):
    nx = mine_ref.shape[-1]
    first, last = ends_ref[0, :, nx:], ends_ref[1, :, nx:]
    mine_ref[...] = (
        ready_ref[0, :, :, nx:] + ready_ref[1, :, :, nx:] * first + ready_ref[2, :, :, nx:] * last
    )


def finish_kernel(ready_ref, tail_ref, bands_ref, theirs_ref, ends_ref, state_ref):
    count, index = (tail_ref.shape[0] - 4) // 2, lax.axis_index("gz")
    blocks = [
        (bands_ref[3 * k], bands_ref[3 * k + 1], tail_ref[4 + 2 * k], bands_ref[3 * k + 2],
         tail_ref[5 + 2 * k])
        for k in range(count)
    ]
    below, last = chain(blocks, count, index, state_ref)
    outer, between, inverse, source_first = (tail_ref[i] for i in range(4))
    first = (source_first + outer * below + between * last) * inverse
    nx = theirs_ref.shape[-1]
    ends_ref[0], ends_ref[1] = first, last
    first, last = first[:, :nx], last[:, :nx]
    theirs_ref[...] = (
        ready_ref[0, :, :, :nx] + ready_ref[1, :, :, :nx] * first + ready_ref[2, :, :, :nx] * last
    )


def ends_kernel(
    conduct_a_ref, edge_a_ref, label_b_ref, edge_b_ref, table_ref, zl_ref, zr_ref, zinv_ref,
    message_ref, conduct_ref, edge_ref
):
    half = conduct_a_ref.shape[-1]
    conduct_ref[:, :, :half] = conduct_a_ref[...]
    conduct_ref[:, :, half:] = look_up(label_b_ref[...], table_ref)
    edge_ref[:, :half] = edge_a_ref[...].astype(F32)
    edge_ref[:, half:] = edge_b_ref[...].astype(F32)
    conduct = conduct_ref[...]
    nz = conduct.shape[0]
    link = link_of(UPWARD_SCALE, conduct[1:], conduct[:-1])
    link = jnp.concatenate([jnp.zeros_like(conduct[:1]), link], 0)
    _, high, inverse, own = reduce_interior(link, 0, zl_ref, zr_ref)
    zinv_ref[...] = inverse
    own_first, own_last, between = end_bands(link, link[1], link[nz - 1], 0, high, own)
    ground = UPWARD_SCALE * conduct[0] * edge_ref[...]
    own_first = own_first + jnp.where(lax.axis_index("gz") == 0, ground, 0.0)
    for i, value in enumerate((own_first, own_last, between, conduct[0], conduct[nz - 1])):
        message_ref[i] = value


def all_bands_kernel(*refs):
    messages, (bands_ref, blocks_ref) = starting_order(refs[:-2], True), refs[-2:]
    count, index = len(messages), lax.axis_index("gz")
    for shift, message in enumerate(messages):
        blocks_ref[lax.rem(index - shift + count, count)] = message[...]
    for k in range(count):
        own_first, own_last, between, first, _ = (blocks_ref[k, i] for i in range(5))
        outer = jnp.zeros_like(first)
        if k > 0:
            outer = link_of(UPWARD_SCALE, first, blocks_ref[k - 1, 4])
        inverse = 1.0 / (own_first + between + outer)
        bands_ref[3 * k] = outer * between * inverse
        bands_ref[3 * k + 1] = outer * own_first * inverse
        bands_ref[3 * k + 2] = own_last + between * own_first * inverse


VMEM = pl.BlockSpec(memory_space=pltpu.VMEM)
HBM = pl.BlockSpec(memory_space=pltpu.HBM)


def call(kernel, outs, operands, scratch=(), specs=None, ops=200_000, vmem=32):
    return pl.pallas_call(
        kernel,
        out_shape=[jax.ShapeDtypeStruct(out, F32) if isinstance(out, tuple) else out for out in outs],
        in_specs=specs or [VMEM] * len(operands),
        out_specs=[VMEM] * len(outs),
        scratch_shapes=[pltpu.VMEM(item, F32) if isinstance(item, tuple) else item for item in scratch],
        compiler_params=pltpu.CompilerParams(vmem_limit_bytes=vmem * 1024 * 1024),
        cost_estimate=pl.CostEstimate(flops=ops, bytes_accessed=ops, transcendentals=0),
    )(*operands)


def neighbour_swaps(name, other, faces):
    count, width = lax.axis_size(name), lax.axis_size(other)
    received = [lax.ppermute(faces[0], name, [(i, i ^ 1) for i in range(count)])]
    if count > 2:
        pairs = []
        for j in range(width):
            for i in range(count):
                at = (j ^ 1, i) if i in (0, count - 1) else (j, ((i + 1) ^ 1) - 1)
                pairs.append(((j, i), at))
        if (other, name) == ("gy", "gz"):
            axes, place = (other, name), lambda at: at[0] * count + at[1]
        else:
            axes, place = (name, other), lambda at: at[1] * width + at[0]
        pairs = [(place(source), place(target)) for source, target in pairs]
        received.append(lax.ppermute(faces[1], axes, pairs))
    return received


def swap_all(name, message, stride=1):
    count = lax.axis_size(name)
    return [message] + [
        lax.ppermute(message, name, [(i, (i + shift) % count) for i in range(count)])
        for shift in range(stride, count, stride)
    ]


def other_core(values):
    count = lax.axis_size("gx")
    return lax.ppermute(values, "gx", [(i, i ^ 1) for i in range(count)])


def chip_step(heat_a, label_a, edge_a, heat_b, conduct_b, edge_b, table):
    nz, ny, half = heat_a.shape
    nx = 2 * half
    block, lines, layer, rows = (nz, ny, nx), (nx, nz * ny), (ny, nx), (nz, nx)
    count_x, count_y, count_z = (lax.axis_size(name) for name in ("gx", "gy", "gz"))
    count_x = count_x // 2
    tiles = (nx // 8, 8, lines[1])
    y_steps, z_steps = (len(steps_of(length)) for length in (ny, nz))

    halo_counts = swaps_along("gz"), swaps_along("gy")
    heat, conduct, edge, *faces = call(
        start_kernel,
        [block, block, layer] + [(2, *layer)] * halo_counts[0] + [(2, *rows)] * halo_counts[1],
        [heat_a, label_a, edge_a, heat_b, conduct_b, edge_b, table],
    )
    z_halo = neighbour_swaps("gz", "gy", faces[: halo_counts[0]])
    y_halo = neighbour_swaps("gy", "gz", faces[halo_counts[0] :])

    (
        x_left, x_right, x_low, x_high, x_kept, x_gone, x_ends, x_local, x_low_block, x_high_block,
        z_left, z_right, z_low, z_high, z_inverse, z_inner,
    ) = call(
        x_bands_kernel,
        [(3, *lines)] * 2 + [lines] * 2 + [(2, *tiles), (3, *tiles), (8, lines[1])] + [block] * 3
        + [(z_steps, *block)] * 2 + [block] * 3 + [(5, *layer)],
        [heat, conduct],
    )
    x_message, z_flow, y_flow, z_ends = call(
        functools.partial(x_message_kernel, halo_counts),
        [(8, lines[1]), (2, *layer), (2, *rows), (5, *layer)],
        [heat, conduct, edge, x_low_block, x_high_block, x_ends, z_inner,
         *join_halos(z_halo, y_halo)],
    )
    x_messages = swap_all("gx", x_message, 2)
    two = count_y == 2
    y_left, y_right, y_low, y_high, y_inverse, y_ends, *y_two = call(
        functools.partial(y_bands_kernel, len(y_halo)),
        [(y_steps, *block)] * 2 + [block] * 3 + [(7, *rows)] + [(2, *rows), block] * two,
        [conduct, *y_halo],
    )
    y_sum, y_share = y_two[:1], y_two[1:]
    (x_part,) = call(
        x_source_kernel,
        [lines],
        [x_local, z_flow, y_flow, x_left, x_right, x_kept, x_gone],
        [block],
    )
    y_rows = 2 if two else 5
    y_source, y_message = call(
        functools.partial(y_message_kernel, count_x, count_y),
        [block, (y_rows, *rows)],
        [heat, x_part, x_low, x_high, y_ends, *x_messages, *(y_share or (y_low, y_high)), *y_sum],
        [(count_x, 8, lines[1]), (8, count_x, lines[1]), (5, count_x, 8, lines[1])],
    )
    y_messages = swap_all("gy", y_message)
    y_part, y_end_sources, spare, heat_out = call(
        y_source_kernel,
        [block, (2, *rows), (bands_rows(count_z, nz), *layer), block],
        [heat, y_source, y_left, y_right, y_inverse, y_ends],
    )
    z_source, z_small, z_message = call(
        functools.partial(z_message_kernel, count_y),
        [block, (6, *layer), (2, *layer)],
        [y_part, y_low, y_high, y_ends, y_end_sources, z_low, z_high, z_ends, *y_messages],
        [(2, *rows)] + ([] if two else [(count_y, y_rows, *rows), (5, count_y, *rows)]),
    )
    return heat_out, spare, z_source, z_left, z_right, z_inverse, z_small, z_message


def bands_rows(count_z, nz):
    return -(-3 * count_z // nz) * nz


def chip_bands(heat_b, label_b, edge_b, heat_a, conduct_a, edge_a, table):
    nz, ny, half = conduct_a.shape
    nx = 2 * half
    block, layer, count_z = (nz, ny, nx), (ny, nx), lax.axis_size("gz")
    z_steps = len(steps_of(nz))
    z_left, z_right, z_inverse, message = call(
        ends_kernel,
        [(z_steps, *block)] * 2 + [block] + [(5, *layer)],
        [conduct_a, edge_a, label_b, edge_b, table],
        [block, layer],
    )
    (bands,) = call(
        all_bands_kernel,
        [(bands_rows(count_z, nz), *layer)],
        starting_order(swap_all("gz", message)),
        [(count_z, 5, *layer)],
    )
    zeros = lambda *shape: jnp.zeros(shape, F32)
    return (
        zeros(*block), bands, zeros(*block), z_left, z_right, z_inverse, zeros(6, *layer),
        zeros(2, *layer),
    )


def z_round(heat, _, z_source, z_left, z_right, z_inverse, z_small, z_message):
    count_z, block, layer = lax.axis_size("gz"), heat.shape, heat.shape[1:]
    messages = swap_all("gz", z_message)
    (ready,) = call(
        z_source_kernel, [(3, *block)], [heat, z_source, z_left, z_right, z_inverse, z_small]
    )
    (tail,) = call(join_kernel, [(4 + 2 * count_z, *layer)], [z_small, *starting_order(messages)])
    return ready, tail


def z_idle(heat, *_):
    count_z, block, layer = lax.axis_size("gz"), heat.shape, heat.shape[1:]
    return jnp.zeros((3, *block), F32), jnp.zeros((4 + 2 * count_z, *layer), F32)


def local(heat, label, table, edge):
    label_a, heat_a, edge_a = (other_core(values) for values in (label, heat, edge))
    entries = table.shape[0]
    own_heat, own_conduct, rows, own_edge = call(
        stage_kernel,
        [heat.shape, heat.shape, (entries, 8, heat.shape[-1]),
         jax.ShapeDtypeStruct(edge.shape, edge.dtype)],
        [heat, label, table, edge],
        [pltpu.VMEM(label.shape, label.dtype), pltpu.SMEM(table.shape, F32),
         pltpu.SemaphoreType.DMA((4,))],
        [HBM] * 4,
        vmem=60,
    )
    second = lax.axis_index("gx") % 2 == 1
    state = lax.cond(
        second, chip_step, chip_bands,
        heat_a, label_a, edge_a, own_heat, own_conduct, own_edge, rows,
    )
    bands = other_core(state[1])
    ready, tail = lax.cond(second, z_round, z_idle, *state)
    theirs, ends = call(
        finish_kernel,
        [heat_a.shape, (2, *tail.shape[1:])],
        [ready, tail, bands],
        [(5, lax.axis_size("gz"), *tail.shape[1:])],
    )
    received = other_core(theirs)
    (mine,) = call(mine_kernel, [heat_a.shape], [ready, ends])
    return jnp.where(second, mine, received)


def solution(mesh):
    return jax.shard_map(
        local,
        mesh=mesh,
        in_specs=(P("gz", "gy", "gx"), P("gz", "gy", "gx"), P(), P("gy", "gx")),
        out_specs=P("gz", "gy", "gx"),
        check_vma=False,
    )
```
